32 devices in a mesh: dp: 8 (over z, y), shard: 4 (over x, core).
Axes of the slice: x: 2, y: 2, z: 4, core: 2. Of those that a mesh axis runs over, the one named last changes fastest.
Arguments:
- tokens: bfloat16 [8192, 2304], P(('dp', 'shard')), may hold values from -6 to 6
- cotangent: bfloat16 [8192, 2304], P(('dp', 'shard')), may hold values from -6 to 6
- arrival: int32 [32, 256], P(('dp', 'shard')), may hold values from 0 to 255, each once within a row
- lengths: int32 [32, 4], P(('dp', 'shard')), may hold values from 1 to 128, 256 in all within a row
- adapter_set: int32 [32, 4], P(('dp', 'shard')), may hold values from 0 to 7
- gain_one: bfloat16 [2304], replicated, may hold values from 0.099609375 to 1.8984375
- gain_two: bfloat16 [2304], replicated, may hold values from 0.099609375 to 1.8984375
- w_query: bfloat16 [2304, 2304], P('dp'), may hold values from -0.125 to 0.125
- w_key: bfloat16 [2304, 2304], P('dp'), may hold values from -0.125 to 0.125
- w_value: bfloat16 [2304, 2304], P('dp'), may hold values from -0.125 to 0.125
- w_out: bfloat16 [2304, 2304], P('dp'), may hold values from -2 to 2
- w_gate: bfloat16 [2304, 5760], P('dp'), may hold values from -0.125 to 0.125
- w_up: bfloat16 [2304, 5760], P('dp'), may hold values from -0.125 to 0.125
- w_down: bfloat16 [5760, 2304], P('dp'), may hold values from -0.5 to 0.5
- adapters: bfloat16 [5455872], replicated, may hold values from -0.5 to 0.5
- first_moment_running: float32 [5455872], P(('dp', 'shard')), may hold values from -6 to 6
- second_moment_running: float32 [5455872], P(('dp', 'shard')), may hold values from 0.01 to 1
Outputs:
- token_layer_output: bfloat16 [8192, 2304], P(('dp', 'shard'))
- token_input_gradient: bfloat16 [8192, 2304], P(('dp', 'shard'))
- adapter_gradients: float32 [5455872], P(('dp', 'shard'))
- fresh_first_moment: float32 [5455872], P(('dp', 'shard'))
- fresh_second_moment: float32 [5455872], P(('dp', 'shard'))
- updated_adapter_weights: bfloat16 [5455872], replicated
The draws below stay inside these ranges and needn't reach their ends.
Inputs may be any that keep to these rules, and one draw needn't show every extreme that they name: `arrival`: each device's row lists every number of 0 to 255 once. Each device's 4 lengths sum to 256; the longest of each device is exactly 128.
All inputs are finite; a program needn't handle non-finite values.
Results may differ from the reference program's by a relative error of at most 0.018.
Values may be sent and summed in bfloat16 or wider, within the bound.
No kernel may reach another device: no remote copies, remote signals or barrier semaphores. Data moves between devices by JAX's collectives and lax.ppermute only.
A program may use at most 320 MiB of HBM per device.

```python
import math
import jax
import jax.numpy as jnp
import numpy as np
from jax import lax

MODEL_WIDTH = 2304
ATTENTION_HEADS = 36
HEAD_SIZE = 64
FEEDFORWARD_UNITS = 5760
ADAPTER_RANK = 16
SETS = 8
OPT_STEP = 10
SEQ_DEV = 4
TOK_DEV = 256
LONGEST = 128
PEER = 32
TOKENS = 8192
ADAPTER_COLUMNS = 128
PARAMS = 5455872
N_SHARD = 4
DEVICES = 32


def set_ends(drawn, rng, low, high):
    longest = drawn.shape.index(max(drawn.shape))
    spots = []
    for shift in (0, 1):
        where = [jax.random.randint(jax.random.fold_in(rng, axis), (), 0, length) for axis, length in enumerate(drawn.shape)]
        where[longest] = (where[longest] + shift) % drawn.shape[longest]
        spots.append(tuple(where))
    return drawn.at[spots[0]].set(low).at[spots[1]].set(high)


def steps_of(stream_key, dims, pieces, smallest, largest):
    loudness = 1.0
    for dim, shards_of in pieces:
        draws = jax.random.uniform(jax.random.fold_in(jax.random.fold_in(stream_key, 6), dim), (shards_of,), jnp.float32, smallest / len(pieces), largest / len(pieces))
        loudness = loudness * jnp.repeat(jnp.exp(draws), dims[dim] // shards_of).reshape((-1,) + (1,) * (len(dims) - 1 - dim))
    return loudness


def length_profile(amount, total, reach, lean):
    weights = [(1 << 20) // math.isqrt(grade ** lean) + 1 for grade in range(2, amount + 1)]
    spare, given = total - reach - (amount - 1), [1] * (amount - 1)
    while spare > 0:
        free = [i for i in range(amount - 1) if given[i] < reach]
        pool, remaining = sum([weights[i] for i in free]), spare
        for i in free:
            addition = min(reach - given[i], max(1, remaining * weights[i] // pool), spare)
            given[i] = given[i] + addition
            spare = spare - addition
    return np.array([reach] + given)


def ragged(rng, count, total, reach, skew):
    if count == 2:
        one = jax.random.randint(rng, (), max(1, total - reach), min(reach, total - 1) + 1)
        return jnp.stack([one, total - one])
    sizes = jnp.asarray(length_profile(count, total, reach, skew), jnp.int32)
    twos = (count - 1) // 2
    source_of, receiver = sizes[1:1 + 2 * twos:2], sizes[2:2 + 2 * twos:2]
    slack = jnp.minimum(source_of - 1, reach - receiver)
    passed = jax.random.randint(jax.random.fold_in(rng, 1), (twos,), 0, 1 << 20) % (slack + 1)
    sizes = sizes.at[1:1 + 2 * twos:2].set(source_of - passed).at[2:2 + 2 * twos:2].set(receiver + passed)
    return sizes[jax.random.permutation(jax.random.fold_in(rng, 2), count)]


def normal_values(rng, dims, scale, reach, shards=(), kind=jnp.bfloat16):
    array = scale * jax.random.normal(rng, dims, jnp.float32)
    if shards:
        array = array * steps_of(rng, dims, shards, -0.22, 0.18)
    return jnp.clip(array, -reach, reach).astype(kind)


def setup_inputs(seed: int = 0) -> dict:
    key_of = jax.random.split(jax.random.key(seed), 18)
    return {
        "tokens": normal_values(key_of[0], (TOKENS, MODEL_WIDTH), 1.0, 6.0, ((0, 32),)),
        "cotangent": normal_values(key_of[1], (TOKENS, MODEL_WIDTH), 1.0, 6.0, ((0, 32),)),
        "arrival": jax.vmap(lambda own: jax.random.permutation(own, TOK_DEV))(jax.random.split(key_of[2], DEVICES)).reshape((DEVICES, TOK_DEV)).astype(jnp.int32),
        "lengths": jax.vmap(lambda own: ragged(own, SEQ_DEV, TOK_DEV, LONGEST, 2))(jax.random.split(key_of[3], DEVICES)).reshape((DEVICES, SEQ_DEV)).astype(jnp.int32),
        "adapter_set": set_ends(jax.random.randint(key_of[4], (DEVICES, SEQ_DEV), 0, SETS), jax.random.fold_in(key_of[4], 1), 0, SETS - 1).astype(jnp.int32),
        "gain_one": jnp.clip(1.0 + 0.18 * jax.random.normal(key_of[5], (MODEL_WIDTH,), jnp.float32), 0.099609375, 1.8984375).astype(jnp.bfloat16),
        "gain_two": jnp.clip(1.0 + 0.18 * jax.random.normal(key_of[6], (MODEL_WIDTH,), jnp.float32), 0.099609375, 1.8984375).astype(jnp.bfloat16),
        "w_query": normal_values(key_of[7], (MODEL_WIDTH, MODEL_WIDTH), MODEL_WIDTH ** -0.5, 0.125, ((0, 8),)),
        "w_key": normal_values(key_of[8], (MODEL_WIDTH, MODEL_WIDTH), MODEL_WIDTH ** -0.5, 0.125, ((0, 8),)),
        "w_value": normal_values(key_of[9], (MODEL_WIDTH, MODEL_WIDTH), MODEL_WIDTH ** -0.5, 0.125, ((0, 8),)),
        "w_out": normal_values(key_of[10], (MODEL_WIDTH, MODEL_WIDTH), (max(MODEL_WIDTH // 256, 1)) ** -0.5, 2.0, ((0, 8),)),
        "w_gate": normal_values(key_of[11], (MODEL_WIDTH, FEEDFORWARD_UNITS), MODEL_WIDTH ** -0.5, 0.125, ((0, 8),)),
        "w_up": normal_values(key_of[12], (MODEL_WIDTH, FEEDFORWARD_UNITS), MODEL_WIDTH ** -0.5, 0.125, ((0, 8),)),
        "w_down": normal_values(key_of[13], (FEEDFORWARD_UNITS, MODEL_WIDTH), (max(FEEDFORWARD_UNITS // 48, 1)) ** -0.5, 0.5, ((0, 8),)),
        "adapters": normal_values(key_of[14], (PARAMS,), (0.5 * (MODEL_WIDTH * ADAPTER_RANK) ** -0.25), 0.5),
        "first_moment_running": normal_values(key_of[15], (PARAMS,), 1.0, 6.0, ((0, 32),), jnp.float32),
        "second_moment_running": jnp.clip(jnp.exp(math.log(1.0) - 4.6051702 * jax.random.uniform(key_of[16], (PARAMS,), jnp.float32) ** steps_of(key_of[16], (PARAMS,), ((0, 32),), -0.2, 0.2)), 0.01, 1.0),
    }


@jax.custom_vjp
def low_rank_rows(v):
    return lax.optimization_barrier(v.astype(jnp.bfloat16)).astype(jnp.float32)

@jax.custom_vjp
def low_rank_backward(v):
    return v

def low_keep(v):
    return (low_rank_rows(v), None)

def low_pass(kept, grad):
    return (grad,)

def back_keep(v):
    return (v, None)

def back_low(kept, grad):
    return (low_rank_rows(grad),)
low_rank_rows.defvjp(low_keep, low_pass)
low_rank_backward.defvjp(back_keep, back_low)
highest = lax.Precision.HIGHEST
norm_eps = 1e-05
residual_branch_scale = 1.4 / math.sqrt(40.0)
adapter_scale = 2.0
rope_base = 10000.0
first_decay_rate = 0.9
second_decay_rate = 0.999
adaptive_epsilon = 1e-08
weight_shrink_rate = 0.01
learning_rate = 0.01

def matrix_product(left_side, right_side):
    return jnp.dot(left_side, right_side, precision=highest)

def block_tables(sequence_lengths, sequence_adapter_index):
    row_ids = jnp.arange(TOK_DEV, dtype=jnp.int32)
    seq_ends = jnp.cumsum(sequence_lengths, dtype=jnp.int32)
    seq_starts = seq_ends - sequence_lengths
    segment = lax.optimization_barrier(jnp.sum((row_ids[:, None] >= seq_ends[None, :]).astype(jnp.int32), axis=1, dtype=jnp.int32))
    member = (segment[:, None] == jnp.arange(SEQ_DEV, dtype=jnp.int32)[None, :]).astype(jnp.int32)
    position = row_ids - lax.optimization_barrier(jnp.sum(member * seq_starts[None, :], axis=1, dtype=jnp.int32))
    token_adapter_index = lax.optimization_barrier(jnp.sum(member * sequence_adapter_index[None, :], axis=1, dtype=jnp.int32))
    adapter_choice_index = (jnp.arange(ADAPTER_COLUMNS, dtype=jnp.int32)[None, :] // ADAPTER_RANK == token_adapter_index[:, None]).astype(jnp.float32)
    allowed = (segment[:, None] == segment[None, :]) & (row_ids[None, :] <= row_ids[:, None])
    half_dim = HEAD_SIZE // 2
    inv_freq = jnp.power(rope_base, -2.0 * jnp.arange(half_dim, dtype=jnp.float32) / HEAD_SIZE)
    angles = position.astype(jnp.float32)[:, None] * inv_freq[None, :]
    return (adapter_choice_index, allowed, jnp.cos(angles)[:, None, :], jnp.sin(angles)[:, None, :])

def rotary_embedding(values, cosine_table, sine_table):
    shaped = values.reshape(values.shape[0], ATTENTION_HEADS, HEAD_SIZE)
    first_half = shaped[..., :HEAD_SIZE // 2]
    second_half = shaped[..., HEAD_SIZE // 2:]
    turned = jnp.concatenate([first_half * cosine_table - second_half * sine_table, second_half * cosine_table + first_half * sine_table], axis=-1)
    return turned.reshape(values.shape)

def restore_structure(flattened_vector):
    first_boundary = 6 * MODEL_WIDTH * ADAPTER_COLUMNS
    second_boundary = first_boundary + FEEDFORWARD_UNITS * ADAPTER_COLUMNS
    third_boundary = second_boundary + 5 * ADAPTER_COLUMNS * MODEL_WIDTH
    return (flattened_vector[:first_boundary].reshape(6, MODEL_WIDTH, ADAPTER_COLUMNS), flattened_vector[first_boundary:second_boundary].reshape(FEEDFORWARD_UNITS, ADAPTER_COLUMNS), flattened_vector[second_boundary:third_boundary].reshape(5, ADAPTER_COLUMNS, MODEL_WIDTH), flattened_vector[third_boundary:].reshape(2, ADAPTER_COLUMNS, FEEDFORWARD_UNITS))

def rms_scale(values):
    return lax.rsqrt(lax.optimization_barrier(jnp.mean(values * values, axis=-1, keepdims=True)) + norm_eps)

def apply_adapter_delta(input_rows, adapter_down_pair, adapter_up_pair, adapter_choice_index):
    reduced_total = low_rank_rows(low_rank_backward(matrix_product(input_rows, adapter_down_pair) * adapter_choice_index))
    return adapter_scale * matrix_product(reduced_total, adapter_up_pair)

def block_forward_pass(input_block, sequence_lengths, sequence_adapter_index, frozen_weights, adapter_groups):
    gain_first, gain_second, w_query, w_key, w_value, w_out, w_gate, w_up, w_down = frozen_weights
    lower_model_factor, lower_hidden_factor, upper_model_factor, upper_hidden_factor = adapter_groups
    adapter_choice_index, allowed, cosine_table, sine_table = block_tables(sequence_lengths, sequence_adapter_index)
    first_normalized = low_rank_rows(input_block * rms_scale(input_block) * gain_first)
    query_lin = low_rank_backward(matrix_product(first_normalized, w_query) + apply_adapter_delta(first_normalized, lower_model_factor[0], upper_model_factor[0], adapter_choice_index))
    key_lin = low_rank_backward(matrix_product(first_normalized, w_key) + apply_adapter_delta(first_normalized, lower_model_factor[1], upper_model_factor[1], adapter_choice_index))
    value_matrix_rows = low_rank_rows(low_rank_backward(matrix_product(first_normalized, w_value) + apply_adapter_delta(first_normalized, lower_model_factor[2], upper_model_factor[2], adapter_choice_index)))
    query_rows = low_rank_rows(rotary_embedding(query_lin, cosine_table, sine_table)).reshape(TOK_DEV, ATTENTION_HEADS, HEAD_SIZE)
    key_rows = low_rank_rows(rotary_embedding(key_lin, cosine_table, sine_table)).reshape(TOK_DEV, ATTENTION_HEADS, HEAD_SIZE)
    scores = low_rank_backward(jnp.einsum('qhd,khd->hqk', query_rows, key_rows, precision=highest) * HEAD_SIZE ** (-0.5))
    scores = jnp.where(allowed[None], scores, -jnp.inf)
    probs_full = low_rank_rows(jax.nn.softmax(scores, axis=-1))
    attention_result = jnp.einsum('hqk,khd->qhd', probs_full, value_matrix_rows.reshape(TOK_DEV, ATTENTION_HEADS, HEAD_SIZE), precision=highest)
    attention_result = low_rank_rows(low_rank_backward(attention_result.reshape(TOK_DEV, MODEL_WIDTH)))
    out_lin = low_rank_backward(matrix_product(attention_result, w_out) + apply_adapter_delta(attention_result, lower_model_factor[3], upper_model_factor[3], adapter_choice_index))
    middle_residual = input_block + residual_branch_scale * out_lin
    second_normalized = low_rank_rows(middle_residual * rms_scale(middle_residual) * gain_second)
    gate_linear_output = low_rank_backward(matrix_product(second_normalized, w_gate) + apply_adapter_delta(second_normalized, lower_model_factor[4], upper_hidden_factor[0], adapter_choice_index))
    up_linear_output = low_rank_backward(matrix_product(second_normalized, w_up) + apply_adapter_delta(second_normalized, lower_model_factor[5], upper_hidden_factor[1], adapter_choice_index))
    hidden_activation = low_rank_rows(jax.nn.silu(gate_linear_output) * up_linear_output)
    down_lin = low_rank_backward(matrix_product(hidden_activation, w_down) + apply_adapter_delta(hidden_activation, lower_hidden_factor, upper_model_factor[4], adapter_choice_index))
    return middle_residual + residual_branch_scale * down_lin

def reference(tokens, cotangent, arrival, lengths, adapter_set, gain_one, gain_two, w_query, w_key, w_value, w_out, w_gate, w_up, w_down, adapters, first_moment_running, second_moment_running):
    blocks = jnp.arange(DEVICES, dtype=jnp.int32)[:, None]
    dp_index = blocks // N_SHARD
    shard_index = blocks % N_SHARD
    source = (arrival // PEER * N_SHARD + shard_index) * TOK_DEV + dp_index * PEER + arrival % PEER
    source = source.reshape(-1).astype(jnp.int32)
    input_block_list = tokens[source].astype(jnp.float32).reshape(DEVICES, TOK_DEV, MODEL_WIDTH)
    incoming_gradient_blocks = cotangent[source].astype(jnp.float32).reshape(DEVICES, TOK_DEV, MODEL_WIDTH)
    frozen_weights = tuple((weight.astype(jnp.float32) for weight in (gain_one, gain_two, w_query, w_key, w_value, w_out, w_gate, w_up, w_down)))
    adapter_flat_vector = adapters.astype(jnp.float32)

    def whole_layer_pass(every_token_row, adapter_collection):
        adapter_groups = restore_structure(adapter_collection)

        def one_block(single_block_entry):
            return jax.checkpoint(block_forward_pass)(single_block_entry[0], single_block_entry[1], single_block_entry[2], frozen_weights, adapter_groups)
        return lax.map(one_block, (every_token_row, lengths, adapter_set))
    output_rows, reverse_function = jax.vjp(whole_layer_pass, input_block_list, adapter_flat_vector)
    input_gradient_rows, adapter_gradients = reverse_function(incoming_gradient_blocks)
    token_layer_output = jnp.zeros((TOKENS, MODEL_WIDTH), jnp.bfloat16).at[source].set(output_rows.reshape(TOKENS, MODEL_WIDTH).astype(jnp.bfloat16))
    token_input_gradient = jnp.zeros((TOKENS, MODEL_WIDTH), jnp.bfloat16).at[source].set(input_gradient_rows.reshape(TOKENS, MODEL_WIDTH).astype(jnp.bfloat16))
    fresh_first_moment = first_decay_rate * first_moment_running + (1.0 - first_decay_rate) * adapter_gradients
    fresh_second_moment = second_decay_rate * second_moment_running + (1.0 - second_decay_rate) * adapter_gradients * adapter_gradients
    unbiased_first = fresh_first_moment / (1.0 - first_decay_rate ** OPT_STEP)
    unbiased_second = fresh_second_moment / (1.0 - second_decay_rate ** OPT_STEP)
    optimizer_update = unbiased_first / (jnp.sqrt(unbiased_second) + adaptive_epsilon) + weight_shrink_rate * adapter_flat_vector
    updated_adapter_weights = (adapter_flat_vector - learning_rate * optimizer_update).astype(jnp.bfloat16)
    return (token_layer_output, token_input_gradient, adapter_gradients, fresh_first_moment, fresh_second_moment, updated_adapter_weights)
```

```python
import functools
import math

import jax
import jax.numpy as jnp
from jax import lax
from jax.sharding import PartitionSpec as P

MODEL_WIDTH = 2304
ATTENTION_HEADS = 36
HEAD_SIZE = 64
FEEDFORWARD_UNITS = 5760
ADAPTER_RANK = 16
OPT_STEP = 10
SEQ_DEV = 4
TOK_DEV = 256
ADAPTER_COLUMNS = 128


norm_eps = 1e-05
residual_branch_scale = 1.4 / math.sqrt(40.0)
adapter_scale = 2.0
rope_base = 10000.0
first_decay_rate = 0.9
second_decay_rate = 0.999
adaptive_epsilon = 1e-08
weight_shrink_rate = 0.01
learning_rate = 0.01


def matrix_product(left_side, right_side):
    return jnp.dot(left_side, right_side, preferred_element_type=jnp.float32)


def matrix_product_backward(left_side, right_side):
    return lax.dot_general(
        left_side, right_side, (((1,), (1,)), ((), ())), preferred_element_type=jnp.float32
    )


def outer_product_sum(left_side, right_side):
    return lax.dot_general(
        left_side, right_side, (((0,), (0,)), ((), ())), preferred_element_type=jnp.float32
    )


def project_to_rank(values):
    return values.astype(jnp.bfloat16)


def block_tables(sequence_lengths, sequence_adapter_index):
    row_ids = jnp.arange(TOK_DEV, dtype=jnp.int32)
    seq_ends = jnp.cumsum(sequence_lengths, dtype=jnp.int32)
    seq_starts = seq_ends - sequence_lengths
    segment = jnp.sum(
        (row_ids[:, None] >= seq_ends[None, :]).astype(jnp.int32), axis=1, dtype=jnp.int32
    )
    member = (segment[:, None] == jnp.arange(SEQ_DEV, dtype=jnp.int32)[None, :]).astype(jnp.int32)
    position = row_ids - jnp.sum(member * seq_starts[None, :], axis=1, dtype=jnp.int32)
    token_adapter_index = jnp.sum(member * sequence_adapter_index[None, :], axis=1, dtype=jnp.int32)
    adapter_choice_index = (
        jnp.arange(ADAPTER_COLUMNS, dtype=jnp.int32)[None, :] // ADAPTER_RANK
        == token_adapter_index[:, None]
    ).astype(jnp.float32)
    allowed = (segment[:, None] == segment[None, :]) & (row_ids[None, :] <= row_ids[:, None])
    half_dim = HEAD_SIZE // 2
    inv_freq = jnp.power(rope_base, -2.0 * jnp.arange(half_dim, dtype=jnp.float32) / HEAD_SIZE)
    angles = position.astype(jnp.float32)[:, None] * inv_freq[None, :]
    return (adapter_choice_index, allowed, jnp.cos(angles)[:, None, :], jnp.sin(angles)[:, None, :])


def rotary_embedding(values, cosine_table, sine_table):
    shaped = values.reshape(values.shape[0], ATTENTION_HEADS, HEAD_SIZE)
    first_half = shaped[..., : HEAD_SIZE // 2]
    second_half = shaped[..., HEAD_SIZE // 2 :]
    turned = jnp.concatenate(
        [
            first_half * cosine_table - second_half * sine_table,
            second_half * cosine_table + first_half * sine_table,
        ],
        axis=-1,
    )
    return turned.reshape(values.shape[0], MODEL_WIDTH)


def rotary_back(gradient_value, cosine_table, sine_table):
    first_half = gradient_value[..., : HEAD_SIZE // 2]
    second_half = gradient_value[..., HEAD_SIZE // 2 :]
    turned = jnp.concatenate(
        [
            first_half * cosine_table + second_half * sine_table,
            second_half * cosine_table - first_half * sine_table,
        ],
        axis=-1,
    )
    return turned.reshape(gradient_value.shape[0], MODEL_WIDTH)


def restore_structure(flattened_vector):
    first_boundary = 6 * MODEL_WIDTH * ADAPTER_COLUMNS
    second_boundary = first_boundary + FEEDFORWARD_UNITS * ADAPTER_COLUMNS
    third_boundary = second_boundary + 5 * ADAPTER_COLUMNS * MODEL_WIDTH
    return (
        flattened_vector[:first_boundary].reshape(6, MODEL_WIDTH, ADAPTER_COLUMNS),
        flattened_vector[first_boundary:second_boundary].reshape(
            FEEDFORWARD_UNITS, ADAPTER_COLUMNS
        ),
        flattened_vector[second_boundary:third_boundary].reshape(5, ADAPTER_COLUMNS, MODEL_WIDTH),
        flattened_vector[third_boundary:].reshape(2, ADAPTER_COLUMNS, FEEDFORWARD_UNITS),
    )


def rms_scale(values):
    return lax.rsqrt(jnp.mean(values * values, axis=-1, keepdims=True) + norm_eps)


def norm_back(values, scale, gain, gradient_value):
    weighted = gradient_value * gain
    return scale * weighted - values * scale**3 * jnp.mean(
        values * weighted, axis=-1, keepdims=True
    )


def apply_adapter_delta(input_rows, adapter_down_pair, adapter_up_pair, adapter_choice_index):
    reduced_total = project_to_rank(
        matrix_product(input_rows, adapter_down_pair) * adapter_choice_index
    )
    return (reduced_total, adapter_scale * matrix_product(reduced_total, adapter_up_pair))


def adapter_backward_pass(
    gradient_value,
    input_rows,
    reduced_total,
    adapter_down_pair,
    adapter_up_pair,
    adapter_choice_index,
):
    reduced_gradient_sum = project_to_rank(
        adapter_scale
        * matrix_product_backward(gradient_value, adapter_up_pair)
        * adapter_choice_index
    )
    up_weight_gradient = adapter_scale * outer_product_sum(reduced_total, gradient_value)
    down_weight_gradient = outer_product_sum(input_rows, reduced_gradient_sum)
    return (
        down_weight_gradient,
        up_weight_gradient,
        matrix_product_backward(reduced_gradient_sum, adapter_down_pair),
    )


def attention_scores(query_rows, key_rows, allowed):
    scores = jnp.einsum(
        "qhd,khd->hqk", query_rows, key_rows, preferred_element_type=jnp.float32
    ) * HEAD_SIZE ** (-0.5)
    return jnp.where(allowed[None], scores, -jnp.inf)


def attention_forward(query_rows, key_rows, value_matrix_rows, allowed):
    scores = attention_scores(query_rows, key_rows, allowed)
    row_top = jnp.max(scores, axis=-1, keepdims=True)
    expanded = jnp.exp(scores - row_top)
    row_total = jnp.sum(expanded, axis=-1, keepdims=True)
    probs_low = project_to_rank(expanded / row_total)
    attention_result = jnp.einsum(
        "hqk,khd->qhd", probs_low, value_matrix_rows, preferred_element_type=jnp.float32
    )
    return (attention_result, row_top, row_total)


def attention_back(
    query_rows, key_rows, value_matrix_rows, allowed, row_top, row_total, grad_attended
):
    probs_full = jnp.exp(attention_scores(query_rows, key_rows, allowed) - row_top) / row_total
    grad_probs = jnp.einsum(
        "qhd,khd->hqk", grad_attended, value_matrix_rows, preferred_element_type=jnp.float32
    )
    row_delta = jnp.sum(probs_full * grad_probs, axis=-1, keepdims=True)
    grad_scores = project_to_rank(probs_full * (grad_probs - row_delta))
    grad_queries = HEAD_SIZE ** (-0.5) * jnp.einsum(
        "hqk,khd->qhd", grad_scores, key_rows, preferred_element_type=jnp.float32
    )
    grad_keys = HEAD_SIZE ** (-0.5) * jnp.einsum(
        "hqk,qhd->khd", grad_scores, query_rows, preferred_element_type=jnp.float32
    )
    grad_values = jnp.einsum(
        "hqk,qhd->khd",
        project_to_rank(probs_full),
        grad_attended,
        preferred_element_type=jnp.float32,
    )
    return (grad_queries, grad_keys, grad_values)


GROUP = 4
AXES = ("dp", "shard")


class Place:
    def __init__(self, dp, shard):
        self.line, self.shard = dp // 2, shard
        i, s = lax.axis_index("dp"), lax.axis_index("shard")
        self.z, self.y, self.x, self.c = i // 2, i % 2, s // 2, s % 2
        self.q = self.y * 2 + self.c
        self.spots = [
            (z, y, x, c)
            for z in range(self.line)
            for y in range(2)
            for x in range(shard // 2)
            for c in range(2)
        ]

    def number(self, z, y, x, c):
        return (z * 2 + y) * self.shard + x * 2 + c

    def move(self, value, target):
        pairs = []
        for spot in self.spots:
            to = target(*spot)
            if to is not None:
                pairs.append((self.number(*spot), self.number(*to)))
        return lax.ppermute(value, AXES, pairs)

    def by_y(self, value):
        return self.move(value, lambda z, y, x, c: (z, 1 - y, x, c))

    def by_x(self, value):
        return self.move(value, lambda z, y, x, c: (z, y, 1 - x, c))

    def by_c(self, value):
        return self.move(value, lambda z, y, x, c: (z, y, x, 1 - c))

    def step_z(self, value, step):
        return self.move(
            value, lambda z, y, x, c: (z + step, y, x, c) if 0 <= z + step < self.line else None
        )

    def ring_z(self, value, step):
        return self.move(value, lambda z, y, x, c: ((z + step) % self.line, y, x, c))

    def along_z(self, block):
        ups, downs = [block], [block]
        for _ in range(self.line - 1):
            ups.append(self.step_z(ups[-1], 1))
            downs.append(self.step_z(downs[-1], -1))
        return jnp.stack(
            [
                jnp.where(self.z >= k, ups[k], downs[self.line - k])
                for k in range(1, self.line)
            ]
        )

    def gather_group(self, rows):
        pair = jnp.concatenate([rows, self.by_y(rows)], axis=0)
        return jnp.concatenate([pair, self.by_c(pair)], axis=0)

    def sum_group(self, partial):
        rows = partial.shape[0] // GROUP
        partial = partial.reshape(GROUP, rows, -1)
        got = self.by_c(partial[2:].astype(jnp.bfloat16))
        pair = partial[:2] + got.astype(jnp.float32)
        got = self.by_y(pair[1].astype(jnp.bfloat16))
        return pair[0] + got.astype(jnp.float32)


def put(buffer, block, *where):
    block = block.reshape((1,) * len(where) + block.shape)
    return lax.dynamic_update_slice(
        buffer, block, tuple(where) + (0,) * (buffer.ndim - len(where))
    )


def gather_quarter(place, own, other):
    got = place.by_y(other)
    same = place.y == place.x
    carry, rest = jnp.where(same, own, got), jnp.where(same, got, own)
    lines = place.along_z(carry)
    mates = place.by_x(lines)
    full = jnp.zeros((place.line, 2) + own.shape, own.dtype)
    full = put(full, carry, place.z, place.x)
    full = put(full, rest, place.z, 1 - place.x)
    for k in range(1, place.line):
        plane = (place.z - k) % place.line
        full = put(full, lines[k - 1], plane, place.x)
        full = put(full, mates[k - 1], plane, 1 - place.x)
    return full.reshape((-1,) + own.shape[1:])


def gather_attention(place, blocks, y_first):
    s = place.x * 2 + place.c
    native = jnp.stack(blocks)
    carry = lax.dynamic_index_in_dim(native, s, 0, keepdims=False)
    lines = place.along_z(carry)
    if y_first:
        y_near, y_lines = place.by_y(carry), place.by_y(lines)
        x_lines, xy_near, xy_lines = place.by_x(lines), place.by_x(y_near), place.by_x(y_lines)
    else:
        x_lines = place.by_x(lines)
        x_near = lax.dynamic_index_in_dim(native, s ^ 2, 0, keepdims=False)
        y_near, y_lines = place.by_y(carry), place.by_y(lines)
        xy_near, xy_lines = place.by_y(x_near), place.by_y(x_lines)
    full = jnp.zeros((GROUP, place.line, 2) + carry.shape, carry.dtype)
    for t in range(GROUP):
        full = put(full, blocks[t], t, place.z, place.y)
    parts = (
        (lines, place.y, s, True),
        (y_near, 1 - place.y, s, False),
        (y_lines, 1 - place.y, s, True),
        (x_lines, place.y, s ^ 2, True),
        (xy_near, 1 - place.y, s ^ 2, False),
        (xy_lines, 1 - place.y, s ^ 2, True),
    )
    for value, y, which, many in parts:
        for held, weight in ((value, which), (place.by_c(value), which ^ 1)):
            if many:
                for k in range(1, place.line):
                    full = put(full, held[k - 1], weight, (place.z - k) % place.line, y)
            else:
                full = put(full, held, weight, place.z, y)
    return [full[t].reshape((-1,) + carry.shape[1:]) for t in range(GROUP)]


def hidden_columns(place, values, blocks, padded):
    each = FEEDFORWARD_UNITS // blocks
    own = each // GROUP

    def take(quarter):
        def cut(value):
            pieces = []
            for i in range(blocks):
                start = each * i + own * quarter
                piece = value[:, start : start + own]
                pieces.append(jnp.pad(piece, ((0, 0), (0, padded - own))))
            return pieces

        return lambda *given: jnp.concatenate([p for v in given for p in cut(v)], axis=1)

    branches = [take(k) for k in range(GROUP)]
    return lax.switch(place.q, branches, *values), lambda: lax.switch(
        place.q ^ 2, branches, *values
    )


def spread_columns(place, value, blocks, padded):
    each = FEEDFORWARD_UNITS // blocks
    own = each // GROUP

    def lay(quarter):
        def build(given):
            pieces = []
            for i in range(blocks):
                piece = given[:, padded * i : padded * i + own]
                pieces.append(
                    jnp.pad(piece, ((0, 0), (own * quarter, each - own * (quarter + 1))))
                )
            return jnp.concatenate(pieces, axis=1)

        return build

    return lax.switch(place.q, [lay(k) for k in range(GROUP)], value)


def hidden_rows(place, value, quarter, blocks, padded):
    own = value.shape[0] // (blocks * GROUP)
    split = value.reshape(blocks, GROUP, own, -1)
    got = lax.dynamic_index_in_dim(split, quarter, 1, keepdims=False)
    return jnp.pad(got, ((0, 0), (0, padded - own), (0, 0))).reshape(blocks * padded, -1)


def reduce_to_owner(place, flat):
    owners = place.line * 2 * place.shard
    share = flat.shape[0] // owners
    half = -(-share // 8) * 8
    start = 2 * share - half
    pairs = flat.reshape(place.line, 2, place.shard // 2, 2 * share, ADAPTER_COLUMNS)
    keep = lax.dynamic_slice_in_dim(pairs, place.c * start, half, 3)
    send = lax.dynamic_slice_in_dim(pairs, (1 - place.c) * start, half, 3)
    total = keep + place.by_c(send.astype(jnp.bfloat16)).astype(jnp.float32)
    for axis, mine, move in ((1, place.y, place.by_y), (1, place.x, place.by_x)):
        keep = lax.dynamic_index_in_dim(total, mine, axis, keepdims=False)
        send = lax.dynamic_index_in_dim(total, 1 - mine, axis, keepdims=False)
        total = keep + move(send.astype(jnp.bfloat16)).astype(jnp.float32)
    low = total.astype(jnp.bfloat16)
    result = lax.dynamic_index_in_dim(total, place.z, 0, keepdims=False)
    for k in range(1, place.line):
        send = lax.dynamic_index_in_dim(low, (place.z + k) % place.line, 0, keepdims=False)
        result = result + place.ring_z(send, k).astype(jnp.float32)
    return lax.dynamic_slice_in_dim(result, place.c * (half - share), share, 0)


def gather_owners(place, own):
    share = own.shape[0]
    half = -(-share // 8) * 8
    start = 2 * share - half
    mate = place.by_c(own)
    first, second = jnp.where(place.c == 0, own, mate), jnp.where(place.c == 0, mate, own)
    pair = jnp.concatenate([first, second], axis=0)
    carry = lax.dynamic_slice_in_dim(pair, place.c * start, half, 0)
    lines = jnp.stack([carry] + [place.ring_z(carry, k) for k in range(1, place.line)])
    mates = place.by_x(lines)
    y_lines, y_mates = place.by_y(lines), place.by_y(mates)
    full = jnp.zeros(
        (place.line, 2, place.shard // 2, 2 * share, ADAPTER_COLUMNS), own.dtype
    )
    for value, y, x in (
        (lines, place.y, place.x),
        (mates, place.y, 1 - place.x),
        (y_lines, 1 - place.y, place.x),
        (y_mates, 1 - place.y, 1 - place.x),
    ):
        for held, c in ((value, place.c), (place.by_c(value), 1 - place.c)):
            for k in range(place.line):
                block = held[k].reshape(1, 1, 1, half, ADAPTER_COLUMNS)
                where = ((place.z - k) % place.line, y, x, c * start, 0)
                full = lax.dynamic_update_slice(full, block, where)
    return full.reshape(-1)


def low(values):
    return values.astype(jnp.bfloat16)


def shards(
    dp,
    shard,
    tokens,
    cotangent,
    arrival,
    lengths,
    adapter_set,
    gain_one,
    gain_two,
    w_query,
    w_key,
    w_value,
    w_out,
    w_gate,
    w_up,
    w_down,
    adapters,
    first_moment_running,
    second_moment_running,
):
    place = Place(dp, shard)
    token_order = arrival[0]
    count = token_order.shape[0]
    padded = -(-(FEEDFORWARD_UNITS // (dp * GROUP)) // 8) * 8
    arrived_x = lax.all_to_all(tokens, "dp", split_axis=0, concat_axis=0, tiled=True)
    arrived_cot = lax.all_to_all(cotangent, "dp", split_axis=0, concat_axis=0, tiled=True)

    half = MODEL_WIDTH // 2
    attention_weights = (w_query, w_key, w_value, w_out)
    left = gather_attention(place, [w[:, :half] for w in attention_weights], True)
    right = gather_attention(place, [w[:, half:] for w in attention_weights], False)
    own, other = hidden_columns(place, (w_gate, w_up), dp, padded)
    gate_up = gather_quarter(place, own, other())
    down = gather_quarter(
        place,
        hidden_rows(place, w_down, place.q, 1, padded),
        hidden_rows(place, w_down, place.q ^ 2, 1, padded),
    )
    hidden = dp * padded

    A_model, A_hidden, B_model, B_hidden = restore_structure(adapters)
    table = jnp.concatenate([lengths, adapter_set], axis=1)
    tables = place.gather_group(table)
    choice, allowed, cosine_table, sine_table = block_tables(lengths[0], adapter_set[0])
    choices = jnp.concatenate(
        [block_tables(tables[k, :SEQ_DEV], tables[k, SEQ_DEV:])[0] for k in range(GROUP)], axis=0
    )
    gain_first = gain_one.astype(jnp.float32)
    gain_second = gain_two.astype(jnp.float32)

    x = arrived_x[token_order].astype(jnp.float32)
    g = arrived_cot[token_order].astype(jnp.float32)
    scale_one = rms_scale(x)
    n1 = low(x * scale_one * gain_first)

    def project(values, which):
        return jnp.concatenate(
            [matrix_product(values, left[which]), matrix_product(values, right[which])], axis=1
        )

    def project_back(values, which):
        return matrix_product_backward(values[:, :half], left[which]) + matrix_product_backward(
            values[:, half:], right[which]
        )

    z_query, delta_query = apply_adapter_delta(n1, A_model[0], B_model[0], choice)
    z_key, delta_key = apply_adapter_delta(n1, A_model[1], B_model[1], choice)
    z_value, delta_value = apply_adapter_delta(n1, A_model[2], B_model[2], choice)
    heads = (count, ATTENTION_HEADS, HEAD_SIZE)
    queries = low(
        rotary_embedding(project(n1, 0) + delta_query, cosine_table, sine_table)
    ).reshape(heads)
    keys = low(rotary_embedding(project(n1, 1) + delta_key, cosine_table, sine_table)).reshape(
        heads
    )
    values = low(project(n1, 2) + delta_value).reshape(heads)
    o, row_top, row_total = attention_forward(queries, keys, values, allowed)
    o = low(o.reshape(count, MODEL_WIDTH))
    z_out, delta_out = apply_adapter_delta(o, A_model[3], B_model[3], choice)
    m = x + residual_branch_scale * (project(o, 3) + delta_out)
    scale_two = rms_scale(m)
    n2 = low(m * scale_two * gain_second)

    n2_all = place.gather_group(n2)
    e_down = low(residual_branch_scale * g)
    dz_down = low(adapter_scale * matrix_product_backward(e_down, B_model[4]) * choice)
    sent = place.gather_group(jnp.concatenate([e_down, dz_down], axis=1))
    e_down_all, dz_down_all = sent[:, :MODEL_WIDTH], sent[:, MODEL_WIDTH:]
    B_gate_up, _ = hidden_columns(place, (B_hidden[0], B_hidden[1]), dp, padded)
    A_down = hidden_rows(place, A_hidden, place.q, dp, padded)
    z_gate = low(matrix_product(n2_all, A_model[4]) * choices)
    z_up = low(matrix_product(n2_all, A_model[5]) * choices)
    both = matrix_product(n2_all, gate_up)
    gt = both[:, :hidden] + adapter_scale * matrix_product(z_gate, B_gate_up[:, :hidden])
    up = both[:, hidden:] + adapter_scale * matrix_product(z_up, B_gate_up[:, hidden:])
    sg = jax.nn.sigmoid(gt)
    act = gt * sg
    h = low(act * up)
    y_sum = place.sum_group(
        jnp.concatenate([matrix_product(h, down), matrix_product(h, A_down)], axis=1)
    )
    z_down = low(y_sum[:, MODEL_WIDTH:] * choice)
    y = m + residual_branch_scale * (
        y_sum[:, :MODEL_WIDTH] + adapter_scale * matrix_product(z_down, B_model[4])
    )
    dh = matrix_product_backward(e_down_all, down) + matrix_product_backward(dz_down_all, A_down)
    e_gate = low(dh * up * (sg + gt * sg * (1.0 - sg)))
    e_up = low(dh * act)
    e_both = jnp.concatenate([e_gate, e_up], axis=1)
    back_sum = place.sum_group(
        jnp.concatenate(
            [
                matrix_product_backward(e_both, gate_up),
                matrix_product_backward(e_gate, B_gate_up[:, :hidden]),
                matrix_product_backward(e_up, B_gate_up[:, hidden:]),
            ],
            axis=1,
        )
    )
    split = MODEL_WIDTH + ADAPTER_COLUMNS
    dz_gate = low(adapter_scale * back_sum[:, MODEL_WIDTH:split] * choice)
    dz_up = low(adapter_scale * back_sum[:, split:] * choice)
    dn2 = (
        back_sum[:, :MODEL_WIDTH]
        + matrix_product_backward(dz_gate, A_model[4])
        + matrix_product_backward(dz_up, A_model[5])
    )
    dA_gate, dA_up = outer_product_sum(n2, dz_gate), outer_product_sum(n2, dz_up)
    dB_gate = adapter_scale * outer_product_sum(z_gate, e_gate)
    dB_up = adapter_scale * outer_product_sum(z_up, e_up)
    dA_down = outer_product_sum(h, dz_down_all)
    dB_down = adapter_scale * outer_product_sum(z_down, e_down)

    dm = g + norm_back(m, scale_two, gain_second, dn2)
    e_out = low(residual_branch_scale * dm)
    dA_out, dB_out, through_out = adapter_backward_pass(
        e_out, o, z_out, A_model[3], B_model[3], choice
    )
    e_o = low(project_back(e_out, 3) + through_out).reshape(heads)
    dq, dk, dv = attention_back(queries, keys, values, allowed, row_top, row_total, e_o)
    e_query = low(rotary_back(dq, cosine_table, sine_table))
    e_key = low(rotary_back(dk, cosine_table, sine_table))
    e_value = low(dv.reshape(count, MODEL_WIDTH))
    dA_query, dB_query, through_query = adapter_backward_pass(
        e_query, n1, z_query, A_model[0], B_model[0], choice
    )
    dA_key, dB_key, through_key = adapter_backward_pass(
        e_key, n1, z_key, A_model[1], B_model[1], choice
    )
    dA_value, dB_value, through_value = adapter_backward_pass(
        e_value, n1, z_value, A_model[2], B_model[2], choice
    )
    dn1 = (
        project_back(e_query, 0)
        + project_back(e_key, 1)
        + project_back(e_value, 2)
        + through_query
        + through_key
        + through_value
    )
    dx = dm + norm_back(x, scale_one, gain_first, dn1)

    own_hidden = FEEDFORWARD_UNITS // (dp * GROUP)
    dA_hidden = lax.dynamic_update_slice(
        jnp.zeros((dp, GROUP, own_hidden, ADAPTER_COLUMNS), jnp.float32),
        dA_down.reshape(dp, 1, padded, ADAPTER_COLUMNS)[:, :, :own_hidden],
        (0, place.q, 0, 0),
    )
    flat = jnp.concatenate(
        [
            piece.reshape(-1, ADAPTER_COLUMNS)
            for piece in (
                dA_query,
                dA_key,
                dA_value,
                dA_out,
                dA_gate,
                dA_up,
                dA_hidden,
                dB_query,
                dB_key,
                dB_value,
                dB_out,
                dB_down,
                spread_columns(place, dB_gate, dp, padded),
                spread_columns(place, dB_up, dp, padded),
            )
        ]
    )
    gradient = reduce_to_owner(place, flat)
    share = gradient.shape[0]
    offset = lax.axis_index(AXES) * share
    own_params = lax.dynamic_slice_in_dim(
        adapters.reshape(-1, ADAPTER_COLUMNS), offset, share
    ).astype(jnp.float32)
    first = first_moment_running.reshape(share, ADAPTER_COLUMNS)
    second = second_moment_running.reshape(share, ADAPTER_COLUMNS)
    fresh_first = first_decay_rate * first + (1.0 - first_decay_rate) * gradient
    fresh_second = second_decay_rate * second + (1.0 - second_decay_rate) * gradient * gradient
    unbiased_first = fresh_first / (1.0 - first_decay_rate**OPT_STEP)
    unbiased_second = fresh_second / (1.0 - second_decay_rate**OPT_STEP)
    update = (
        unbiased_first / (jnp.sqrt(unbiased_second) + adaptive_epsilon)
        + weight_shrink_rate * own_params
    )
    updated = gather_owners(place, low(own_params - learning_rate * update))

    inverse = (
        jnp.zeros_like(token_order).at[token_order].set(jnp.arange(count, dtype=jnp.int32))
    )
    back_out = lax.all_to_all(low(y)[inverse], "dp", split_axis=0, concat_axis=0, tiled=True)
    back_grad = lax.all_to_all(low(dx)[inverse], "dp", split_axis=0, concat_axis=0, tiled=True)
    return (
        back_out,
        back_grad,
        gradient.reshape(-1),
        fresh_first.reshape(-1),
        fresh_second.reshape(-1),
        updated,
    )


def solution(mesh):
    rows = P(AXES, None)
    weight = P("dp", None)
    return jax.shard_map(
        functools.partial(shards, mesh.shape["dp"], mesh.shape["shard"]),
        mesh=mesh,
        in_specs=(rows,) * 5 + (P(), P()) + (weight,) * 7 + (P(), P(AXES), P(AXES)),
        out_specs=(rows, rows, P(AXES), P(AXES), P(AXES), P()),
        check_vma=False,
    )
```

```python
import functools
import math

import jax
import jax.numpy as jnp
from jax import lax
from jax.experimental import pallas as pl
from jax.experimental.pallas import tpu as pltpu
from jax.sharding import PartitionSpec as P

MODEL_WIDTH = 2304
ATTENTION_HEADS = 36
HEAD_SIZE = 64
FEEDFORWARD_UNITS = 5760
ADAPTER_RANK = 16
OPT_STEP = 10
SEQ_DEV = 4
TOK_DEV = 256
ADAPTER_COLUMNS = 128


norm_eps = 1e-05
residual_branch_scale = 1.4 / math.sqrt(40.0)
adapter_scale = 2.0
rope_base = 10000.0
first_decay_rate = 0.9
second_decay_rate = 0.999
adaptive_epsilon = 1e-08
weight_shrink_rate = 0.01
learning_rate = 0.01


def matrix_product(left_side, right_side):
    return jnp.dot(left_side, right_side, preferred_element_type=jnp.float32)


def matrix_product_backward(left_side, right_side):
    return lax.dot_general(
        left_side, right_side, (((1,), (1,)), ((), ())), preferred_element_type=jnp.float32
    )


def outer_product_sum(left_side, right_side):
    return lax.dot_general(
        left_side, right_side, (((0,), (0,)), ((), ())), preferred_element_type=jnp.float32
    )


def low(values):
    return values.astype(jnp.bfloat16)


def block_tables(sequence_lengths, sequence_adapter_index):
    row_ids = jnp.arange(TOK_DEV, dtype=jnp.int32)
    seq_ends = jnp.cumsum(sequence_lengths, dtype=jnp.int32)
    seq_starts = seq_ends - sequence_lengths
    segment = jnp.sum(
        (row_ids[:, None] >= seq_ends[None, :]).astype(jnp.int32), axis=1, dtype=jnp.int32
    )
    member = (segment[:, None] == jnp.arange(SEQ_DEV, dtype=jnp.int32)[None, :]).astype(jnp.int32)
    position = row_ids - jnp.sum(member * seq_starts[None, :], axis=1, dtype=jnp.int32)
    token_adapter_index = jnp.sum(member * sequence_adapter_index[None, :], axis=1, dtype=jnp.int32)
    adapter_choice_index = (
        jnp.arange(ADAPTER_COLUMNS, dtype=jnp.int32)[None, :] // ADAPTER_RANK
        == token_adapter_index[:, None]
    ).astype(jnp.float32)
    allowed = (segment[:, None] == segment[None, :]) & (row_ids[None, :] <= row_ids[:, None])
    half_dim = HEAD_SIZE // 2
    inv_freq = jnp.power(rope_base, -2.0 * jnp.arange(half_dim, dtype=jnp.float32) / HEAD_SIZE)
    angles = position.astype(jnp.float32)[:, None] * inv_freq[None, :]
    cosine, sine = jnp.cos(angles), jnp.sin(angles)
    return (
        adapter_choice_index,
        allowed,
        jnp.concatenate([cosine] * 4, axis=1),
        jnp.concatenate([-sine, sine] * 2, axis=1),
    )


def restore_structure(flattened_vector):
    first_boundary = 6 * MODEL_WIDTH * ADAPTER_COLUMNS
    second_boundary = first_boundary + FEEDFORWARD_UNITS * ADAPTER_COLUMNS
    third_boundary = second_boundary + 5 * ADAPTER_COLUMNS * MODEL_WIDTH
    return (
        flattened_vector[:first_boundary].reshape(6, MODEL_WIDTH, ADAPTER_COLUMNS),
        flattened_vector[first_boundary:second_boundary].reshape(
            FEEDFORWARD_UNITS, ADAPTER_COLUMNS
        ),
        flattened_vector[second_boundary:third_boundary].reshape(5, ADAPTER_COLUMNS, MODEL_WIDTH),
        flattened_vector[third_boundary:].reshape(2, ADAPTER_COLUMNS, FEEDFORWARD_UNITS),
    )


def rms_scale(values):
    return lax.rsqrt(jnp.mean(values * values, axis=-1, keepdims=True) + norm_eps)


def norm_back(values, scale, gain, gradient_value):
    weighted = gradient_value * gain
    return scale * weighted - values * scale**3 * jnp.mean(
        values * weighted, axis=-1, keepdims=True
    )


def apply_adapter_delta(input_rows, adapter_down_pair, adapter_up_pair, adapter_choice_index):
    reduced_total = low(
        matrix_product(input_rows, adapter_down_pair) * adapter_choice_index
    )
    return (reduced_total, adapter_scale * matrix_product(reduced_total, adapter_up_pair))


def swap_halves(values):
    lane = lax.broadcasted_iota(jnp.int32, values.shape, 1)
    half, width = HEAD_SIZE // 2, values.shape[1]
    return jnp.where(
        lane % HEAD_SIZE < half, pltpu.roll(values, width - half, 1), pltpu.roll(values, half, 1)
    )


def head_scores(query, key, bias):
    scores = matrix_product_backward(query, key) * HEAD_SIZE ** (-0.5) + bias
    expanded = jnp.exp(scores - jnp.max(scores, axis=-1, keepdims=True))
    return expanded / jnp.sum(expanded, axis=-1, keepdims=True)


def attention_kernel(lin, z, up, cosine, sine, bias, qkv, attended):
    full = [lin[t] + adapter_scale * matrix_product(z[t], up[t]) for t in range(3)]
    query, key = (
        low(v * cosine[...] + swap_halves(v) * sine[...]) for v in full[:2]
    )
    value = low(full[2])
    qkv[0], qkv[1], qkv[2] = query, key, value
    first = lax.broadcasted_iota(jnp.int32, query.shape, 1) < HEAD_SIZE
    results = []
    for mine in (first, ~first):
        probs = head_scores(jnp.where(mine, query, jnp.zeros_like(query)), key, bias[...])
        results.append(matrix_product(low(probs), value))
    attended[...] = low(jnp.where(first, results[0], results[1]))


def attention_back_kernel(qkv, lin, dz, down, cosine, sine, bias, grads):
    query, key, value = qkv[0], qkv[1], qkv[2]
    grad = low(lin[...] + matrix_product_backward(dz[...], down[...]))
    first = lax.broadcasted_iota(jnp.int32, query.shape, 1) < HEAD_SIZE
    nothing = jnp.zeros_like(query)
    results = []
    for mine in (first, ~first):
        probs = head_scores(jnp.where(mine, query, nothing), key, bias[...])
        grad_probs = matrix_product_backward(jnp.where(mine, grad, nothing), value)
        row_delta = jnp.sum(probs * grad_probs, axis=-1, keepdims=True)
        grad_scores = low(probs * (grad_probs - row_delta))
        results.append(
            (
                matrix_product(grad_scores, key),
                outer_product_sum(grad_scores, query),
                outer_product_sum(low(probs), grad),
            )
        )
    scale = HEAD_SIZE ** (-0.5)
    grad_query, grad_key, grad_value = (
        jnp.where(first, one, two) for one, two in zip(*results)
    )
    for t, v in enumerate((grad_query * scale, grad_key * scale)):
        grads[t] = low(v * cosine[...] - swap_halves(v) * sine[...])
    grads[2] = low(grad_value)


def attention_call(kernel, operands, outs):
    pairs = 2 * HEAD_SIZE

    def spec(shape, axis):
        block = tuple(pairs if k == axis else n for k, n in enumerate(shape))
        return pl.BlockSpec(block, lambda i: tuple(i if k == axis else 0 for k in range(len(shape))))

    count = operands[-1][0].shape[0]
    return pl.pallas_call(
        kernel,
        grid=(ATTENTION_HEADS // 2,),
        out_shape=[jax.ShapeDtypeStruct(shape, jnp.bfloat16) for shape, _ in outs],
        in_specs=[spec(v.shape, axis) for v, axis in operands],
        out_specs=[spec(shape, axis) for shape, axis in outs],
        compiler_params=pltpu.CompilerParams(vmem_limit_bytes=48 << 20),
        cost_estimate=pl.CostEstimate(
            flops=8 * count * count * MODEL_WIDTH,
            bytes_accessed=24 * count * MODEL_WIDTH,
            transcendentals=count * count * ATTENTION_HEADS,
        ),
    )(*[v for v, _ in operands])


GROUP = 4
AXES = ("dp", "shard")


def together(*values):
    return lax.optimization_barrier(values)


class Place:
    def __init__(self, dp, shard):
        self.line, self.shard = dp // 2, shard
        i, s = lax.axis_index("dp"), lax.axis_index("shard")
        self.z, self.y, self.x, self.c = i // 2, i % 2, s // 2, s % 2
        self.q = self.y * 2 + self.c
        self.spots = [
            (z, y, x, c)
            for z in range(self.line)
            for y in range(2)
            for x in range(shard // 2)
            for c in range(2)
        ]

    def number(self, z, y, x, c):
        return (z * 2 + y) * self.shard + x * 2 + c

    def move(self, value, target):
        pairs = []
        for spot in self.spots:
            to = target(*spot)
            if to is not None:
                pairs.append((self.number(*spot), self.number(*to)))
        return lax.ppermute(value, AXES, pairs)

    def by_y(self, value):
        return self.move(value, lambda z, y, x, c: (z, 1 - y, x, c))

    def by_x(self, value):
        return self.move(value, lambda z, y, x, c: (z, y, 1 - x, c))

    def by_c(self, value):
        return self.move(value, lambda z, y, x, c: (z, y, x, 1 - c))

    def ring_z(self, value, step):
        return self.move(value, lambda z, y, x, c: ((z + step) % self.line, y, x, c))

    def all_z(self, block):
        groups = [[z * 2 + y for z in range(self.line)] for y in range(2)]
        return lax.all_gather(block, "dp", axis=0, axis_index_groups=groups)

    def other_z(self, blocks):
        return jnp.stack(
            [
                lax.dynamic_index_in_dim(blocks, (self.z + k) % self.line, 0, keepdims=False)
                for k in range(1, self.line)
            ]
        )

    def gather_group(self, rows):
        pair = jnp.concatenate([rows, self.by_y(rows)], axis=0)
        return jnp.concatenate([pair, self.by_c(pair)], axis=0)

    def sum_group(self, partial):
        rows = partial.shape[0] // GROUP
        partial = partial.reshape(GROUP, rows, -1)
        got = self.by_c(partial[2:].astype(jnp.bfloat16))
        pair = partial[:2] + got.astype(jnp.float32)
        got = self.by_y(pair[1].astype(jnp.bfloat16))
        return pair[0] + got.astype(jnp.float32)


def put(buffer, block, *where):
    block = block.reshape((1,) * len(where) + block.shape)
    return lax.dynamic_update_slice(
        buffer, block, tuple(where) + (0,) * (buffer.ndim - len(where))
    )


def put_quarter(place, planes, rest, mates):
    full = jnp.zeros((place.line, 2) + rest.shape, rest.dtype)
    full = lax.dynamic_update_slice(full, planes[:, None], (0, place.x) + (0,) * rest.ndim)
    full = put(full, rest, place.z, 1 - place.x)
    for k in range(1, place.line):
        full = put(full, mates[k - 1], (place.z + k) % place.line, 1 - place.x)
    return full.reshape((-1,) + rest.shape[1:])


class AttentionWeights:
    def __init__(self, place, weights, same, across, near):
        self.place, self.native = place, weights
        self.same, self.across, self.near = same, across, near
        self.s = place.x * 2 + place.c
        self.rows, self.half = weights[0].shape[0], weights[0].shape[1] // 2

    def full(self, t):
        place = self.place
        halves = []
        for h in range(2):
            cols = slice(h * self.half, (h + 1) * self.half)
            buffer = jnp.zeros((place.line, 2, self.rows, self.half), self.native[t].dtype)
            buffer = put(buffer, self.native[t][:, cols], place.z, place.y)
            for r in range(4):
                near = self.near[r][:, cols]
                with_r = put(buffer, near, place.z, 1 - place.y)
                for k in range(1, place.line):
                    plane = (place.z + k) % place.line
                    with_r = put(with_r, self.same[h][r][k - 1], plane, place.y)
                    with_r = put(with_r, self.across[h][r][k - 1], plane, 1 - place.y)
                buffer = jnp.where(self.s ^ r == t, with_r, buffer)
            halves.append(buffer.reshape(-1, self.half))
        return jnp.concatenate(halves, axis=1)

    def times(self, values, first, count):
        if self.rows % 16:
            return jnp.stack([matrix_product(values, self.full(first + j)) for j in range(count)])
        return self.call(values, first, count, False)

    def times_transposed(self, values, first, count):
        if self.rows % 16:
            return sum(
                matrix_product_backward(values[j], self.full(first + j)) for j in range(count)
            )
        return self.call(values, first, count, True)

    def call(self, values, first, count, back):
        place, rows, half = self.place, self.rows, self.half
        where = jnp.stack([place.z, place.y, self.s]).astype(jnp.int32)
        width, depth = 2 * half, rows * 2 * place.line
        tokens = values.shape[-2]
        shape = (tokens, depth) if back else (count, tokens, width)
        held = pl.BlockSpec(memory_space=pltpu.VMEM)
        given = pl.BlockSpec(memory_space=pl.ANY)
        pieces = (
            list(self.native[first : first + count])
            + [v for h in range(2) for v in self.same[h]]
            + [v for h in range(2) for v in self.across[h]]
            + list(self.near)
        )
        return pl.pallas_call(
            functools.partial(weights_kernel, place.line, first, count, back),
            out_shape=jax.ShapeDtypeStruct(shape, jnp.float32),
            in_specs=[pl.BlockSpec(memory_space=pltpu.SMEM), held] + [given] * len(pieces),
            out_specs=held,
            scratch_shapes=[
                pltpu.VMEM((2, count, depth, half), jnp.bfloat16),
                pltpu.SemaphoreType.DMA((2, count)),
            ],
            compiler_params=pltpu.CompilerParams(vmem_limit_bytes=56 << 20),
            cost_estimate=pl.CostEstimate(
                flops=2 * tokens * depth * width * count,
                bytes_accessed=2 * depth * width * count + 4 * math.prod(shape),
                transcendentals=0,
            ),
        )(where, values, *pieces)


def weights_kernel(line, first, count, back, where, values, *refs):
    native = refs[:count]
    same = (refs[count : count + 4], refs[count + 4 : count + 8])
    across = (refs[count + 8 : count + 12], refs[count + 12 : count + 16])
    near = refs[count + 16 : count + 20]
    out, held, sems = refs[count + 20 :]
    z, y, s = where[0], where[1], where[2]
    rows, width = native[0].shape
    half = width // 2

    def place(h, j, plane, side):
        start = pl.multiple_of(rows * (2 * plane + side), 16)
        return held.at[h, j, pl.ds(start, rows)]

    for h in range(2):
        cols = pl.ds(h * half, half)
        for j in range(count):
            pltpu.make_async_copy(
                native[j].at[:, cols], place(h, j, z, y), sems.at[h, j]
            ).start()
        for r in range(4):
            j = (s ^ r) - first

            @pl.when((j >= 0) & (j < count))
            def _():
                pltpu.make_async_copy(
                    near[r].at[:, cols], place(h, j, z, 1 - y), sems.at[h, j]
                ).start()
                for k in range(1, line):
                    plane = lax.rem(z + k, line)
                    pltpu.make_async_copy(
                        same[h][r].at[k - 1], place(h, j, plane, y), sems.at[h, j]
                    ).start()
                    pltpu.make_async_copy(
                        across[h][r].at[k - 1], place(h, j, plane, 1 - y), sems.at[h, j]
                    ).start()

    if back:
        out[...] = jnp.zeros_like(out)

    def step(i, carry):
        h, j = i // count, lax.rem(i, count)
        cols = pl.ds(pl.multiple_of(h * half, 128), half)
        pltpu.make_async_copy(held.at[h, j], held.at[h, j], sems.at[h, j]).wait()
        if back:
            out[...] += matrix_product_backward(values[j, :, cols], held[h, j])
        else:
            out[j, :, cols] = matrix_product(values[...], held[h, j])
        return carry

    lax.fori_loop(0, 2 * count, step, 0)


def columns_kernel(own, padded, quarter, value, *outs):
    each, window = GROUP * own, 2 * padded
    rows, width = value.shape
    step = pl.program_id(0)
    lane = lax.broadcasted_iota(jnp.int32, (rows, window), 1)
    for out, k in zip(outs, (quarter[0], quarter[0] ^ 2)):
        turned = []
        for n in range(2):
            start = each * (2 * step + n) + own * k
            base = jnp.minimum(start // 128, (width - window) // 128) * 128
            piece = value[:, pl.ds(pl.multiple_of(base, 128), window)].astype(jnp.float32)
            turned.append(pltpu.roll(piece, lax.rem(window + n * padded - (start - base), window), 1))
        kept = jnp.where(lane < own, turned[0], 0.0)
        kept = jnp.where((lane >= padded) & (lane < padded + own), turned[1], kept)
        out[...] = low(kept)


def hidden_columns(place, value, blocks, padded):
    rows, width = value.shape
    own = width // (blocks * GROUP)
    if padded % 64 or 2 * padded > width:

        def take(k):
            def cut(given):
                pieces = []
                for i in range(blocks):
                    start = own * (GROUP * i + k)
                    piece = given[:, start : start + own]
                    pieces.append(jnp.pad(piece, ((0, 0), (0, padded - own))))
                return jnp.concatenate(pieces, axis=1)

            return cut

        branches = [take(k) for k in range(GROUP)]
        return [lax.switch(k, branches, value) for k in (place.q, place.q ^ 2)]
    return pl.pallas_call(
        functools.partial(columns_kernel, own, padded),
        grid=(blocks // 2,),
        out_shape=[jax.ShapeDtypeStruct((rows, blocks * padded), value.dtype)] * 2,
        in_specs=[
            pl.BlockSpec(memory_space=pltpu.SMEM),
            pl.BlockSpec((rows, width), lambda i: (0, 0)),
        ],
        out_specs=[pl.BlockSpec((rows, 2 * padded), lambda i: (0, i))] * 2,
        compiler_params=pltpu.CompilerParams(vmem_limit_bytes=32 << 20),
        cost_estimate=pl.CostEstimate(
            flops=8 * rows * width, bytes_accessed=4 * rows * width, transcendentals=0
        ),
    )(place.q.astype(jnp.int32).reshape(1), value)


def hidden_rows(place, value, quarter, blocks, padded):
    own = value.shape[0] // (blocks * GROUP)
    split = value.reshape(blocks, GROUP, own, -1)
    got = lax.dynamic_index_in_dim(split, quarter, 1, keepdims=False)
    return jnp.pad(got, ((0, 0), (0, padded - own), (0, 0))).reshape(blocks * padded, -1)


def spread_kernel(own, padded, quarter, value, out, total):
    rows, width = total.shape
    window = 2 * padded
    total[...] = jnp.zeros_like(total)
    lane = lax.broadcasted_iota(jnp.int32, (rows, window), 1)
    for i in range(width // (GROUP * own)):
        pair, n = i // 2, i % 2
        start = own * (GROUP * i + quarter[0])
        base = jnp.minimum(start // 128, (width - window) // 128) * 128
        piece = value[:, pair * window : (pair + 1) * window].astype(jnp.float32)
        inside = (lane >= n * padded) & (lane < n * padded + own)
        turned = pltpu.roll(
            jnp.where(inside, piece, 0.0),
            lax.rem(window - n * padded + (start - base), window),
            1,
        )
        total[:, pl.ds(pl.multiple_of(base, 128), window)] += turned
    out[...] = low(total[...])


def spread_columns(place, value, width, blocks, padded):
    rows = value.shape[0]
    own = width // (blocks * GROUP)
    if padded % 64 or 2 * padded > width:

        def lay(k):
            def build(given):
                pieces = []
                for i in range(blocks):
                    piece = given[:, padded * i : padded * i + own]
                    pieces.append(jnp.pad(piece, ((0, 0), (own * k, own * (GROUP - 1 - k)))))
                return jnp.concatenate(pieces, axis=1)

            return build

        return lax.switch(place.q, [lay(k) for k in range(GROUP)], value)
    return pl.pallas_call(
        functools.partial(spread_kernel, own, padded),
        out_shape=jax.ShapeDtypeStruct((rows, width), jnp.bfloat16),
        in_specs=[
            pl.BlockSpec(memory_space=pltpu.SMEM),
            pl.BlockSpec(memory_space=pltpu.VMEM),
        ],
        out_specs=pl.BlockSpec(memory_space=pltpu.VMEM),
        scratch_shapes=[pltpu.VMEM((rows, width), jnp.float32)],
        compiler_params=pltpu.CompilerParams(vmem_limit_bytes=32 << 20),
        cost_estimate=pl.CostEstimate(
            flops=8 * rows * width, bytes_accessed=4 * rows * width, transcendentals=0
        ),
    )(place.q.astype(jnp.int32).reshape(1), value)


def both(kept, got):
    return low(kept.astype(jnp.float32) + got.astype(jnp.float32))


def pick(values, index, axis):
    return lax.dynamic_index_in_dim(values, index, axis, keepdims=False)


def reduce_over_cores(place, flat):
    pairs = place.line * 2 * (place.shard // 2)
    rows = flat.shape[0] // pairs
    half = -(-rows // 16) * 8
    split = flat.reshape(place.line, 2, place.shard // 2, rows, ADAPTER_COLUMNS)
    start = rows - half
    keep = lax.dynamic_slice_in_dim(split, place.c * start, half, 3)
    send = lax.dynamic_slice_in_dim(split, (1 - place.c) * start, half, 3)
    return both(keep, place.by_c(send))


def reduce_to_owner(place, total, share):
    half = total.shape[3]
    cut = half // 16 * 8
    one, two = total[:, :, :, :cut], total[:, :, :, cut:]
    got_one = place.by_y(pick(one, 1 - place.y, 1))
    got_two = place.by_x(pick(two, 1 - place.x, 2))
    one, two = both(pick(one, place.y, 1), got_one), both(pick(two, place.x, 2), got_two)
    got_one = place.by_x(pick(one, 1 - place.x, 1))
    got_two = place.by_y(pick(two, 1 - place.y, 1))
    one, two = both(pick(one, place.x, 1), got_one), both(pick(two, place.y, 1), got_two)
    total = jnp.concatenate([one, two], axis=1)
    result = pick(total, place.z, 0).astype(jnp.float32)
    for k in range(1, place.line):
        send = pick(total, (place.z + k) % place.line, 0)
        result = result + place.ring_z(send, k).astype(jnp.float32)
    return lax.dynamic_slice_in_dim(result, place.c * (half - share), share, 0)


def gather_owners(place, own):
    share = own.shape[0]
    half = -(-share // 8) * 8
    start = 2 * share - half
    mate = place.by_c(own)
    head, tail = jnp.where(place.c == 0, own, mate), jnp.where(place.c == 0, mate, own)
    pair = jnp.concatenate([head, tail], axis=0)
    planes = place.all_z(lax.dynamic_slice_in_dim(pair, place.c * start, half, 0))
    cut = half // 16 * 8
    full = jnp.zeros(
        (place.line, 2, place.shard // 2, 2 * share, ADAPTER_COLUMNS), own.dtype
    )
    for part, x_first, at in ((planes[:, :cut], True, 0), (planes[:, cut:], False, cut)):
        x_part, y_part = place.by_x(part), place.by_y(part)
        xy_part = place.by_y(x_part) if x_first else place.by_x(y_part)
        for value, y, x in (
            (part, place.y, place.x),
            (x_part, place.y, 1 - place.x),
            (y_part, 1 - place.y, place.x),
            (xy_part, 1 - place.y, 1 - place.x),
        ):
            for held, c in ((value, place.c), (place.by_c(value), 1 - place.c)):
                where = (0, y, x, c * start + at, 0)
                full = lax.dynamic_update_slice(full, held[:, None, None], where)
    return full.reshape(-1)


def shards(
    dp,
    shard,
    tokens,
    cotangent,
    arrival,
    lengths,
    adapter_set,
    gain_one,
    gain_two,
    w_query,
    w_key,
    w_value,
    w_out,
    w_gate,
    w_up,
    w_down,
    adapters,
    first_moment_running,
    second_moment_running,
):
    place = Place(dp, shard)
    token_order = arrival[0]
    count = token_order.shape[0]
    padded = -(-(FEEDFORWARD_UNITS // (dp * GROUP)) // 16) * 16


    weights = (w_query, w_key, w_value, w_out)
    s, half = place.x * 2 + place.c, MODEL_WIDTH // 2
    stacked = jnp.stack(weights)
    mine = lax.dynamic_index_in_dim(stacked, s, 0, keepdims=False)
    first = place.all_z(mine[:, :half])
    second = place.all_z(mine[:, half:])
    near_y = place.by_y(mine)
    table = jnp.concatenate([lengths, adapter_set], axis=1)
    table_y = place.by_y(table)
    own_gate, other_gate = hidden_columns(place, w_gate, dp, padded)
    own_up, other_up = hidden_columns(place, w_up, dp, padded)
    near_y, table_y, other_gate, other_up = together(near_y, table_y, other_gate, other_up)

    near_x = place.by_x(near_y)
    got_gate, got_up = place.by_y(other_gate), place.by_y(other_up)
    near_y_c = place.by_c(near_y)
    tables = jnp.concatenate([table, table_y], axis=0)
    tables_c = place.by_c(tables)
    own_down = hidden_rows(place, w_down, place.q, 1, padded)
    other_down = hidden_rows(place, w_down, place.q ^ 2, 1, padded)
    first, got_gate, got_up, near_x, near_y_c, tables_c, tokens = together(
        first, got_gate, got_up, near_x, near_y_c, tables_c, tokens
    )

    straight = place.y == place.x
    gate_planes = place.all_z(jnp.where(straight, own_gate, got_gate))
    up_planes = place.all_z(jnp.where(straight, own_up, got_up))
    gate_rest, up_rest = (
        jnp.where(straight, got_gate, own_gate),
        jnp.where(straight, got_up, own_up),
    )
    tables = jnp.concatenate([tables, tables_c], axis=0)
    lines = place.other_z(first)
    x0, y0, lines_c = place.by_x(lines), place.by_y(lines), place.by_c(lines)
    near_x_c = place.by_c(near_x)
    arrived_x = lax.all_to_all(tokens, "dp", split_axis=0, concat_axis=0, tiled=True)
    x0, y0, lines_c, near_x_c, second, cotangent = together(
        x0, y0, lines_c, near_x_c, second, cotangent
    )

    lines2 = place.other_z(second)
    x1, y1, lines2_c = place.by_x(lines2), place.by_y(lines2), place.by_c(lines2)
    x0_c, y0_c = place.by_c(x0), place.by_c(y0)
    x1, y1, lines2_c, x0_c, y0_c, x0, other_down, arrived_x, cotangent = together(
        x1, y1, lines2_c, x0_c, y0_c, x0, other_down, arrived_x, cotangent
    )

    arrived_cot = lax.all_to_all(cotangent, "dp", split_axis=0, concat_axis=0, tiled=True)
    xy0, xy1, got_down = place.by_y(x0), place.by_x(y1), place.by_y(other_down)
    x1_c, y1_c = place.by_c(x1), place.by_c(y1)
    xy0, xy1, x1_c, y1_c, gate_planes, got_down = together(
        xy0, xy1, x1_c, y1_c, gate_planes, got_down
    )

    down_planes = place.all_z(jnp.where(straight, own_down, got_down))
    down_rest = jnp.where(straight, got_down, own_down)
    gate_mates = place.by_x(place.other_z(gate_planes))
    attention = AttentionWeights(
        place,
        weights,
        ((lines, lines_c, x0, x0_c), (lines2, lines2_c, x1, x1_c)),
        ((y0, y0_c, xy0, place.by_c(xy0)), (y1, y1_c, xy1, place.by_c(xy1))),
        (near_y, near_y_c, near_x, near_x_c),
    )
    A_model, A_hidden, B_model, B_hidden = restore_structure(adapters)
    choice, allowed, cosine_table, sine_table = block_tables(lengths[0], adapter_set[0])
    choices = jnp.concatenate(
        [block_tables(tables[k, :SEQ_DEV], tables[k, SEQ_DEV:])[0] for k in range(GROUP)], axis=0
    )
    gain_first = gain_one.astype(jnp.float32)
    gain_second = gain_two.astype(jnp.float32)

    x = arrived_x[token_order].astype(jnp.float32)
    scale_one = rms_scale(x)
    n1 = low(x * scale_one * gain_first)

    z_qkv = low(
        jnp.einsum("nd,tdr->tnr", n1, A_model[:3], preferred_element_type=jnp.float32) * choice
    )
    bias = jnp.where(allowed, 0.0, -jnp.inf)
    qkv, o = attention_call(
        attention_kernel,
        (
            (attention.times(n1, 0, 3), 2),
            (z_qkv, None),
            (B_model[:3], 2),
            (cosine_table, None),
            (sine_table, None),
            (bias, None),
        ),
        (((3, count, MODEL_WIDTH), 2), ((count, MODEL_WIDTH), 1)),
    )
    o, up_planes, arrived_cot = together(o, up_planes, arrived_cot)
    up_mates = place.by_x(place.other_z(up_planes))
    z_out, delta_out = apply_adapter_delta(o, A_model[3], B_model[3], choice)
    m = x + residual_branch_scale * (attention.times(o, 3, 1)[0] + delta_out)
    scale_two = rms_scale(m)
    n2 = low(m * scale_two * gain_second)

    g = arrived_cot[token_order].astype(jnp.float32)
    e_down = low(residual_branch_scale * g)
    dz_down = low(adapter_scale * matrix_product_backward(e_down, B_model[4]) * choice)
    sent = jnp.concatenate([e_down, dz_down], axis=1)
    sent_pair = jnp.concatenate([sent, place.by_y(sent)], axis=0)
    gate_mates, down_planes, n2 = together(gate_mates, down_planes, n2)
    down_mates = place.by_x(place.other_z(down_planes))
    n2_all = place.gather_group(n2)
    sent = jnp.concatenate([sent_pair, place.by_c(sent_pair)], axis=0)
    gate = put_quarter(place, gate_planes, gate_rest, gate_mates)
    up_part = put_quarter(place, up_planes, up_rest, up_mates)
    down = put_quarter(place, down_planes, down_rest, down_mates)
    e_down_all, dz_down_all = sent[:, :MODEL_WIDTH], sent[:, MODEL_WIDTH:]
    B_gate, _ = hidden_columns(place, B_hidden[0], dp, padded)
    B_up, _ = hidden_columns(place, B_hidden[1], dp, padded)
    A_down = hidden_rows(place, A_hidden, place.q, dp, padded)
    z_gate = low(matrix_product(n2_all, A_model[4]) * choices)
    z_up = low(matrix_product(n2_all, A_model[5]) * choices)
    gt = matrix_product(n2_all, gate) + adapter_scale * matrix_product(z_gate, B_gate)
    up = matrix_product(n2_all, up_part) + adapter_scale * matrix_product(z_up, B_up)
    sg = jax.nn.sigmoid(gt)
    act = gt * sg
    h = low(act * up)
    dh = matrix_product_backward(e_down_all, down) + matrix_product_backward(dz_down_all, A_down)
    e_gate = low(dh * up * (sg + gt * sg * (1.0 - sg)))
    e_up = low(dh * act)
    back_sum = place.sum_group(
        jnp.concatenate(
            [
                matrix_product_backward(e_gate, gate)
                + matrix_product_backward(e_up, up_part),
                matrix_product_backward(e_gate, B_gate),
                matrix_product_backward(e_up, B_up),
                matrix_product(h, A_down),
            ],
            axis=1,
        )
    )
    cuts = [MODEL_WIDTH + k * ADAPTER_COLUMNS for k in range(3)]
    dz_gate, dz_up, z_down = jnp.split(back_sum, cuts, axis=1)[1:]
    dz_gate, dz_up = low(adapter_scale * dz_gate * choice), low(adapter_scale * dz_up * choice)
    z_down = low(z_down * choice)
    dn2 = (
        back_sum[:, :MODEL_WIDTH]
        + matrix_product_backward(dz_gate, A_model[4])
        + matrix_product_backward(dz_up, A_model[5])
    )
    dA_gate, dA_up = outer_product_sum(n2, dz_gate), outer_product_sum(n2, dz_up)
    dB_gate = adapter_scale * outer_product_sum(z_gate, e_gate)
    dB_up = adapter_scale * outer_product_sum(z_up, e_up)
    dA_down = outer_product_sum(h, dz_down_all)
    dB_down = adapter_scale * outer_product_sum(z_down, e_down)

    dm = g + norm_back(m, scale_two, gain_second, dn2)
    e_out = low(residual_branch_scale * dm)
    dz_out = low(adapter_scale * matrix_product_backward(e_out, B_model[3]) * choice)
    (e_qkv,) = attention_call(
        attention_back_kernel,
        (
            (qkv, 2),
            (attention.times_transposed(e_out[None], 3, 1), 1),
            (dz_out, None),
            (A_model[3], 0),
            (cosine_table, None),
            (sine_table, None),
            (bias, None),
        ),
        (((3, count, MODEL_WIDTH), 2),),
    )
    dA_out, dB_out = outer_product_sum(o, dz_out), adapter_scale * outer_product_sum(z_out, e_out)
    dz_qkv = low(
        adapter_scale
        * jnp.einsum("tnd,trd->tnr", e_qkv, B_model[:3], preferred_element_type=jnp.float32)
        * choice
    )
    dA_qkv = jnp.einsum("nd,tnr->tdr", n1, dz_qkv, preferred_element_type=jnp.float32)
    dB_qkv = adapter_scale * jnp.einsum(
        "tnr,tnd->trd", z_qkv, e_qkv, preferred_element_type=jnp.float32
    )
    own_hidden = FEEDFORWARD_UNITS // (dp * GROUP)
    dA_hidden = lax.dynamic_update_slice(
        jnp.zeros((dp, GROUP, own_hidden, ADAPTER_COLUMNS), jnp.bfloat16),
        low(dA_down).reshape(dp, 1, padded, ADAPTER_COLUMNS)[:, :, :own_hidden],
        (0, place.q, 0, 0),
    )
    flat = jnp.concatenate(
        [
            low(piece).reshape(-1, ADAPTER_COLUMNS)
            for piece in (
                dA_qkv,
                dA_out,
                dA_gate,
                dA_up,
                dA_hidden,
                dB_qkv,
                dB_out,
                dB_down,
                spread_columns(place, low(dB_gate), FEEDFORWARD_UNITS, dp, padded),
                spread_columns(place, low(dB_up), FEEDFORWARD_UNITS, dp, padded),
            )
        ]
    )
    flat, e_qkv, dz_qkv = together(flat, e_qkv, dz_qkv)
    total = reduce_over_cores(place, flat)
    dn1 = attention.times_transposed(e_qkv, 0, 3) + jnp.einsum(
        "tnr,tdr->nd", dz_qkv, A_model[:3], preferred_element_type=jnp.float32
    )
    dx = dm + norm_back(x, scale_one, gain_first, dn1)
    total, h = together(total, h)
    y = m + residual_branch_scale * (
        place.sum_group(matrix_product(h, down))
        + adapter_scale * matrix_product(z_down, B_model[4])
    )
    share = flat.shape[0] // (dp * shard)
    gradient = reduce_to_owner(place, total, share)
    offset = lax.axis_index(AXES) * share
    own_params = lax.dynamic_slice_in_dim(
        adapters.reshape(-1, ADAPTER_COLUMNS), offset, share
    ).astype(jnp.float32)
    first = first_moment_running.reshape(share, ADAPTER_COLUMNS)
    second = second_moment_running.reshape(share, ADAPTER_COLUMNS)
    fresh_first = first_decay_rate * first + (1.0 - first_decay_rate) * gradient
    fresh_second = second_decay_rate * second + (1.0 - second_decay_rate) * gradient * gradient
    unbiased_first = fresh_first / (1.0 - first_decay_rate**OPT_STEP)
    unbiased_second = fresh_second / (1.0 - second_decay_rate**OPT_STEP)
    update = (
        unbiased_first / (jnp.sqrt(unbiased_second) + adaptive_epsilon)
        + weight_shrink_rate * own_params
    )
    updated = gather_owners(place, low(own_params - learning_rate * update))

    inverse = (
        jnp.zeros_like(token_order).at[token_order].set(jnp.arange(count, dtype=jnp.int32))
    )
    back_out = lax.all_to_all(low(y)[inverse], "dp", split_axis=0, concat_axis=0, tiled=True)
    back_grad = lax.all_to_all(low(dx)[inverse], "dp", split_axis=0, concat_axis=0, tiled=True)
    return (
        back_out,
        back_grad,
        gradient.reshape(-1),
        fresh_first.reshape(-1),
        fresh_second.reshape(-1),
        updated,
    )


def solution(mesh):
    rows = P(AXES, None)
    weight = P("dp", None)
    return jax.shard_map(
        functools.partial(shards, mesh.shape["dp"], mesh.shape["shard"]),
        mesh=mesh,
        in_specs=(rows,) * 5 + (P(), P()) + (weight,) * 7 + (P(), P(AXES), P(AXES)),
        out_specs=(rows, rows, P(AXES), P(AXES), P(AXES), P()),
        check_vma=False,
    )
```

```python
import functools
import math

import jax
import jax.numpy as jnp
from jax import lax
from jax.experimental import pallas as pl
from jax.experimental.pallas import tpu as pltpu
from jax.sharding import PartitionSpec as P

MODEL_WIDTH = 2304
ATTENTION_HEADS = 36
HEAD_SIZE = 64
FEEDFORWARD_UNITS = 5760
ADAPTER_RANK = 16
OPT_STEP = 10
SEQ_DEV = 4
TOK_DEV = 256
ADAPTER_COLUMNS = 128


norm_eps = 1e-05
residual_branch_scale = 1.4 / math.sqrt(40.0)
adapter_scale = 2.0
rope_base = 10000.0
first_decay_rate = 0.9
second_decay_rate = 0.999
adaptive_epsilon = 1e-08
weight_shrink_rate = 0.01
learning_rate = 0.01


def matrix_product(left_side, right_side):
    return jnp.dot(left_side, right_side, preferred_element_type=jnp.float32)


def matrix_product_backward(left_side, right_side):
    return lax.dot_general(
        left_side, right_side, (((1,), (1,)), ((), ())), preferred_element_type=jnp.float32
    )


def outer_product_sum(left_side, right_side):
    return lax.dot_general(
        left_side, right_side, (((0,), (0,)), ((), ())), preferred_element_type=jnp.float32
    )


def low(values):
    return values.astype(jnp.bfloat16)


def block_tables(sequence_lengths, sequence_adapter_index):
    row_ids = jnp.arange(TOK_DEV, dtype=jnp.int32)
    seq_ends = jnp.cumsum(sequence_lengths, dtype=jnp.int32)
    seq_starts = seq_ends - sequence_lengths
    segment = jnp.sum(
        (row_ids[:, None] >= seq_ends[None, :]).astype(jnp.int32), axis=1, dtype=jnp.int32
    )
    member = (segment[:, None] == jnp.arange(SEQ_DEV, dtype=jnp.int32)[None, :]).astype(jnp.int32)
    position = row_ids - jnp.sum(member * seq_starts[None, :], axis=1, dtype=jnp.int32)
    token_adapter_index = jnp.sum(member * sequence_adapter_index[None, :], axis=1, dtype=jnp.int32)
    adapter_choice_index = (
        jnp.arange(ADAPTER_COLUMNS, dtype=jnp.int32)[None, :] // ADAPTER_RANK
        == token_adapter_index[:, None]
    ).astype(jnp.float32)
    allowed = (segment[:, None] == segment[None, :]) & (row_ids[None, :] <= row_ids[:, None])
    half_dim = HEAD_SIZE // 2
    inv_freq = jnp.power(rope_base, -2.0 * jnp.arange(half_dim, dtype=jnp.float32) / HEAD_SIZE)
    angles = position.astype(jnp.float32)[:, None] * inv_freq[None, :]
    cosine, sine = jnp.cos(angles), jnp.sin(angles)
    return (
        adapter_choice_index,
        allowed,
        jnp.concatenate([cosine] * 4, axis=1),
        jnp.concatenate([-sine, sine] * 2, axis=1),
    )


def restore_structure(flattened_vector):
    first_boundary = 6 * MODEL_WIDTH * ADAPTER_COLUMNS
    second_boundary = first_boundary + FEEDFORWARD_UNITS * ADAPTER_COLUMNS
    third_boundary = second_boundary + 5 * ADAPTER_COLUMNS * MODEL_WIDTH
    return (
        flattened_vector[:first_boundary].reshape(6, MODEL_WIDTH, ADAPTER_COLUMNS),
        flattened_vector[first_boundary:second_boundary].reshape(
            FEEDFORWARD_UNITS, ADAPTER_COLUMNS
        ),
        flattened_vector[second_boundary:third_boundary].reshape(5, ADAPTER_COLUMNS, MODEL_WIDTH),
        flattened_vector[third_boundary:].reshape(2, ADAPTER_COLUMNS, FEEDFORWARD_UNITS),
    )


def rms_scale(values):
    return lax.rsqrt(jnp.mean(values * values, axis=-1, keepdims=True) + norm_eps)


def norm_back(values, scale, gain, gradient_value):
    weighted = gradient_value * gain
    return scale * weighted - values * scale**3 * jnp.mean(
        values * weighted, axis=-1, keepdims=True
    )


def apply_adapter_delta(input_rows, adapter_down_pair, adapter_up_pair, adapter_choice_index):
    reduced_total = low(
        matrix_product(input_rows, adapter_down_pair) * adapter_choice_index
    )
    return (reduced_total, adapter_scale * matrix_product(reduced_total, adapter_up_pair))


def swap_halves(values):
    lane = lax.broadcasted_iota(jnp.int32, values.shape, 1)
    half, width = HEAD_SIZE // 2, values.shape[1]
    return jnp.where(
        lane % HEAD_SIZE < half, pltpu.roll(values, width - half, 1), pltpu.roll(values, half, 1)
    )


def head_scores(query, key, bias):
    scores = matrix_product_backward(query, key) * HEAD_SIZE ** (-0.5) + bias
    expanded = jnp.exp(scores - jnp.max(scores, axis=-1, keepdims=True))
    return expanded / jnp.sum(expanded, axis=-1, keepdims=True)


def attention_kernel(lin, z, up, cosine, sine, bias, qkv, attended):
    full = [lin[t] + adapter_scale * matrix_product(z[t], up[t]) for t in range(3)]
    query, key = (
        low(v * cosine[...] + swap_halves(v) * sine[...]) for v in full[:2]
    )
    value = low(full[2])
    qkv[0], qkv[1], qkv[2] = query, key, value
    first = lax.broadcasted_iota(jnp.int32, query.shape, 1) < HEAD_SIZE
    results = []
    for mine in (first, ~first):
        probs = head_scores(jnp.where(mine, query, jnp.zeros_like(query)), key, bias[...])
        results.append(matrix_product(low(probs), value))
    attended[...] = low(jnp.where(first, results[0], results[1]))


def attention_back_kernel(qkv, lin, dz, down, cosine, sine, bias, grads):
    query, key, value = qkv[0], qkv[1], qkv[2]
    grad = low(lin[...] + matrix_product_backward(dz[...], down[...]))
    first = lax.broadcasted_iota(jnp.int32, query.shape, 1) < HEAD_SIZE
    nothing = jnp.zeros_like(query)
    results = []
    for mine in (first, ~first):
        probs = head_scores(jnp.where(mine, query, nothing), key, bias[...])
        grad_probs = matrix_product_backward(jnp.where(mine, grad, nothing), value)
        row_delta = jnp.sum(probs * grad_probs, axis=-1, keepdims=True)
        grad_scores = low(probs * (grad_probs - row_delta))
        results.append(
            (
                matrix_product(grad_scores, key),
                outer_product_sum(grad_scores, query),
                outer_product_sum(low(probs), grad),
            )
        )
    scale = HEAD_SIZE ** (-0.5)
    grad_query, grad_key, grad_value = (
        jnp.where(first, one, two) for one, two in zip(*results)
    )
    for t, v in enumerate((grad_query * scale, grad_key * scale)):
        grads[t] = low(v * cosine[...] - swap_halves(v) * sine[...])
    grads[2] = low(grad_value)


def attention_call(kernel, operands, outs):
    pairs = 2 * HEAD_SIZE

    def spec(shape, axis):
        block = tuple(pairs if k == axis else n for k, n in enumerate(shape))
        return pl.BlockSpec(block, lambda i: tuple(i if k == axis else 0 for k in range(len(shape))))

    count = operands[-1][0].shape[0]
    return pl.pallas_call(
        kernel,
        grid=(ATTENTION_HEADS // 2,),
        out_shape=[jax.ShapeDtypeStruct(shape, jnp.bfloat16) for shape, _ in outs],
        in_specs=[spec(v.shape, axis) for v, axis in operands],
        out_specs=[spec(shape, axis) for shape, axis in outs],
        compiler_params=pltpu.CompilerParams(vmem_limit_bytes=48 << 20),
        cost_estimate=pl.CostEstimate(
            flops=8 * count * count * MODEL_WIDTH // 16,
            bytes_accessed=24 * count * MODEL_WIDTH // 16,
            transcendentals=0,
        ),
    )(*[v for v, _ in operands])


GROUP = 4
AXES = ("dp", "shard")


def together(*values):
    return lax.optimization_barrier(values)


class Place:
    def __init__(self, dp, shard):
        self.line, self.shard = dp // 2, shard
        i, s = lax.axis_index("dp"), lax.axis_index("shard")
        self.z, self.y, self.x, self.c = i // 2, i % 2, s // 2, s % 2
        self.q = self.y * 2 + self.c
        self.spots = [
            (z, y, x, c)
            for z in range(self.line)
            for y in range(2)
            for x in range(shard // 2)
            for c in range(2)
        ]

    def number(self, z, y, x, c):
        return (z * 2 + y) * self.shard + x * 2 + c

    def move(self, value, target):
        pairs = []
        for spot in self.spots:
            to = target(*spot)
            if to is not None:
                pairs.append((self.number(*spot), self.number(*to)))
        return lax.ppermute(value, AXES, pairs)

    def by_y(self, value):
        return self.move(value, lambda z, y, x, c: (z, 1 - y, x, c))

    def by_x(self, value):
        return self.move(value, lambda z, y, x, c: (z, y, 1 - x, c))

    def by_c(self, value):
        return self.move(value, lambda z, y, x, c: (z, y, x, 1 - c))

    def ring_z(self, value, step):
        return self.move(value, lambda z, y, x, c: ((z + step) % self.line, y, x, c))

    def all_z(self, block):
        groups = [[z * 2 + y for z in range(self.line)] for y in range(2)]
        return lax.all_gather(block, "dp", axis=0, axis_index_groups=groups)

    def other_z(self, blocks):
        return jnp.stack(
            [
                lax.dynamic_index_in_dim(blocks, (self.z + k) % self.line, 0, keepdims=False)
                for k in range(1, self.line)
            ]
        )

    def gather_group(self, rows):
        pair = jnp.concatenate([rows, self.by_y(rows)], axis=0)
        return jnp.concatenate([pair, self.by_c(pair)], axis=0)

    def half_sum(self, keep, send):
        return (keep + self.by_c(send).astype(jnp.float32)).reshape(2, -1, keep.shape[1])


def put(buffer, block, *where):
    block = block.reshape((1,) * len(where) + block.shape)
    return lax.dynamic_update_slice(
        buffer, block, tuple(where) + (0,) * (buffer.ndim - len(where))
    )


def put_quarter(place, planes, rest, mates):
    full = jnp.zeros((place.line, 2) + rest.shape, rest.dtype)
    full = lax.dynamic_update_slice(full, planes[:, None], (0, place.x) + (0,) * rest.ndim)
    full = put(full, rest, place.z, 1 - place.x)
    for k in range(1, place.line):
        full = put(full, mates[k - 1], (place.z + k) % place.line, 1 - place.x)
    return full.reshape((-1,) + rest.shape[1:])


class AttentionWeights:
    def __init__(self, place, weights, same, across, near):
        self.place, self.native = place, weights
        self.same, self.across, self.near = same, across, near
        self.s = place.x * 2 + place.c
        self.rows, self.half = weights[0].shape[0], weights[0].shape[1] // 2

    def full(self, t):
        place = self.place
        halves = []
        for h in range(2):
            cols = slice(h * self.half, (h + 1) * self.half)
            buffer = jnp.zeros((place.line, 2, self.rows, self.half), self.native[t].dtype)
            buffer = put(buffer, self.native[t][:, cols], place.z, place.y)
            for r in range(4):
                near = self.near[r][:, cols]
                with_r = put(buffer, near, place.z, 1 - place.y)
                for k in range(1, place.line):
                    plane = (place.z + k) % place.line
                    with_r = put(with_r, self.same[h][r][k - 1], plane, place.y)
                    with_r = put(with_r, self.across[h][r][k - 1], plane, 1 - place.y)
                buffer = jnp.where(self.s ^ r == t, with_r, buffer)
            halves.append(buffer.reshape(-1, self.half))
        return jnp.concatenate(halves, axis=1)

    def times(self, values, first, count):
        if self.rows % 16:
            return jnp.stack([matrix_product(values, self.full(first + j)) for j in range(count)])
        return self.call(values, first, count, False)

    def times_transposed(self, values, first, count):
        if self.rows % 16:
            return sum(
                matrix_product_backward(values[j], self.full(first + j)) for j in range(count)
            )
        return self.call(values, first, count, True)

    def call(self, values, first, count, back):
        place, rows, half = self.place, self.rows, self.half
        where = jnp.stack([place.z, place.y, self.s]).astype(jnp.int32)
        width, depth = 2 * half, rows * 2 * place.line
        tokens = values.shape[-2]
        shape = (tokens, depth) if back else (count, tokens, width)
        held = pl.BlockSpec(memory_space=pltpu.VMEM)
        given = pl.BlockSpec(memory_space=pl.ANY)
        pieces = (
            list(self.native[first : first + count])
            + [v for h in range(2) for v in self.same[h]]
            + [v for h in range(2) for v in self.across[h]]
            + list(self.near)
        )
        return pl.pallas_call(
            functools.partial(weights_kernel, place.line, first, count, back),
            out_shape=jax.ShapeDtypeStruct(shape, jnp.float32),
            in_specs=[pl.BlockSpec(memory_space=pltpu.SMEM), held] + [given] * len(pieces),
            out_specs=held,
            scratch_shapes=[
                pltpu.VMEM((2, count, depth, half), jnp.bfloat16),
                pltpu.SemaphoreType.DMA((2, count)),
            ],
            compiler_params=pltpu.CompilerParams(vmem_limit_bytes=56 << 20),
            cost_estimate=pl.CostEstimate(
                flops=2 * tokens * depth * width * count // 16,
                bytes_accessed=2 * depth * width * count // 16,
                transcendentals=0,
            ),
        )(where, values, *pieces)


def weights_kernel(line, first, count, back, where, values, *refs):
    native = refs[:count]
    same = (refs[count : count + 4], refs[count + 4 : count + 8])
    across = (refs[count + 8 : count + 12], refs[count + 12 : count + 16])
    near = refs[count + 16 : count + 20]
    out, held, sems = refs[count + 20 :]
    z, y, s = where[0], where[1], where[2]
    rows, width = native[0].shape
    half = width // 2

    def place(h, j, plane, side):
        start = pl.multiple_of(rows * (2 * plane + side), 16)
        return held.at[h, j, pl.ds(start, rows)]

    for h in range(2):
        cols = pl.ds(h * half, half)
        for j in range(count):
            pltpu.make_async_copy(
                native[j].at[:, cols], place(h, j, z, y), sems.at[h, j]
            ).start()
        for r in range(4):
            j = (s ^ r) - first

            @pl.when((j >= 0) & (j < count))
            def _():
                pltpu.make_async_copy(
                    near[r].at[:, cols], place(h, j, z, 1 - y), sems.at[h, j]
                ).start()
                for k in range(1, line):
                    plane = lax.rem(z + k, line)
                    pltpu.make_async_copy(
                        same[h][r].at[k - 1], place(h, j, plane, y), sems.at[h, j]
                    ).start()
                    pltpu.make_async_copy(
                        across[h][r].at[k - 1], place(h, j, plane, 1 - y), sems.at[h, j]
                    ).start()

    if back:
        out[...] = jnp.zeros_like(out)

    def step(i, carry):
        h, j = i // count, lax.rem(i, count)
        cols = pl.ds(pl.multiple_of(h * half, 128), half)
        pltpu.make_async_copy(held.at[h, j], held.at[h, j], sems.at[h, j]).wait()
        if back:
            out[...] += matrix_product_backward(values[j, :, cols], held[h, j])
        else:
            out[j, :, cols] = matrix_product(values[...], held[h, j])
        return carry

    lax.fori_loop(0, 2 * count, step, 0)


HIDDEN_TILE = 256


def quarter_copies(line, z, x, pieces, target, sem):
    planes, rest, mates = pieces
    rows = rest.shape[0]

    def copy(source, plane, side):
        start = pl.multiple_of(rows * (2 * plane + side), 16)
        pltpu.make_async_copy(source, target.at[pl.ds(start, rows)], sem).start()

    for plane in range(line):
        copy(planes.at[plane], plane, x)
    copy(rest, z, 1 - x)
    for k in range(1, line):
        copy(mates.at[k - 1], lax.rem(z + k, line), 1 - x)


def hidden_kernel(line, where, values, choices, down, up, planes, rest, mates, out, reduced, held, sems):
    step = pl.program_id(0)
    tiles = held.shape[0]

    @pl.when(step == 0)
    def _():
        def start(tile, carry):
            cols = pl.ds(pl.multiple_of(tile * HIDDEN_TILE, 128), HIDDEN_TILE)
            pieces = (planes.at[:, :, cols], rest.at[:, cols], mates.at[:, :, cols])
            quarter_copies(line, where[0], where[2], pieces, held.at[tile], sems.at[tile])
            return carry

        lax.fori_loop(0, tiles, start, 0)
        reduced[...] = low(matrix_product(values[...], down[...]) * choices[...])

    pltpu.make_async_copy(held.at[step], held.at[step], sems.at[step]).wait()
    out[...] = matrix_product(values[...], held[step]) + adapter_scale * matrix_product(
        reduced[...], up[...]
    )


def down_copies(line, where, left, right, target, sems):
    planes, rest, mates = left
    z, y, x = where[0], where[1], where[2]
    rows, cut = rest.shape

    def copy(source, plane, side, cols):
        block = 2 * plane + side
        start = pl.multiple_of(rows * block, 16)
        pltpu.make_async_copy(source, target.at[pl.ds(start, rows), cols], sems.at[block]).start()

    first, second = pl.ds(0, cut), pl.ds(cut, target.shape[1] - cut)
    for plane in range(line):
        copy(planes.at[plane], plane, x, first)
        copy(right.at[plane, 0], plane, y, second)
        copy(right.at[plane, 1], plane, 1 - y, second)
    copy(rest, z, 1 - x, first)
    for k in range(1, line):
        copy(mates.at[k - 1], lax.rem(z + k, line), 1 - x, first)


def wait_rows(target, rows, sems, block):
    part = target.at[pl.ds(pl.multiple_of(rows * block, 16), rows)]
    pltpu.make_async_copy(part, part, sems.at[block]).wait()


def feed_forward_back_kernel(line, where, gt, up, sent, down_lower, upper_gate, upper_up, *refs):
    left, right, gate_pieces, up_pieces = refs[:3], refs[3], refs[4:7], refs[7:10]
    hidden, e_gate, e_up, keep, send, total, down, held, down_sems, sems = refs[10:]
    step = pl.program_id(0)
    tiles, rows = held.shape[1], left[1].shape[0]
    blocks, width = 2 * line, down.shape[1]

    @pl.when(step == 0)
    def _():
        down_copies(line, where, left, right, down, down_sems)

        def start(tile, carry):
            cols = pl.ds(pl.multiple_of(tile * HIDDEN_TILE, 128), HIDDEN_TILE)
            for t, (planes, rest, mates) in enumerate((gate_pieces, up_pieces)):
                pieces = (planes.at[:, :, cols], rest.at[:, cols], mates.at[:, :, cols])
                quarter_copies(line, where[0], where[2], pieces, held.at[t, tile], sems.at[t, tile])
            return carry

        lax.fori_loop(0, tiles, start, 0)
        keep[...] = jnp.zeros_like(keep)
        total[...] = jnp.zeros_like(total)

    seen = 0
    for tile in range(tiles):
        until = -(-(tile + 1) * HIDDEN_TILE // rows)

        @pl.when(step == tile)
        def _(seen=seen, until=until):
            for block in range(seen, until):
                wait_rows(down, rows, down_sems, block)

        seen = until
    for t in range(2):
        pltpu.make_async_copy(held.at[t, step], held.at[t, step], sems.at[t, step]).wait()

    tile_rows = down[pl.ds(pl.multiple_of(step * HIDDEN_TILE, HIDDEN_TILE), HIDDEN_TILE), :]
    count = keep.shape[0]
    for n, sums in enumerate((keep, total)):
        own = slice(n * count, (n + 1) * count)
        gate_value, up_value = gt[own, :], up[own, :]
        dh = matrix_product_backward(sent[own, :width], tile_rows) + matrix_product_backward(
            sent[own, width:], down_lower[...]
        )
        sg = jax.nn.sigmoid(gate_value)
        act = gate_value * sg
        h = low(act * up_value)
        grad_gate = low(dh * up_value * (sg + gate_value * sg * (1.0 - sg)))
        grad_up = low(dh * act)
        hidden[own, :], e_gate[own, :], e_up[own, :] = h, grad_gate, grad_up
        sums[:, :width] += matrix_product_backward(
            grad_gate, held[0, step]
        ) + matrix_product_backward(grad_up, held[1, step])
        lanes = [width + k * ADAPTER_COLUMNS for k in range(4)]
        sums[:, lanes[0] : lanes[1]] += matrix_product_backward(grad_gate, upper_gate[...])
        sums[:, lanes[1] : lanes[2]] += matrix_product_backward(grad_up, upper_up[...])
        sums[:, lanes[2] : lanes[3]] += matrix_product(h, down_lower[...])

    @pl.when(step == tiles - 1)
    def _():
        send[...] = low(total[...])


def feed_forward_out_kernel(line, where, hidden, *refs):
    left, right = refs[:3], refs[3]
    keep, send, down, down_sems = refs[4:]
    rows = left[1].shape[0]
    down_copies(line, where, left, right, down, down_sems)
    for block in range(2 * line):
        wait_rows(down, rows, down_sems, block)
    count = keep.shape[0]
    keep[...] = matrix_product(hidden[:count, :], down[...])
    send[...] = low(matrix_product(hidden[count:, :], down[...]))


def small_cost(flops):
    return pl.CostEstimate(flops=flops // 16, bytes_accessed=flops // 8192, transcendentals=0)


class FeedForward:
    def __init__(self, place, left, right):
        self.place, self.left, self.right = place, left, right
        self.cut = left[1].shape[1]
        self.padded = left[1].shape[0]
        self.kernels = self.padded % 64 == 0
        self.where = jnp.stack([place.z, place.y, place.x]).astype(jnp.int32)

    def down(self):
        right = jnp.where(self.place.y == 0, self.right, self.right[:, ::-1])
        right = right.reshape(-1, right.shape[-1])
        return jnp.concatenate([put_quarter(self.place, *self.left), right], axis=1)

    def hidden(self, values, choices, lower, upper, pieces):
        count, width = values.shape[0], upper.shape[1]
        if not self.kernels:
            reduced = low(matrix_product(values, lower) * choices)
            full = put_quarter(self.place, *pieces)
            return matrix_product(values, full) + adapter_scale * matrix_product(
                reduced, upper
            ), reduced
        tiles = width // HIDDEN_TILE
        once = lambda v: pl.BlockSpec(v.shape, lambda i: (0, 0), pipeline_mode=pl.Buffered(1))
        columns = lambda n: pl.BlockSpec((n, HIDDEN_TILE), lambda i: (0, i))
        return pl.pallas_call(
            functools.partial(hidden_kernel, self.place.line),
            grid=(tiles,),
            out_shape=[
                jax.ShapeDtypeStruct((count, width), jnp.float32),
                jax.ShapeDtypeStruct((count, ADAPTER_COLUMNS), jnp.bfloat16),
            ],
            in_specs=[pl.BlockSpec(memory_space=pltpu.SMEM)]
            + [once(v) for v in (values, choices, lower)]
            + [columns(upper.shape[0])]
            + [pl.BlockSpec(memory_space=pl.ANY)] * 3,
            out_specs=[
                columns(count),
                pl.BlockSpec((count, ADAPTER_COLUMNS), lambda i: (0, 0)),
            ],
            scratch_shapes=[
                pltpu.VMEM((tiles, values.shape[1], HIDDEN_TILE), jnp.bfloat16),
                pltpu.SemaphoreType.DMA((tiles,)),
            ],
            compiler_params=pltpu.CompilerParams(vmem_limit_bytes=40 << 20),
            cost_estimate=small_cost(2 * count * width * values.shape[1]),
        )(self.where, values, choices, lower, upper, *pieces)

    def back(self, gt, up, sent, lower, upper_gate, upper_up, gate_pieces, up_pieces):
        count, width = gt.shape
        half = count // 2
        model = sent.shape[1] - ADAPTER_COLUMNS
        sums = model + 3 * ADAPTER_COLUMNS
        if not self.kernels:
            down = self.down()
            gate, up_part = put_quarter(self.place, *gate_pieces), put_quarter(self.place, *up_pieces)
            sg = jax.nn.sigmoid(gt)
            act = gt * sg
            h = low(act * up)
            dh = matrix_product_backward(sent[:, :model], down) + matrix_product_backward(
                sent[:, model:], lower
            )
            e_gate = low(dh * up * (sg + gt * sg * (1.0 - sg)))
            e_up = low(dh * act)
            total = jnp.concatenate(
                [
                    matrix_product_backward(e_gate, gate) + matrix_product_backward(e_up, up_part),
                    matrix_product_backward(e_gate, upper_gate),
                    matrix_product_backward(e_up, upper_up),
                    matrix_product(h, lower),
                ],
                axis=1,
            )
            return h, e_gate, e_up, total[:half], low(total[half:])
        tiles = width // HIDDEN_TILE
        once = lambda shape: pl.BlockSpec(shape, lambda i: (0, 0), pipeline_mode=pl.Buffered(1))
        columns = lambda n: pl.BlockSpec((n, HIDDEN_TILE), lambda i: (0, i))
        pieces = (*self.left, self.right, *gate_pieces, *up_pieces)
        return pl.pallas_call(
            functools.partial(feed_forward_back_kernel, self.place.line),
            grid=(tiles,),
            out_shape=[jax.ShapeDtypeStruct((count, width), jnp.bfloat16)] * 3
            + [
                jax.ShapeDtypeStruct((half, sums), jnp.float32),
                jax.ShapeDtypeStruct((half, sums), jnp.bfloat16),
            ],
            in_specs=[
                pl.BlockSpec(memory_space=pltpu.SMEM),
                columns(count),
                columns(count),
                once(sent.shape),
                pl.BlockSpec((HIDDEN_TILE, ADAPTER_COLUMNS), lambda i: (i, 0)),
                columns(ADAPTER_COLUMNS),
                columns(ADAPTER_COLUMNS),
            ]
            + [pl.BlockSpec(memory_space=pl.ANY)] * len(pieces),
            out_specs=[columns(count)] * 3 + [once((half, sums))] * 2,
            scratch_shapes=[
                pltpu.VMEM((half, sums), jnp.float32),
                pltpu.VMEM((width, model), jnp.bfloat16),
                pltpu.VMEM((2, tiles, model, HIDDEN_TILE), jnp.bfloat16),
                pltpu.SemaphoreType.DMA((2 * self.place.line,)),
                pltpu.SemaphoreType.DMA((2, tiles)),
            ],
            compiler_params=pltpu.CompilerParams(vmem_limit_bytes=60 << 20),
            cost_estimate=small_cost(6 * count * width * model),
        )(self.where, gt, up, sent, lower, upper_gate, upper_up, *pieces)

    def out(self, h, model):
        count, width = h.shape
        half = count // 2
        if not self.kernels:
            total = matrix_product(h, self.down())
            return total[:half], low(total[half:])
        held = pl.BlockSpec(memory_space=pltpu.VMEM)
        return pl.pallas_call(
            functools.partial(feed_forward_out_kernel, self.place.line),
            out_shape=[
                jax.ShapeDtypeStruct((half, model), jnp.float32),
                jax.ShapeDtypeStruct((half, model), jnp.bfloat16),
            ],
            in_specs=[pl.BlockSpec(memory_space=pltpu.SMEM), held]
            + [pl.BlockSpec(memory_space=pl.ANY)] * 4,
            out_specs=[held] * 2,
            scratch_shapes=[
                pltpu.VMEM((width, model), jnp.bfloat16),
                pltpu.SemaphoreType.DMA((2 * self.place.line,)),
            ],
            compiler_params=pltpu.CompilerParams(vmem_limit_bytes=40 << 20),
            cost_estimate=small_cost(2 * count * width * model),
        )(self.where, h, *self.left, self.right)


def columns_kernel(own, padded, quarter, value, *outs):
    each, window = GROUP * own, 2 * padded
    rows, width = value.shape
    step = pl.program_id(0)
    lane = lax.broadcasted_iota(jnp.int32, (rows, window), 1)
    for out, k in zip(outs, (quarter[0], quarter[0] ^ 2)):
        turned = []
        for n in range(2):
            start = each * (2 * step + n) + own * k
            base = jnp.minimum(start // 128, (width - window) // 128) * 128
            piece = value[:, pl.ds(pl.multiple_of(base, 128), window)].astype(jnp.float32)
            turned.append(pltpu.roll(piece, lax.rem(window + n * padded - (start - base), window), 1))
        kept = jnp.where(lane < own, turned[0], 0.0)
        kept = jnp.where((lane >= padded) & (lane < padded + own), turned[1], kept)
        out[...] = low(kept)


def hidden_columns(place, value, blocks, padded):
    rows, width = value.shape
    own = width // (blocks * GROUP)
    if padded % 64 or 2 * padded > width:

        def take(k):
            def cut(given):
                pieces = []
                for i in range(blocks):
                    start = own * (GROUP * i + k)
                    piece = given[:, start : start + own]
                    pieces.append(jnp.pad(piece, ((0, 0), (0, padded - own))))
                return jnp.concatenate(pieces, axis=1)

            return cut

        branches = [take(k) for k in range(GROUP)]
        return [lax.switch(k, branches, value) for k in (place.q, place.q ^ 2)]
    return pl.pallas_call(
        functools.partial(columns_kernel, own, padded),
        grid=(blocks // 2,),
        out_shape=[jax.ShapeDtypeStruct((rows, blocks * padded), value.dtype)] * 2,
        in_specs=[
            pl.BlockSpec(memory_space=pltpu.SMEM),
            pl.BlockSpec((rows, width), lambda i: (0, 0)),
        ],
        out_specs=[pl.BlockSpec((rows, 2 * padded), lambda i: (0, i))] * 2,
        compiler_params=pltpu.CompilerParams(vmem_limit_bytes=32 << 20),
        cost_estimate=pl.CostEstimate(
            flops=8 * rows * width, bytes_accessed=4 * rows * width, transcendentals=0
        ),
    )(place.q.astype(jnp.int32).reshape(1), value)


def hidden_rows(place, value, quarter, blocks, padded):
    own = value.shape[0] // (blocks * GROUP)
    split = value.reshape(blocks, GROUP, own, -1)
    got = lax.dynamic_index_in_dim(split, quarter, 1, keepdims=False)
    return jnp.pad(got, ((0, 0), (0, padded - own), (0, 0))).reshape(blocks * padded, -1)


def spread_kernel(own, padded, quarter, value, out, total):
    rows, width = total.shape
    window = 2 * padded
    total[...] = jnp.zeros_like(total)
    lane = lax.broadcasted_iota(jnp.int32, (rows, window), 1)
    for i in range(width // (GROUP * own)):
        pair, n = i // 2, i % 2
        start = own * (GROUP * i + quarter[0])
        base = jnp.minimum(start // 128, (width - window) // 128) * 128
        piece = value[:, pair * window : (pair + 1) * window].astype(jnp.float32)
        inside = (lane >= n * padded) & (lane < n * padded + own)
        turned = pltpu.roll(
            jnp.where(inside, piece, 0.0),
            lax.rem(window - n * padded + (start - base), window),
            1,
        )
        total[:, pl.ds(pl.multiple_of(base, 128), window)] += turned
    out[...] = low(total[...])


def spread_columns(place, value, width, blocks, padded):
    rows = value.shape[0]
    own = width // (blocks * GROUP)
    if padded % 64 or 2 * padded > width:

        def lay(k):
            def build(given):
                pieces = []
                for i in range(blocks):
                    piece = given[:, padded * i : padded * i + own]
                    pieces.append(jnp.pad(piece, ((0, 0), (own * k, own * (GROUP - 1 - k)))))
                return jnp.concatenate(pieces, axis=1)

            return build

        return lax.switch(place.q, [lay(k) for k in range(GROUP)], value)
    return pl.pallas_call(
        functools.partial(spread_kernel, own, padded),
        out_shape=jax.ShapeDtypeStruct((rows, width), jnp.bfloat16),
        in_specs=[
            pl.BlockSpec(memory_space=pltpu.SMEM),
            pl.BlockSpec(memory_space=pltpu.VMEM),
        ],
        out_specs=pl.BlockSpec(memory_space=pltpu.VMEM),
        scratch_shapes=[pltpu.VMEM((rows, width), jnp.float32)],
        compiler_params=pltpu.CompilerParams(vmem_limit_bytes=32 << 20),
        cost_estimate=pl.CostEstimate(
            flops=8 * rows * width, bytes_accessed=4 * rows * width, transcendentals=0
        ),
    )(place.q.astype(jnp.int32).reshape(1), value)


def both(kept, got):
    return low(kept.astype(jnp.float32) + got.astype(jnp.float32))


def pick(values, index, axis):
    return lax.dynamic_index_in_dim(values, index, axis, keepdims=False)


def reduce_over_cores(place, flat):
    pairs = place.line * 2 * (place.shard // 2)
    rows = flat.shape[0] // pairs
    half = -(-rows // 16) * 8
    split = flat.reshape(place.line, 2, place.shard // 2, rows, ADAPTER_COLUMNS)
    start = rows - half
    keep = lax.dynamic_slice_in_dim(split, place.c * start, half, 3)
    send = lax.dynamic_slice_in_dim(split, (1 - place.c) * start, half, 3)
    return both(keep, place.by_c(send))


class OwnerSum:
    def __init__(self, place, total, share):
        self.place, self.share, self.half = place, share, total.shape[3]
        cut = self.half // 16 * 8
        one, two = total[:, :, :, :cut], total[:, :, :, cut:]
        self.kept = (pick(one, place.y, 1), pick(two, place.x, 2))
        self.got = (
            place.by_y(pick(one, 1 - place.y, 1)),
            place.by_x(pick(two, 1 - place.x, 2)),
        )

    def over_chips(self):
        place = self.place
        one, two = both(self.kept[0], self.got[0]), both(self.kept[1], self.got[1])
        got_one = place.by_x(pick(one, 1 - place.x, 1))
        got_two = place.by_y(pick(two, 1 - place.y, 1))
        one, two = both(pick(one, place.x, 1), got_one), both(pick(two, place.y, 1), got_two)
        return jnp.concatenate([one, two], axis=1)

    def over_planes(self, total):
        place = self.place
        got = [
            place.ring_z(pick(total, (place.z + k) % place.line, 0), k)
            for k in range(1, place.line)
        ]
        result = pick(total, place.z, 0).astype(jnp.float32)
        for value in got:
            result = result + value.astype(jnp.float32)
        start = place.c * (self.half - self.share)
        return lax.dynamic_slice_in_dim(result, start, self.share, 0)


def gather_owners(place, own, event):
    share = own.shape[0]
    half = -(-share // 8) * 8
    start = 2 * share - half
    mate = place.by_c(own)
    head, tail = jnp.where(place.c == 0, own, mate), jnp.where(place.c == 0, mate, own)
    pair = jnp.concatenate([head, tail], axis=0)
    planes = place.all_z(lax.dynamic_slice_in_dim(pair, place.c * start, half, 0))
    planes, event = together(planes, event)
    cut = half // 16 * 8
    full = jnp.zeros(
        (place.line, 2, place.shard // 2, 2 * share, ADAPTER_COLUMNS), own.dtype
    )
    for part, x_first, at in ((planes[:, :cut], True, 0), (planes[:, cut:], False, cut)):
        x_part, y_part = place.by_x(part), place.by_y(part)
        xy_part = place.by_y(x_part) if x_first else place.by_x(y_part)
        for value, y, x in (
            (part, place.y, place.x),
            (x_part, place.y, 1 - place.x),
            (y_part, 1 - place.y, place.x),
            (xy_part, 1 - place.y, 1 - place.x),
        ):
            for held, c in ((value, place.c), (place.by_c(value), 1 - place.c)):
                where = (0, y, x, c * start + at, 0)
                full = lax.dynamic_update_slice(full, held[:, None, None], where)
    return full.reshape(-1), event


def shards(
    dp,
    shard,
    tokens,
    cotangent,
    arrival,
    lengths,
    adapter_set,
    gain_one,
    gain_two,
    w_query,
    w_key,
    w_value,
    w_out,
    w_gate,
    w_up,
    w_down,
    adapters,
    first_moment_running,
    second_moment_running,
):
    place = Place(dp, shard)
    token_order = arrival[0]
    count = token_order.shape[0]
    padded = -(-(FEEDFORWARD_UNITS // (dp * GROUP)) // 16) * 16


    weights = (w_query, w_key, w_value, w_out)
    s, half = place.x * 2 + place.c, MODEL_WIDTH // 2
    cut = MODEL_WIDTH - MODEL_WIDTH * 2 // 9
    stacked = jnp.stack(weights)
    mine = lax.dynamic_index_in_dim(stacked, s, 0, keepdims=False)
    first = place.all_z(mine[:, :half])
    second = place.all_z(mine[:, half:])
    near_y = place.by_y(mine)
    table = jnp.concatenate([lengths, adapter_set], axis=1)
    table_y = place.by_y(table)
    own_gate, other_gate = hidden_columns(place, w_gate, dp, padded)
    own_up, other_up = hidden_columns(place, w_up, dp, padded)
    near_y, table_y, other_gate, other_up = together(near_y, table_y, other_gate, other_up)

    near_x = place.by_x(near_y)
    got_gate, got_up = place.by_y(other_gate), place.by_y(other_up)
    near_y_c = place.by_c(near_y)
    tables = jnp.concatenate([table, table_y], axis=0)
    tables_c = place.by_c(tables)
    own_down = hidden_rows(place, w_down, place.q, 1, padded)
    other_down = hidden_rows(place, w_down, place.q ^ 2, 1, padded)
    first, got_gate, got_up, near_x, near_y_c, tables_c, tokens = together(
        first, got_gate, got_up, near_x, near_y_c, tables_c, tokens
    )

    straight = place.y == place.x
    gate_planes = place.all_z(jnp.where(straight, own_gate, got_gate))
    up_planes = place.all_z(jnp.where(straight, own_up, got_up))
    gate_rest, up_rest = (
        jnp.where(straight, got_gate, own_gate),
        jnp.where(straight, got_up, own_up),
    )
    tables = jnp.concatenate([tables, tables_c], axis=0)
    lines = place.other_z(first)
    x0, y0, lines_c = place.by_x(lines), place.by_y(lines), place.by_c(lines)
    near_x_c = place.by_c(near_x)
    arrived_x = lax.all_to_all(tokens, "dp", split_axis=0, concat_axis=0, tiled=True)
    x0, y0, lines_c, near_x_c, second = together(x0, y0, lines_c, near_x_c, second)

    lines2 = place.other_z(second)
    x1, y1, lines2_c = place.by_x(lines2), place.by_y(lines2), place.by_c(lines2)
    x0_c, y0_c = place.by_c(x0), place.by_c(y0)
    x1, y1, lines2_c, x0_c, y0_c, x0, arrived_x = together(
        x1, y1, lines2_c, x0_c, y0_c, x0, arrived_x
    )

    A_model, A_hidden, B_model, B_hidden = restore_structure(adapters)
    B_gate, _ = hidden_columns(place, B_hidden[0], dp, padded)
    B_up, _ = hidden_columns(place, B_hidden[1], dp, padded)
    A_down = hidden_rows(place, A_hidden, place.q, dp, padded)
    choice, allowed, cosine_table, sine_table = block_tables(lengths[0], adapter_set[0])
    choices = jnp.concatenate(
        [block_tables(tables[k, :SEQ_DEV], tables[k, SEQ_DEV:])[0] for k in range(GROUP)], axis=0
    )
    xy0, xy1 = place.by_y(x0), place.by_x(y1)
    x1_c, y1_c = place.by_c(x1), place.by_c(y1)
    xy0, xy1, x1_c, y1_c, B_gate, B_up, A_down, choices, gate_planes, other_down, cotangent = together(
        xy0, xy1, x1_c, y1_c, B_gate, B_up, A_down, choices, gate_planes, other_down, cotangent
    )

    got_down = place.by_y(other_down)
    arrived_cot = lax.all_to_all(cotangent, "dp", split_axis=0, concat_axis=0, tiled=True)
    gate_mates = place.by_x(place.other_z(gate_planes))
    attention = AttentionWeights(
        place,
        weights,
        ((lines, lines_c, x0, x0_c), (lines2, lines2_c, x1, x1_c)),
        ((y0, y0_c, xy0, place.by_c(xy0)), (y1, y1_c, xy1, place.by_c(xy1))),
        (near_y, near_y_c, near_x, near_x_c),
    )
    gain_first = gain_one.astype(jnp.float32)
    gain_second = gain_two.astype(jnp.float32)

    x = arrived_x[token_order].astype(jnp.float32)
    scale_one = rms_scale(x)
    n1 = low(x * scale_one * gain_first)

    z_qkv = low(
        jnp.einsum("nd,tdr->tnr", n1, A_model[:3], preferred_element_type=jnp.float32) * choice
    )
    bias = jnp.where(allowed, 0.0, -jnp.inf)
    lin, got_down = together(attention.times(n1, 0, 3), got_down)
    left_planes = place.all_z(jnp.where(straight, own_down, got_down)[:, :cut])
    left_rest = jnp.where(straight, got_down, own_down)[:, :cut]
    right_planes = place.all_z(jnp.stack([own_down[:, cut:], got_down[:, cut:]]))
    qkv, o = attention_call(
        attention_kernel,
        (
            (lin, 2),
            (z_qkv, None),
            (B_model[:3], 2),
            (cosine_table, None),
            (sine_table, None),
            (bias, None),
        ),
        (((3, count, MODEL_WIDTH), 2), ((count, MODEL_WIDTH), 1)),
    )
    o, up_planes, gate_mates = together(o, up_planes, gate_mates)
    up_mates = place.by_x(place.other_z(up_planes))
    z_out, delta_out = apply_adapter_delta(o, A_model[3], B_model[3], choice)
    m = x + residual_branch_scale * (attention.times(o, 3, 1)[0] + delta_out)
    scale_two = rms_scale(m)
    n2 = low(m * scale_two * gain_second)

    n2_y = place.by_y(n2)
    n2_y, arrived_cot, left_planes, up_mates = together(
        n2_y, arrived_cot, left_planes, up_mates
    )
    left_mates = place.by_x(place.other_z(left_planes))
    g = arrived_cot[token_order].astype(jnp.float32)
    e_down = low(residual_branch_scale * g)
    dz_down = low(adapter_scale * matrix_product_backward(e_down, B_model[4]) * choice)
    sent = jnp.concatenate([e_down, dz_down], axis=1)
    sent_y = place.by_y(sent)
    n2_all = jnp.concatenate([n2, n2_y], axis=0)
    n2_all = jnp.concatenate([n2_all, place.by_c(n2_all)], axis=0)
    gate_pieces = (gate_planes, gate_rest, gate_mates)
    forward = FeedForward(place, (left_planes, left_rest, left_mates), right_planes)
    gt, z_gate = forward.hidden(n2_all, choices, A_model[4], B_gate, gate_pieces)
    up_pieces = (up_planes, up_rest, up_mates)
    up, z_up = forward.hidden(n2_all, choices, A_model[5], B_up, up_pieces)
    gt, up, left_mates, right_planes, sent_y = together(gt, up, left_mates, right_planes, sent_y)
    sent = jnp.concatenate([sent, sent_y], axis=0)
    sent = jnp.concatenate([sent, place.by_c(sent)], axis=0)
    dz_down_all = sent[:, MODEL_WIDTH:]
    feed = FeedForward(place, (left_planes, left_rest, left_mates), right_planes)
    h, e_gate, e_up, keep, send = feed.back(
        gt, up, sent, A_down, B_gate, B_up, gate_pieces, up_pieces
    )
    own_sum, other_sum = place.half_sum(keep, send)
    other_sum, h = together(low(other_sum), h)
    got = place.by_y(other_sum)
    y_keep, y_send = feed.out(h, MODEL_WIDTH)
    got, y_send = together(got, y_send)
    back_sum = own_sum + got.astype(jnp.float32)
    y_own, y_other = place.half_sum(y_keep, y_send)
    y_got = place.by_y(low(y_other))
    cuts = [MODEL_WIDTH + k * ADAPTER_COLUMNS for k in range(3)]
    dz_gate, dz_up, z_down = jnp.split(back_sum, cuts, axis=1)[1:]
    dz_gate, dz_up = low(adapter_scale * dz_gate * choice), low(adapter_scale * dz_up * choice)
    z_down = low(z_down * choice)
    dn2 = (
        back_sum[:, :MODEL_WIDTH]
        + matrix_product_backward(dz_gate, A_model[4])
        + matrix_product_backward(dz_up, A_model[5])
    )
    dA_gate, dA_up = outer_product_sum(n2, dz_gate), outer_product_sum(n2, dz_up)
    dB_gate = adapter_scale * outer_product_sum(z_gate, e_gate)
    dB_up = adapter_scale * outer_product_sum(z_up, e_up)
    dA_down = outer_product_sum(h, dz_down_all)
    dB_down = adapter_scale * outer_product_sum(z_down, e_down)

    dm = g + norm_back(m, scale_two, gain_second, dn2)
    e_out = low(residual_branch_scale * dm)
    dz_out = low(adapter_scale * matrix_product_backward(e_out, B_model[3]) * choice)
    (e_qkv,) = attention_call(
        attention_back_kernel,
        (
            (qkv, 2),
            (attention.times_transposed(e_out[None], 3, 1), 1),
            (dz_out, None),
            (A_model[3], 0),
            (cosine_table, None),
            (sine_table, None),
            (bias, None),
        ),
        (((3, count, MODEL_WIDTH), 2),),
    )
    dA_out, dB_out = outer_product_sum(o, dz_out), adapter_scale * outer_product_sum(z_out, e_out)
    e_qkv, y_got = together(e_qkv, y_got)
    y = m + residual_branch_scale * (
        y_own + y_got.astype(jnp.float32) + adapter_scale * matrix_product(z_down, B_model[4])
    )
    inverse = (
        jnp.zeros_like(token_order).at[token_order].set(jnp.arange(count, dtype=jnp.int32))
    )
    dz_qkv = low(
        adapter_scale
        * jnp.einsum("tnd,trd->tnr", e_qkv, B_model[:3], preferred_element_type=jnp.float32)
        * choice
    )
    dA_qkv = jnp.einsum("nd,tnr->tdr", n1, dz_qkv, preferred_element_type=jnp.float32)
    dB_qkv = adapter_scale * jnp.einsum(
        "tnr,tnd->trd", z_qkv, e_qkv, preferred_element_type=jnp.float32
    )
    own_hidden = FEEDFORWARD_UNITS // (dp * GROUP)
    dA_hidden = lax.dynamic_update_slice(
        jnp.zeros((dp, GROUP, own_hidden, ADAPTER_COLUMNS), jnp.bfloat16),
        low(dA_down).reshape(dp, 1, padded, ADAPTER_COLUMNS)[:, :, :own_hidden],
        (0, place.q, 0, 0),
    )
    flat = jnp.concatenate(
        [
            low(piece).reshape(-1, ADAPTER_COLUMNS)
            for piece in (
                dA_qkv,
                dA_out,
                dA_gate,
                dA_up,
                dA_hidden,
                dB_qkv,
                dB_out,
                dB_down,
                spread_columns(place, low(dB_gate), FEEDFORWARD_UNITS, dp, padded),
                spread_columns(place, low(dB_up), FEEDFORWARD_UNITS, dp, padded),
            )
        ]
    )
    share = flat.shape[0] // (dp * shard)
    total, e_qkv, dz_qkv, y = together(reduce_over_cores(place, flat), e_qkv, dz_qkv, y)
    owner = OwnerSum(place, total, share)
    back_out = lax.all_to_all(low(y)[inverse], "dp", split_axis=0, concat_axis=0, tiled=True)
    dn1 = attention.times_transposed(e_qkv, 0, 3) + jnp.einsum(
        "tnr,tdr->nd", dz_qkv, A_model[:3], preferred_element_type=jnp.float32
    )
    dx = dm + norm_back(x, scale_one, gain_first, dn1)
    owner.got, back_out = together(owner.got, back_out)
    gradient = owner.over_planes(owner.over_chips())
    offset = lax.axis_index(AXES) * share
    own_params = lax.dynamic_slice_in_dim(
        adapters.reshape(-1, ADAPTER_COLUMNS), offset, share
    ).astype(jnp.float32)
    first = first_moment_running.reshape(share, ADAPTER_COLUMNS)
    second = second_moment_running.reshape(share, ADAPTER_COLUMNS)
    fresh_first = first_decay_rate * first + (1.0 - first_decay_rate) * gradient
    fresh_second = second_decay_rate * second + (1.0 - second_decay_rate) * gradient * gradient
    unbiased_first = fresh_first / (1.0 - first_decay_rate**OPT_STEP)
    unbiased_second = fresh_second / (1.0 - second_decay_rate**OPT_STEP)
    update = (
        unbiased_first / (jnp.sqrt(unbiased_second) + adaptive_epsilon)
        + weight_shrink_rate * own_params
    )
    updated, dx = gather_owners(place, low(own_params - learning_rate * update), dx)
    back_grad = lax.all_to_all(low(dx)[inverse], "dp", split_axis=0, concat_axis=0, tiled=True)

    return (
        back_out,
        back_grad,
        gradient.reshape(-1),
        fresh_first.reshape(-1),
        fresh_second.reshape(-1),
        updated,
    )


def solution(mesh):
    rows = P(AXES, None)
    weight = P("dp", None)
    return jax.shard_map(
        functools.partial(shards, mesh.shape["dp"], mesh.shape["shard"]),
        mesh=mesh,
        in_specs=(rows,) * 5 + (P(), P()) + (weight,) * 7 + (P(), P(AXES), P(AXES)),
        out_specs=(rows, rows, P(AXES), P(AXES), P(AXES), P()),
        check_vma=False,
    )
```

```python
import functools
import math

import jax
import jax.numpy as jnp
from jax import lax
from jax.experimental import pallas as pl
from jax.experimental.pallas import tpu as pltpu
from jax.sharding import PartitionSpec as P

MODEL_WIDTH = 2304
ATTENTION_HEADS = 36
HEAD_SIZE = 64
FEEDFORWARD_UNITS = 5760
ADAPTER_RANK = 16
OPT_STEP = 10
SEQ_DEV = 4
TOK_DEV = 256
ADAPTER_COLUMNS = 128


norm_eps = 1e-05
residual_branch_scale = 1.4 / math.sqrt(40.0)
adapter_scale = 2.0
rope_base = 10000.0
first_decay_rate = 0.9
second_decay_rate = 0.999
adaptive_epsilon = 1e-08
weight_shrink_rate = 0.01
learning_rate = 0.01


def matrix_product(left_side, right_side):
    return jnp.dot(left_side, right_side, preferred_element_type=jnp.float32)


def matrix_product_backward(left_side, right_side):
    return lax.dot_general(
        left_side, right_side, (((1,), (1,)), ((), ())), preferred_element_type=jnp.float32
    )


def outer_product_sum(left_side, right_side):
    return lax.dot_general(
        left_side, right_side, (((0,), (0,)), ((), ())), preferred_element_type=jnp.float32
    )


def low(values):
    return values.astype(jnp.bfloat16)


def block_tables(sequence_lengths, sequence_adapter_index):
    row_ids = jnp.arange(TOK_DEV, dtype=jnp.int32)
    seq_ends = jnp.cumsum(sequence_lengths, dtype=jnp.int32)
    seq_starts = seq_ends - sequence_lengths
    segment = jnp.sum(
        (row_ids[:, None] >= seq_ends[None, :]).astype(jnp.int32), axis=1, dtype=jnp.int32
    )
    member = (segment[:, None] == jnp.arange(SEQ_DEV, dtype=jnp.int32)[None, :]).astype(jnp.int32)
    position = row_ids - jnp.sum(member * seq_starts[None, :], axis=1, dtype=jnp.int32)
    token_adapter_index = jnp.sum(member * sequence_adapter_index[None, :], axis=1, dtype=jnp.int32)
    adapter_choice_index = (
        jnp.arange(ADAPTER_COLUMNS, dtype=jnp.int32)[None, :] // ADAPTER_RANK
        == token_adapter_index[:, None]
    ).astype(jnp.float32)
    allowed = (segment[:, None] == segment[None, :]) & (row_ids[None, :] <= row_ids[:, None])
    half_dim = HEAD_SIZE // 2
    inv_freq = jnp.power(rope_base, -2.0 * jnp.arange(half_dim, dtype=jnp.float32) / HEAD_SIZE)
    angles = position.astype(jnp.float32)[:, None] * inv_freq[None, :]
    cosine, sine = jnp.cos(angles), jnp.sin(angles)
    return (
        adapter_choice_index,
        allowed,
        jnp.concatenate([cosine] * 4, axis=1),
        jnp.concatenate([-sine, sine] * 2, axis=1),
    )


def restore_structure(flattened_vector):
    first_boundary = 6 * MODEL_WIDTH * ADAPTER_COLUMNS
    second_boundary = first_boundary + FEEDFORWARD_UNITS * ADAPTER_COLUMNS
    third_boundary = second_boundary + 5 * ADAPTER_COLUMNS * MODEL_WIDTH
    return (
        flattened_vector[:first_boundary].reshape(6, MODEL_WIDTH, ADAPTER_COLUMNS),
        flattened_vector[first_boundary:second_boundary].reshape(
            FEEDFORWARD_UNITS, ADAPTER_COLUMNS
        ),
        flattened_vector[second_boundary:third_boundary].reshape(5, ADAPTER_COLUMNS, MODEL_WIDTH),
        flattened_vector[third_boundary:].reshape(2, ADAPTER_COLUMNS, FEEDFORWARD_UNITS),
    )


def rms_scale(values):
    return lax.rsqrt(jnp.mean(values * values, axis=-1, keepdims=True) + norm_eps)


def norm_back(values, scale, gain, gradient_value):
    weighted = gradient_value * gain
    return scale * weighted - values * scale**3 * jnp.mean(
        values * weighted, axis=-1, keepdims=True
    )


def apply_adapter_delta(input_rows, adapter_down_pair, adapter_up_pair, adapter_choice_index):
    reduced_total = low(
        matrix_product(input_rows, adapter_down_pair) * adapter_choice_index
    )
    return (reduced_total, adapter_scale * matrix_product(reduced_total, adapter_up_pair))


def swap_halves(values):
    lane = lax.broadcasted_iota(jnp.int32, values.shape, 1)
    half, width = HEAD_SIZE // 2, values.shape[1]
    return jnp.where(
        lane % HEAD_SIZE < half, pltpu.roll(values, width - half, 1), pltpu.roll(values, half, 1)
    )


def head_scores(query, key, bias):
    scores = matrix_product_backward(query, key) * HEAD_SIZE ** (-0.5) + bias
    expanded = jnp.exp(scores - jnp.max(scores, axis=-1, keepdims=True))
    return expanded / jnp.sum(expanded, axis=-1, keepdims=True)


def attention_kernel(lin, z, up, cosine, sine, bias, qkv, attended):
    full = [lin[t] + adapter_scale * matrix_product(z[t], up[t]) for t in range(3)]
    query, key = (
        low(v * cosine[...] + swap_halves(v) * sine[...]) for v in full[:2]
    )
    value = low(full[2])
    qkv[0], qkv[1], qkv[2] = query, key, value
    first = lax.broadcasted_iota(jnp.int32, query.shape, 1) < HEAD_SIZE
    results = []
    for mine in (first, ~first):
        probs = head_scores(jnp.where(mine, query, jnp.zeros_like(query)), key, bias[...])
        results.append(matrix_product(low(probs), value))
    attended[...] = low(jnp.where(first, results[0], results[1]))


def attention_back_kernel(qkv, lin, dz, down, cosine, sine, bias, grads):
    query, key, value = qkv[0], qkv[1], qkv[2]
    grad = low(lin[...] + matrix_product_backward(dz[...], down[...]))
    first = lax.broadcasted_iota(jnp.int32, query.shape, 1) < HEAD_SIZE
    nothing = jnp.zeros_like(query)
    results = []
    for mine in (first, ~first):
        probs = head_scores(jnp.where(mine, query, nothing), key, bias[...])
        grad_probs = matrix_product_backward(jnp.where(mine, grad, nothing), value)
        row_delta = jnp.sum(probs * grad_probs, axis=-1, keepdims=True)
        grad_scores = low(probs * (grad_probs - row_delta))
        results.append(
            (
                matrix_product(grad_scores, key),
                outer_product_sum(grad_scores, query),
                outer_product_sum(low(probs), grad),
            )
        )
    scale = HEAD_SIZE ** (-0.5)
    grad_query, grad_key, grad_value = (
        jnp.where(first, one, two) for one, two in zip(*results)
    )
    for t, v in enumerate((grad_query * scale, grad_key * scale)):
        grads[t] = low(v * cosine[...] - swap_halves(v) * sine[...])
    grads[2] = low(grad_value)


def attention_call(kernel, operands, outs):
    pairs = 2 * HEAD_SIZE

    def spec(shape, axis):
        block = tuple(pairs if k == axis else n for k, n in enumerate(shape))
        return pl.BlockSpec(block, lambda i: tuple(i if k == axis else 0 for k in range(len(shape))))

    count = operands[-1][0].shape[0]
    return pl.pallas_call(
        kernel,
        grid=(ATTENTION_HEADS // 2,),
        out_shape=[jax.ShapeDtypeStruct(shape, jnp.bfloat16) for shape, _ in outs],
        in_specs=[spec(v.shape, axis) for v, axis in operands],
        out_specs=[spec(shape, axis) for shape, axis in outs],
        compiler_params=pltpu.CompilerParams(vmem_limit_bytes=48 << 20),
        cost_estimate=pl.CostEstimate(
            flops=8 * count * count * MODEL_WIDTH // 16,
            bytes_accessed=24 * count * MODEL_WIDTH // 16,
            transcendentals=0,
        ),
    )(*[v for v, _ in operands])


GROUP = 4
AXES = ("dp", "shard")


def together(*values):
    return lax.optimization_barrier(values)


class Place:
    def __init__(self, dp, shard):
        self.line, self.shard = dp // 2, shard
        i, s = lax.axis_index("dp"), lax.axis_index("shard")
        self.z, self.y, self.x, self.c = i // 2, i % 2, s // 2, s % 2
        self.q = self.y * 2 + self.c
        self.spots = [
            (z, y, x, c)
            for z in range(self.line)
            for y in range(2)
            for x in range(shard // 2)
            for c in range(2)
        ]

    def number(self, z, y, x, c):
        return (z * 2 + y) * self.shard + x * 2 + c

    def move(self, value, target):
        pairs = []
        for spot in self.spots:
            to = target(*spot)
            if to is not None:
                pairs.append((self.number(*spot), self.number(*to)))
        return lax.ppermute(value, AXES, pairs)

    def by_y(self, value):
        return self.move(value, lambda z, y, x, c: (z, 1 - y, x, c))

    def by_x(self, value):
        return self.move(value, lambda z, y, x, c: (z, y, 1 - x, c))

    def by_c(self, value):
        return self.move(value, lambda z, y, x, c: (z, y, x, 1 - c))

    def ring_z(self, value, step):
        return self.move(value, lambda z, y, x, c: ((z + step) % self.line, y, x, c))

    def all_z(self, block):
        groups = [[z * 2 + y for z in range(self.line)] for y in range(2)]
        return lax.all_gather(block, "dp", axis=0, axis_index_groups=groups)

    def other_z(self, blocks):
        return jnp.stack(
            [
                lax.dynamic_index_in_dim(blocks, (self.z + k) % self.line, 0, keepdims=False)
                for k in range(1, self.line)
            ]
        )

    def gather_group(self, rows):
        pair = jnp.concatenate([rows, self.by_y(rows)], axis=0)
        return jnp.concatenate([pair, self.by_c(pair)], axis=0)

    def half_sum(self, keep, send):
        return (keep + self.by_c(send).astype(jnp.float32)).reshape(2, -1, keep.shape[1])


def put(buffer, block, *where):
    block = block.reshape((1,) * len(where) + block.shape)
    return lax.dynamic_update_slice(
        buffer, block, tuple(where) + (0,) * (buffer.ndim - len(where))
    )


def put_quarter(place, planes, rest, mates):
    full = jnp.zeros((place.line, 2) + rest.shape, rest.dtype)
    full = lax.dynamic_update_slice(full, planes[:, None], (0, place.x) + (0,) * rest.ndim)
    full = put(full, rest, place.z, 1 - place.x)
    for k in range(1, place.line):
        full = put(full, mates[k - 1], (place.z + k) % place.line, 1 - place.x)
    return full.reshape((-1,) + rest.shape[1:])


class AttentionWeights:
    def __init__(self, place, weights, same, across, near):
        self.place, self.native = place, weights
        self.same, self.across, self.near = same, across, near
        self.s = place.x * 2 + place.c
        self.rows, self.half = weights[0].shape[0], weights[0].shape[1] // 2

    def full(self, t):
        place = self.place
        halves = []
        for h in range(2):
            cols = slice(h * self.half, (h + 1) * self.half)
            buffer = jnp.zeros((place.line, 2, self.rows, self.half), self.native[t].dtype)
            buffer = put(buffer, self.native[t][:, cols], place.z, place.y)
            for r in range(4):
                near = self.near[r][:, cols]
                with_r = put(buffer, near, place.z, 1 - place.y)
                for k in range(1, place.line):
                    plane = (place.z + k) % place.line
                    with_r = put(with_r, self.same[h][r][k - 1], plane, place.y)
                    with_r = put(with_r, self.across[h][r][k - 1], plane, 1 - place.y)
                buffer = jnp.where(self.s ^ r == t, with_r, buffer)
            halves.append(buffer.reshape(-1, self.half))
        return jnp.concatenate(halves, axis=1)

    def times(self, values, first, count):
        if self.rows % 16:
            return jnp.stack([matrix_product(values, self.full(first + j)) for j in range(count)])
        return self.call(values, first, count, False)

    def times_transposed(self, values, first, count):
        if self.rows % 16:
            return sum(
                matrix_product_backward(values[j], self.full(first + j)) for j in range(count)
            )
        return self.call(values, first, count, True)

    def call(self, values, first, count, back):
        place, rows, half = self.place, self.rows, self.half
        where = jnp.stack([place.z, place.y, self.s]).astype(jnp.int32)
        width, depth = 2 * half, rows * 2 * place.line
        tokens = values.shape[-2]
        shape = (tokens, depth) if back else (count, tokens, width)
        held = pl.BlockSpec(memory_space=pltpu.VMEM)
        given = pl.BlockSpec(memory_space=pl.ANY)
        pieces = (
            list(self.native[first : first + count])
            + [v for h in range(2) for v in self.same[h]]
            + [v for h in range(2) for v in self.across[h]]
            + list(self.near)
        )
        return pl.pallas_call(
            functools.partial(weights_kernel, place.line, first, count, back),
            out_shape=jax.ShapeDtypeStruct(shape, jnp.float32),
            in_specs=[pl.BlockSpec(memory_space=pltpu.SMEM), held] + [given] * len(pieces),
            out_specs=held,
            scratch_shapes=[
                pltpu.VMEM((2, count, depth, half), jnp.bfloat16),
                pltpu.SemaphoreType.DMA((2, count)),
            ],
            compiler_params=pltpu.CompilerParams(vmem_limit_bytes=56 << 20),
            cost_estimate=pl.CostEstimate(
                flops=2 * tokens * depth * width * count // 16,
                bytes_accessed=2 * depth * width * count // 16,
                transcendentals=0,
            ),
        )(where, values, *pieces)


def weights_kernel(line, first, count, back, where, values, *refs):
    native = refs[:count]
    same = (refs[count : count + 4], refs[count + 4 : count + 8])
    across = (refs[count + 8 : count + 12], refs[count + 12 : count + 16])
    near = refs[count + 16 : count + 20]
    out, held, sems = refs[count + 20 :]
    z, y, s = where[0], where[1], where[2]
    rows, width = native[0].shape
    half = width // 2

    def place(h, j, plane, side):
        start = pl.multiple_of(rows * (2 * plane + side), 16)
        return held.at[h, j, pl.ds(start, rows)]

    for h in range(2):
        cols = pl.ds(h * half, half)
        for j in range(count):
            pltpu.make_async_copy(
                native[j].at[:, cols], place(h, j, z, y), sems.at[h, j]
            ).start()
        for r in range(4):
            j = (s ^ r) - first

            @pl.when((j >= 0) & (j < count))
            def _():
                pltpu.make_async_copy(
                    near[r].at[:, cols], place(h, j, z, 1 - y), sems.at[h, j]
                ).start()
                for k in range(1, line):
                    plane = lax.rem(z + k, line)
                    pltpu.make_async_copy(
                        same[h][r].at[k - 1], place(h, j, plane, y), sems.at[h, j]
                    ).start()
                    pltpu.make_async_copy(
                        across[h][r].at[k - 1], place(h, j, plane, 1 - y), sems.at[h, j]
                    ).start()

    if back:
        out[...] = jnp.zeros_like(out)

    def step(i, carry):
        h, j = i // count, lax.rem(i, count)
        cols = pl.ds(pl.multiple_of(h * half, 128), half)
        pltpu.make_async_copy(held.at[h, j], held.at[h, j], sems.at[h, j]).wait()
        if back:
            out[...] += matrix_product_backward(values[j, :, cols], held[h, j])
        else:
            out[j, :, cols] = matrix_product(values[...], held[h, j])
        return carry

    lax.fori_loop(0, 2 * count, step, 0)


HIDDEN_TILE = 256


def quarter_copies(line, z, x, pieces, target, sem):
    planes, rest, mates = pieces
    rows = rest.shape[0]

    def copy(source, plane, side):
        start = pl.multiple_of(rows * (2 * plane + side), 16)
        pltpu.make_async_copy(source, target.at[pl.ds(start, rows)], sem).start()

    for plane in range(line):
        copy(planes.at[plane], plane, x)
    copy(rest, z, 1 - x)
    for k in range(1, line):
        copy(mates.at[k - 1], lax.rem(z + k, line), 1 - x)


def hidden_kernel(line, where, values, choices, down, up, planes, rest, mates, out, reduced, held, sems):
    step = pl.program_id(0)
    tiles = held.shape[0]

    @pl.when(step == 0)
    def _():
        def start(tile, carry):
            cols = pl.ds(pl.multiple_of(tile * HIDDEN_TILE, 128), HIDDEN_TILE)
            pieces = (planes.at[:, :, cols], rest.at[:, cols], mates.at[:, :, cols])
            quarter_copies(line, where[0], where[2], pieces, held.at[tile], sems.at[tile])
            return carry

        lax.fori_loop(0, tiles, start, 0)
        reduced[...] = low(matrix_product(values[...], down[...]) * choices[...])

    pltpu.make_async_copy(held.at[step], held.at[step], sems.at[step]).wait()
    out[...] = matrix_product(values[...], held[step]) + adapter_scale * matrix_product(
        reduced[...], up[...]
    )


def down_copies(line, where, left, right, target, sems):
    planes, rest, mates = left
    z, y, x = where[0], where[1], where[2]
    rows, cut = rest.shape

    def copy(source, plane, side, cols):
        block = 2 * plane + side
        start = pl.multiple_of(rows * block, 16)
        pltpu.make_async_copy(source, target.at[pl.ds(start, rows), cols], sems.at[block]).start()

    first, second = pl.ds(0, cut), pl.ds(cut, target.shape[1] - cut)
    for plane in range(line):
        copy(planes.at[plane], plane, x, first)
        copy(right.at[plane, 0], plane, y, second)
        copy(right.at[plane, 1], plane, 1 - y, second)
    copy(rest, z, 1 - x, first)
    for k in range(1, line):
        copy(mates.at[k - 1], lax.rem(z + k, line), 1 - x, first)


def wait_rows(target, rows, sems, block):
    part = target.at[pl.ds(pl.multiple_of(rows * block, 16), rows)]
    pltpu.make_async_copy(part, part, sems.at[block]).wait()


def feed_forward_back_kernel(line, where, gt, up, sent, down_lower, upper_gate, upper_up, *refs):
    left, right, gate_pieces, up_pieces = refs[:3], refs[3], refs[4:7], refs[7:10]
    hidden, e_gate, e_up, keep, send, total, down, held, down_sems, sems = refs[10:]
    step = pl.program_id(0)
    tiles, rows = held.shape[1], left[1].shape[0]
    blocks, width = 2 * line, down.shape[1]

    @pl.when(step == 0)
    def _():
        def start(tile, carry):
            cols = pl.ds(pl.multiple_of(tile * HIDDEN_TILE, 128), HIDDEN_TILE)
            for t, (planes, rest, mates) in enumerate((gate_pieces, up_pieces)):
                pieces = (planes.at[:, :, cols], rest.at[:, cols], mates.at[:, :, cols])
                quarter_copies(line, where[0], where[2], pieces, held.at[t, tile], sems.at[t, tile])
            return carry

        start(0, 0)
        down_copies(line, where, left, right, down, down_sems)
        lax.fori_loop(1, tiles, start, 0)
        keep[...] = jnp.zeros_like(keep)
        total[...] = jnp.zeros_like(total)

    seen = 0
    for tile in range(tiles):
        until = -(-(tile + 1) * HIDDEN_TILE // rows)

        @pl.when(step == tile)
        def _(seen=seen, until=until):
            for block in range(seen, until):
                wait_rows(down, rows, down_sems, block)

        seen = until
    for t in range(2):
        pltpu.make_async_copy(held.at[t, step], held.at[t, step], sems.at[t, step]).wait()

    tile_rows = down[pl.ds(pl.multiple_of(step * HIDDEN_TILE, HIDDEN_TILE), HIDDEN_TILE), :]
    count = keep.shape[0]
    for n, sums in enumerate((keep, total)):
        own = slice(n * count, (n + 1) * count)
        gate_value, up_value = gt[own, :], up[own, :]
        dh = matrix_product_backward(sent[own, :width], tile_rows) + matrix_product_backward(
            sent[own, width:], down_lower[...]
        )
        sg = jax.nn.sigmoid(gate_value)
        act = gate_value * sg
        h = low(act * up_value)
        grad_gate = low(dh * up_value * (sg + gate_value * sg * (1.0 - sg)))
        grad_up = low(dh * act)
        hidden[own, :], e_gate[own, :], e_up[own, :] = h, grad_gate, grad_up
        sums[:, :width] += matrix_product_backward(
            grad_gate, held[0, step]
        ) + matrix_product_backward(grad_up, held[1, step])
        lanes = [width + k * ADAPTER_COLUMNS for k in range(4)]
        sums[:, lanes[0] : lanes[1]] += matrix_product_backward(grad_gate, upper_gate[...])
        sums[:, lanes[1] : lanes[2]] += matrix_product_backward(grad_up, upper_up[...])
        sums[:, lanes[2] : lanes[3]] += matrix_product(h, down_lower[...])

    @pl.when(step == tiles - 1)
    def _():
        send[...] = low(total[...])


def feed_forward_out_kernel(line, where, hidden, *refs):
    left, right = refs[:3], refs[3]
    keep, send, down, down_sems = refs[4:]
    rows = left[1].shape[0]
    down_copies(line, where, left, right, down, down_sems)
    for block in range(2 * line):
        wait_rows(down, rows, down_sems, block)
    count = keep.shape[0]
    keep[...] = matrix_product(hidden[:count, :], down[...])
    send[...] = low(matrix_product(hidden[count:, :], down[...]))


def small_cost(flops):
    return pl.CostEstimate(flops=flops // 16, bytes_accessed=flops // 8192, transcendentals=0)


class FeedForward:
    def __init__(self, place, left, right):
        self.place, self.left, self.right = place, left, right
        self.cut = left[1].shape[1]
        self.padded = left[1].shape[0]
        self.kernels = self.padded % 64 == 0
        self.where = jnp.stack([place.z, place.y, place.x]).astype(jnp.int32)

    def down(self):
        right = jnp.where(self.place.y == 0, self.right, self.right[:, ::-1])
        right = right.reshape(-1, right.shape[-1])
        return jnp.concatenate([put_quarter(self.place, *self.left), right], axis=1)

    def hidden(self, values, choices, lower, upper, pieces):
        count, width = values.shape[0], upper.shape[1]
        if not self.kernels:
            reduced = low(matrix_product(values, lower) * choices)
            full = put_quarter(self.place, *pieces)
            return matrix_product(values, full) + adapter_scale * matrix_product(
                reduced, upper
            ), reduced
        tiles = width // HIDDEN_TILE
        once = lambda v: pl.BlockSpec(v.shape, lambda i: (0, 0), pipeline_mode=pl.Buffered(1))
        columns = lambda n: pl.BlockSpec((n, HIDDEN_TILE), lambda i: (0, i))
        return pl.pallas_call(
            functools.partial(hidden_kernel, self.place.line),
            grid=(tiles,),
            out_shape=[
                jax.ShapeDtypeStruct((count, width), jnp.float32),
                jax.ShapeDtypeStruct((count, ADAPTER_COLUMNS), jnp.bfloat16),
            ],
            in_specs=[pl.BlockSpec(memory_space=pltpu.SMEM)]
            + [once(v) for v in (values, choices, lower)]
            + [columns(upper.shape[0])]
            + [pl.BlockSpec(memory_space=pl.ANY)] * 3,
            out_specs=[
                columns(count),
                pl.BlockSpec((count, ADAPTER_COLUMNS), lambda i: (0, 0)),
            ],
            scratch_shapes=[
                pltpu.VMEM((tiles, values.shape[1], HIDDEN_TILE), jnp.bfloat16),
                pltpu.SemaphoreType.DMA((tiles,)),
            ],
            compiler_params=pltpu.CompilerParams(vmem_limit_bytes=40 << 20),
            cost_estimate=small_cost(2 * count * width * values.shape[1]),
        )(self.where, values, choices, lower, upper, *pieces)

    def back(self, gt, up, sent, lower, upper_gate, upper_up, gate_pieces, up_pieces):
        count, width = gt.shape
        half = count // 2
        model = sent.shape[1] - ADAPTER_COLUMNS
        sums = model + 3 * ADAPTER_COLUMNS
        if not self.kernels:
            down = self.down()
            gate, up_part = put_quarter(self.place, *gate_pieces), put_quarter(self.place, *up_pieces)
            sg = jax.nn.sigmoid(gt)
            act = gt * sg
            h = low(act * up)
            dh = matrix_product_backward(sent[:, :model], down) + matrix_product_backward(
                sent[:, model:], lower
            )
            e_gate = low(dh * up * (sg + gt * sg * (1.0 - sg)))
            e_up = low(dh * act)
            total = jnp.concatenate(
                [
                    matrix_product_backward(e_gate, gate) + matrix_product_backward(e_up, up_part),
                    matrix_product_backward(e_gate, upper_gate),
                    matrix_product_backward(e_up, upper_up),
                    matrix_product(h, lower),
                ],
                axis=1,
            )
            return h, e_gate, e_up, total[:half], low(total[half:])
        tiles = width // HIDDEN_TILE
        once = lambda shape: pl.BlockSpec(shape, lambda i: (0, 0), pipeline_mode=pl.Buffered(1))
        columns = lambda n: pl.BlockSpec((n, HIDDEN_TILE), lambda i: (0, i))
        pieces = (*self.left, self.right, *gate_pieces, *up_pieces)
        return pl.pallas_call(
            functools.partial(feed_forward_back_kernel, self.place.line),
            grid=(tiles,),
            out_shape=[jax.ShapeDtypeStruct((count, width), jnp.bfloat16)] * 3
            + [
                jax.ShapeDtypeStruct((half, sums), jnp.float32),
                jax.ShapeDtypeStruct((half, sums), jnp.bfloat16),
            ],
            in_specs=[
                pl.BlockSpec(memory_space=pltpu.SMEM),
                columns(count),
                columns(count),
                once(sent.shape),
                pl.BlockSpec((HIDDEN_TILE, ADAPTER_COLUMNS), lambda i: (i, 0)),
                columns(ADAPTER_COLUMNS),
                columns(ADAPTER_COLUMNS),
            ]
            + [pl.BlockSpec(memory_space=pl.ANY)] * len(pieces),
            out_specs=[columns(count)] * 3 + [once((half, sums))] * 2,
            scratch_shapes=[
                pltpu.VMEM((half, sums), jnp.float32),
                pltpu.VMEM((width, model), jnp.bfloat16),
                pltpu.VMEM((2, tiles, model, HIDDEN_TILE), jnp.bfloat16),
                pltpu.SemaphoreType.DMA((2 * self.place.line,)),
                pltpu.SemaphoreType.DMA((2, tiles)),
            ],
            compiler_params=pltpu.CompilerParams(vmem_limit_bytes=60 << 20),
            cost_estimate=small_cost(6 * count * width * model),
        )(self.where, gt, up, sent, lower, upper_gate, upper_up, *pieces)

    def out(self, h, model):
        count, width = h.shape
        half = count // 2
        if not self.kernels:
            total = matrix_product(h, self.down())
            return total[:half], low(total[half:])
        held = pl.BlockSpec(memory_space=pltpu.VMEM)
        return pl.pallas_call(
            functools.partial(feed_forward_out_kernel, self.place.line),
            out_shape=[
                jax.ShapeDtypeStruct((half, model), jnp.float32),
                jax.ShapeDtypeStruct((half, model), jnp.bfloat16),
            ],
            in_specs=[pl.BlockSpec(memory_space=pltpu.SMEM), held]
            + [pl.BlockSpec(memory_space=pl.ANY)] * 4,
            out_specs=[held] * 2,
            scratch_shapes=[
                pltpu.VMEM((width, model), jnp.bfloat16),
                pltpu.SemaphoreType.DMA((2 * self.place.line,)),
            ],
            compiler_params=pltpu.CompilerParams(vmem_limit_bytes=40 << 20),
            cost_estimate=small_cost(2 * count * width * model),
        )(self.where, h, *self.left, self.right)


def columns_kernel(own, padded, quarter, value, *outs):
    each, window = GROUP * own, 2 * padded
    rows, width = value.shape
    step = pl.program_id(0)
    lane = lax.broadcasted_iota(jnp.int32, (rows, window), 1)
    for out, k in zip(outs, (quarter[0], quarter[0] ^ 2)):
        turned = []
        for n in range(2):
            start = each * (2 * step + n) + own * k
            base = jnp.minimum(start // 128, (width - window) // 128) * 128
            piece = value[:, pl.ds(pl.multiple_of(base, 128), window)].astype(jnp.float32)
            turned.append(pltpu.roll(piece, lax.rem(window + n * padded - (start - base), window), 1))
        kept = jnp.where(lane < own, turned[0], 0.0)
        kept = jnp.where((lane >= padded) & (lane < padded + own), turned[1], kept)
        out[...] = low(kept)


def hidden_columns(place, value, blocks, padded):
    rows, width = value.shape
    own = width // (blocks * GROUP)
    if padded % 64 or 2 * padded > width:

        def take(k):
            def cut(given):
                pieces = []
                for i in range(blocks):
                    start = own * (GROUP * i + k)
                    piece = given[:, start : start + own]
                    pieces.append(jnp.pad(piece, ((0, 0), (0, padded - own))))
                return jnp.concatenate(pieces, axis=1)

            return cut

        branches = [take(k) for k in range(GROUP)]
        return [lax.switch(k, branches, value) for k in (place.q, place.q ^ 2)]
    return pl.pallas_call(
        functools.partial(columns_kernel, own, padded),
        grid=(blocks // 2,),
        out_shape=[jax.ShapeDtypeStruct((rows, blocks * padded), value.dtype)] * 2,
        in_specs=[
            pl.BlockSpec(memory_space=pltpu.SMEM),
            pl.BlockSpec((rows, width), lambda i: (0, 0)),
        ],
        out_specs=[pl.BlockSpec((rows, 2 * padded), lambda i: (0, i))] * 2,
        compiler_params=pltpu.CompilerParams(vmem_limit_bytes=32 << 20),
        cost_estimate=pl.CostEstimate(
            flops=8 * rows * width, bytes_accessed=4 * rows * width, transcendentals=0
        ),
    )(place.q.astype(jnp.int32).reshape(1), value)


def hidden_rows(place, value, quarter, blocks, padded):
    own = value.shape[0] // (blocks * GROUP)
    split = value.reshape(blocks, GROUP, own, -1)
    got = lax.dynamic_index_in_dim(split, quarter, 1, keepdims=False)
    return jnp.pad(got, ((0, 0), (0, padded - own), (0, 0))).reshape(blocks * padded, -1)


def spread_kernel(own, padded, quarter, value, out, total):
    rows, width = total.shape
    window = 2 * padded
    total[...] = jnp.zeros_like(total)
    lane = lax.broadcasted_iota(jnp.int32, (rows, window), 1)
    for i in range(width // (GROUP * own)):
        pair, n = i // 2, i % 2
        start = own * (GROUP * i + quarter[0])
        base = jnp.minimum(start // 128, (width - window) // 128) * 128
        piece = value[:, pair * window : (pair + 1) * window].astype(jnp.float32)
        inside = (lane >= n * padded) & (lane < n * padded + own)
        turned = pltpu.roll(
            jnp.where(inside, piece, 0.0),
            lax.rem(window - n * padded + (start - base), window),
            1,
        )
        total[:, pl.ds(pl.multiple_of(base, 128), window)] += turned
    out[...] = low(total[...])


def spread_columns(place, value, width, blocks, padded):
    rows = value.shape[0]
    own = width // (blocks * GROUP)
    if padded % 64 or 2 * padded > width:

        def lay(k):
            def build(given):
                pieces = []
                for i in range(blocks):
                    piece = given[:, padded * i : padded * i + own]
                    pieces.append(jnp.pad(piece, ((0, 0), (own * k, own * (GROUP - 1 - k)))))
                return jnp.concatenate(pieces, axis=1)

            return build

        return lax.switch(place.q, [lay(k) for k in range(GROUP)], value)
    return pl.pallas_call(
        functools.partial(spread_kernel, own, padded),
        out_shape=jax.ShapeDtypeStruct((rows, width), jnp.bfloat16),
        in_specs=[
            pl.BlockSpec(memory_space=pltpu.SMEM),
            pl.BlockSpec(memory_space=pltpu.VMEM),
        ],
        out_specs=pl.BlockSpec(memory_space=pltpu.VMEM),
        scratch_shapes=[pltpu.VMEM((rows, width), jnp.float32)],
        compiler_params=pltpu.CompilerParams(vmem_limit_bytes=32 << 20),
        cost_estimate=pl.CostEstimate(
            flops=8 * rows * width, bytes_accessed=4 * rows * width, transcendentals=0
        ),
    )(place.q.astype(jnp.int32).reshape(1), value)


def both(kept, got):
    return low(kept.astype(jnp.float32) + got.astype(jnp.float32))


def pick(values, index, axis):
    return lax.dynamic_index_in_dim(values, index, axis, keepdims=False)


def gradients_kernel(lower_rows, upper_rows, *refs):
    n1, dz_qkv, z_qkv, e_qkv, o, dz_out, z_out, e_out = refs[:8]
    n2, dz_gate, dz_up, z_down, e_down, _, flat, turned, staged, sems = refs[8:]
    lower = [(n1[...], dz_qkv[t]) for t in range(3)]
    lower += [(o[...], dz_out[...]), (n2[...], dz_gate[...]), (n2[...], dz_up[...])]
    upper = [(z_qkv[t], e_qkv[t]) for t in range(3)]
    upper += [(z_out[...], e_out[...]), (z_down[...], e_down[...])]
    rows = staged.shape[1]
    ranks = ADAPTER_COLUMNS
    parts = rows // ranks
    starts = [lower_rows + rows * k for k in range(6)] + [upper_rows + rows * k for k in range(5)]
    copies = []
    for k, start in enumerate(starts):
        slot = k % 2
        if k > 1:
            copies[k - 2].wait()
        if k < 6:
            staged[slot] = low(outer_product_sum(*lower[k]))
        else:
            full = adapter_scale * outer_product_sum(*upper[k - 6])
            for j in range(parts):
                turned[pl.ds(j, ranks, parts), :] = full[:, j * ranks : (j + 1) * ranks]
            staged[slot] = low(turned[...])
        copies.append(
            pltpu.make_async_copy(staged.at[slot], flat.at[pl.ds(start, rows)], sems.at[slot])
        )
        copies[k].start()
    copies[-2].wait()
    copies[-1].wait()


def model_gradients(operands, flat, lower_rows, upper_rows):
    held = pl.BlockSpec(memory_space=pltpu.VMEM)
    apart = pl.BlockSpec(memory_space=pl.ANY)
    return pl.pallas_call(
        functools.partial(gradients_kernel, lower_rows, upper_rows),
        out_shape=jax.ShapeDtypeStruct(flat.shape, flat.dtype),
        in_specs=[held] * len(operands) + [apart],
        out_specs=apart,
        scratch_shapes=[
            pltpu.VMEM((MODEL_WIDTH, ADAPTER_COLUMNS), jnp.float32),
            pltpu.VMEM((2, MODEL_WIDTH, ADAPTER_COLUMNS), jnp.bfloat16),
            pltpu.SemaphoreType.DMA((2,)),
        ],
        input_output_aliases={len(operands): 0},
        compiler_params=pltpu.CompilerParams(vmem_limit_bytes=40 << 20),
        cost_estimate=pl.CostEstimate(flops=1 << 28, bytes_accessed=1 << 22, transcendentals=0),
    )(*operands, flat)


def reduce_over_cores(place, flat, later):
    pairs = place.line * 2 * (place.shard // 2)
    rows = flat.shape[0] // pairs
    half = -(-rows // 16) * 8
    split = flat.reshape(place.line, 2, place.shard // 2, rows, ADAPTER_COLUMNS)
    start = rows - half
    keep = lax.dynamic_slice_in_dim(split, place.c * start, half, 3)
    send = lax.dynamic_slice_in_dim(split, (1 - place.c) * start, half, 3)
    got, later = together(place.by_c(send), later)
    return both(keep, got), later


class OwnerSum:
    def __init__(self, place, total, share):
        self.place, self.share, self.half = place, share, total.shape[3]
        cut = self.half // 16 * 8
        one, two = total[:, :, :, :cut], total[:, :, :, cut:]
        self.kept = (pick(one, place.y, 1), pick(two, place.x, 2))
        self.got = (
            place.by_y(pick(one, 1 - place.y, 1)),
            place.by_x(pick(two, 1 - place.x, 2)),
        )

    def over_chips(self):
        place = self.place
        one, two = both(self.kept[0], self.got[0]), both(self.kept[1], self.got[1])
        got_one = place.by_x(pick(one, 1 - place.x, 1))
        got_two = place.by_y(pick(two, 1 - place.y, 1))
        one, two = both(pick(one, place.x, 1), got_one), both(pick(two, place.y, 1), got_two)
        return jnp.concatenate([one, two], axis=1)

    def over_planes(self, total):
        place = self.place
        got = [
            place.ring_z(pick(total, (place.z + k) % place.line, 0), k)
            for k in range(1, place.line)
        ]
        result = pick(total, place.z, 0).astype(jnp.float32)
        for value in got:
            result = result + value.astype(jnp.float32)
        start = place.c * (self.half - self.share)
        return lax.dynamic_slice_in_dim(result, start, self.share, 0)


def gather_owners(place, own):
    share = own.shape[0]
    half = -(-share // 8) * 8
    start = 2 * share - half
    mate = place.by_c(own)
    head, tail = jnp.where(place.c == 0, own, mate), jnp.where(place.c == 0, mate, own)
    pair = jnp.concatenate([head, tail], axis=0)
    planes = place.all_z(lax.dynamic_slice_in_dim(pair, place.c * start, half, 0))
    cut = half // 16 * 8
    full = jnp.zeros(
        (place.line, 2, place.shard // 2, 2 * share, ADAPTER_COLUMNS), own.dtype
    )
    for part, x_first, at in ((planes[:, :cut], True, 0), (planes[:, cut:], False, cut)):
        x_part, y_part = place.by_x(part), place.by_y(part)
        xy_part = place.by_y(x_part) if x_first else place.by_x(y_part)
        for value, y, x in (
            (part, place.y, place.x),
            (x_part, place.y, 1 - place.x),
            (y_part, 1 - place.y, place.x),
            (xy_part, 1 - place.y, 1 - place.x),
        ):
            for held, c in ((value, place.c), (place.by_c(value), 1 - place.c)):
                where = (0, y, x, c * start + at, 0)
                full = lax.dynamic_update_slice(full, held[:, None, None], where)
    return full.reshape(-1)


def shards(
    dp,
    shard,
    tokens,
    cotangent,
    arrival,
    lengths,
    adapter_set,
    gain_one,
    gain_two,
    w_query,
    w_key,
    w_value,
    w_out,
    w_gate,
    w_up,
    w_down,
    adapters,
    first_moment_running,
    second_moment_running,
):
    place = Place(dp, shard)
    token_order = arrival[0]
    count = token_order.shape[0]
    padded = -(-(FEEDFORWARD_UNITS // (dp * GROUP)) // 16) * 16


    weights = (w_query, w_key, w_value, w_out)
    s, half = place.x * 2 + place.c, MODEL_WIDTH // 2
    cut = MODEL_WIDTH - MODEL_WIDTH * 2 // 9
    stacked = jnp.stack(weights)
    mine = lax.dynamic_index_in_dim(stacked, s, 0, keepdims=False)
    first = place.all_z(mine[:, :half])
    second = place.all_z(mine[:, half:])
    near_y = place.by_y(mine)
    table = jnp.concatenate([lengths, adapter_set], axis=1)
    table_y = place.by_y(table)
    own_gate, other_gate = hidden_columns(place, w_gate, dp, padded)
    own_up, other_up = hidden_columns(place, w_up, dp, padded)
    near_y, table_y, other_gate, other_up = together(near_y, table_y, other_gate, other_up)

    near_x = place.by_x(near_y)
    got_gate, got_up = place.by_y(other_gate), place.by_y(other_up)
    near_y_c = place.by_c(near_y)
    tables = jnp.concatenate([table, table_y], axis=0)
    tables_c = place.by_c(tables)
    own_down = hidden_rows(place, w_down, place.q, 1, padded)
    other_down = hidden_rows(place, w_down, place.q ^ 2, 1, padded)
    first, got_gate, got_up, near_x, near_y_c, tables_c, tokens = together(
        first, got_gate, got_up, near_x, near_y_c, tables_c, tokens
    )

    straight = place.y == place.x
    gate_planes = place.all_z(jnp.where(straight, own_gate, got_gate))
    up_planes = place.all_z(jnp.where(straight, own_up, got_up))
    gate_rest, up_rest = (
        jnp.where(straight, got_gate, own_gate),
        jnp.where(straight, got_up, own_up),
    )
    tables = jnp.concatenate([tables, tables_c], axis=0)
    lines = place.other_z(first)
    x0, y0, lines_c = place.by_x(lines), place.by_y(lines), place.by_c(lines)
    near_x_c = place.by_c(near_x)
    arrived_x = lax.all_to_all(tokens, "dp", split_axis=0, concat_axis=0, tiled=True)
    x0, y0, lines_c, near_x_c, second = together(x0, y0, lines_c, near_x_c, second)

    lines2 = place.other_z(second)
    x1, y1, lines2_c = place.by_x(lines2), place.by_y(lines2), place.by_c(lines2)
    x0_c, y0_c = place.by_c(x0), place.by_c(y0)
    x1, y1, lines2_c, x0_c, y0_c, x0, arrived_x = together(
        x1, y1, lines2_c, x0_c, y0_c, x0, arrived_x
    )

    A_model, A_hidden, B_model, B_hidden = restore_structure(adapters)
    B_gate, _ = hidden_columns(place, B_hidden[0], dp, padded)
    B_up, _ = hidden_columns(place, B_hidden[1], dp, padded)
    A_down = hidden_rows(place, A_hidden, place.q, dp, padded)
    choice, allowed, cosine_table, sine_table = block_tables(lengths[0], adapter_set[0])
    choices = jnp.concatenate(
        [block_tables(tables[k, :SEQ_DEV], tables[k, SEQ_DEV:])[0] for k in range(GROUP)], axis=0
    )
    xy0, xy1 = place.by_y(x0), place.by_x(y1)
    x1_c, y1_c = place.by_c(x1), place.by_c(y1)
    xy0, xy1, x1_c, y1_c, B_gate, B_up, A_down, choices, gate_planes, other_down, cotangent = together(
        xy0, xy1, x1_c, y1_c, B_gate, B_up, A_down, choices, gate_planes, other_down, cotangent
    )

    got_down = place.by_y(other_down)
    arrived_cot = lax.all_to_all(cotangent, "dp", split_axis=0, concat_axis=0, tiled=True)
    gate_mates = place.by_x(place.other_z(gate_planes))
    attention = AttentionWeights(
        place,
        weights,
        ((lines, lines_c, x0, x0_c), (lines2, lines2_c, x1, x1_c)),
        ((y0, y0_c, xy0, place.by_c(xy0)), (y1, y1_c, xy1, place.by_c(xy1))),
        (near_y, near_y_c, near_x, near_x_c),
    )
    gain_first = gain_one.astype(jnp.float32)
    gain_second = gain_two.astype(jnp.float32)

    x = arrived_x[token_order].astype(jnp.float32)
    scale_one = rms_scale(x)
    n1 = low(x * scale_one * gain_first)

    z_qkv = low(
        jnp.einsum("nd,tdr->tnr", n1, A_model[:3], preferred_element_type=jnp.float32) * choice
    )
    bias = jnp.where(allowed, 0.0, -jnp.inf)
    lin, got_down = together(attention.times(n1, 0, 3), got_down)
    left_planes = place.all_z(jnp.where(straight, own_down, got_down)[:, :cut])
    left_rest = jnp.where(straight, got_down, own_down)[:, :cut]
    right_planes = place.all_z(jnp.stack([own_down[:, cut:], got_down[:, cut:]]))
    qkv, o = attention_call(
        attention_kernel,
        (
            (lin, 2),
            (z_qkv, None),
            (B_model[:3], 2),
            (cosine_table, None),
            (sine_table, None),
            (bias, None),
        ),
        (((3, count, MODEL_WIDTH), 2), ((count, MODEL_WIDTH), 1)),
    )
    o, up_planes, gate_mates = together(o, up_planes, gate_mates)
    up_mates = place.by_x(place.other_z(up_planes))
    z_out, delta_out = apply_adapter_delta(o, A_model[3], B_model[3], choice)
    m = x + residual_branch_scale * (attention.times(o, 3, 1)[0] + delta_out)
    scale_two = rms_scale(m)
    n2 = low(m * scale_two * gain_second)

    n2_y = place.by_y(n2)
    n2_y, arrived_cot, left_planes, up_mates = together(
        n2_y, arrived_cot, left_planes, up_mates
    )
    left_mates = place.by_x(place.other_z(left_planes))
    g = arrived_cot[token_order].astype(jnp.float32)
    e_down = low(residual_branch_scale * g)
    dz_down = low(adapter_scale * matrix_product_backward(e_down, B_model[4]) * choice)
    sent = jnp.concatenate([e_down, dz_down], axis=1)
    sent_y = place.by_y(sent)
    n2_all = jnp.concatenate([n2, n2_y], axis=0)
    n2_all = jnp.concatenate([n2_all, place.by_c(n2_all)], axis=0)
    gate_pieces = (gate_planes, gate_rest, gate_mates)
    forward = FeedForward(place, (left_planes, left_rest, left_mates), right_planes)
    gt, z_gate = forward.hidden(n2_all, choices, A_model[4], B_gate, gate_pieces)
    up_pieces = (up_planes, up_rest, up_mates)
    up, z_up = forward.hidden(n2_all, choices, A_model[5], B_up, up_pieces)
    gt, up, left_mates, right_planes, sent_y = together(gt, up, left_mates, right_planes, sent_y)
    sent = jnp.concatenate([sent, sent_y], axis=0)
    sent = jnp.concatenate([sent, place.by_c(sent)], axis=0)
    dz_down_all = sent[:, MODEL_WIDTH:]
    feed = FeedForward(place, (left_planes, left_rest, left_mates), right_planes)
    h, e_gate, e_up, keep, send = feed.back(
        gt, up, sent, A_down, B_gate, B_up, gate_pieces, up_pieces
    )
    own_sum, other_sum = place.half_sum(keep, send)
    other_sum, h, e_gate, e_up = together(low(other_sum), h, e_gate, e_up)
    got = place.by_y(other_sum)
    y_keep, y_send = feed.out(h, MODEL_WIDTH)
    dA_down = low(outer_product_sum(h, dz_down_all))
    own_hidden = FEEDFORWARD_UNITS // (dp * GROUP)
    dA_hidden = lax.dynamic_update_slice(
        jnp.zeros((dp, GROUP, own_hidden, ADAPTER_COLUMNS), jnp.bfloat16),
        dA_down.reshape(dp, 1, padded, ADAPTER_COLUMNS)[:, :, :own_hidden],
        (0, place.q, 0, 0),
    )
    lower_rows, upper_rows = 6 * MODEL_WIDTH, 5 * MODEL_WIDTH
    hidden_rows_count = FEEDFORWARD_UNITS
    flat = jnp.concatenate(
        [
            jnp.zeros((lower_rows, ADAPTER_COLUMNS), jnp.bfloat16),
            dA_hidden.reshape(-1, ADAPTER_COLUMNS),
            jnp.zeros((upper_rows, ADAPTER_COLUMNS), jnp.bfloat16),
        ]
        + [
            spread_columns(
                place, low(adapter_scale * outer_product_sum(z, e)), FEEDFORWARD_UNITS, dp, padded
            ).reshape(-1, ADAPTER_COLUMNS)
            for z, e in ((z_gate, e_gate), (z_up, e_up))
        ]
    )
    got, y_send, flat = together(got, y_send, flat)
    back_sum = own_sum + got.astype(jnp.float32)
    y_own, y_other = place.half_sum(y_keep, y_send)
    y_got = place.by_y(low(y_other))
    cuts = [MODEL_WIDTH + k * ADAPTER_COLUMNS for k in range(3)]
    dz_gate, dz_up, z_down = jnp.split(back_sum, cuts, axis=1)[1:]
    dz_gate, dz_up = low(adapter_scale * dz_gate * choice), low(adapter_scale * dz_up * choice)
    z_down = low(z_down * choice)
    dn2 = (
        back_sum[:, :MODEL_WIDTH]
        + matrix_product_backward(dz_gate, A_model[4])
        + matrix_product_backward(dz_up, A_model[5])
    )
    dm = g + norm_back(m, scale_two, gain_second, dn2)
    e_out = low(residual_branch_scale * dm)
    dz_out = low(adapter_scale * matrix_product_backward(e_out, B_model[3]) * choice)
    (e_qkv,) = attention_call(
        attention_back_kernel,
        (
            (qkv, 2),
            (attention.times_transposed(e_out[None], 3, 1), 1),
            (dz_out, None),
            (A_model[3], 0),
            (cosine_table, None),
            (sine_table, None),
            (bias, None),
        ),
        (((3, count, MODEL_WIDTH), 2),),
    )
    e_qkv, y_got = together(e_qkv, y_got)
    y = m + residual_branch_scale * (
        y_own + y_got.astype(jnp.float32) + adapter_scale * matrix_product(z_down, B_model[4])
    )
    inverse = (
        jnp.zeros_like(token_order).at[token_order].set(jnp.arange(count, dtype=jnp.int32))
    )
    dz_qkv = low(
        adapter_scale
        * jnp.einsum("tnd,trd->tnr", e_qkv, B_model[:3], preferred_element_type=jnp.float32)
        * choice
    )
    flat = model_gradients(
        (
            n1,
            dz_qkv,
            z_qkv,
            e_qkv,
            o,
            dz_out,
            z_out,
            e_out,
            n2,
            dz_gate,
            dz_up,
            z_down,
            e_down,
        ),
        flat,
        0,
        lower_rows + hidden_rows_count,
    )
    share = flat.shape[0] // (dp * shard)
    total, (e_qkv, dz_qkv, y) = reduce_over_cores(place, flat, (e_qkv, dz_qkv, y))
    owner = OwnerSum(place, total, share)
    back_out = lax.all_to_all(low(y)[inverse], "dp", split_axis=0, concat_axis=0, tiled=True)
    dn1 = attention.times_transposed(e_qkv, 0, 3) + jnp.einsum(
        "tnr,tdr->nd", dz_qkv, A_model[:3], preferred_element_type=jnp.float32
    )
    dx = dm + norm_back(x, scale_one, gain_first, dn1)
    owner.got, back_out, dx = together(owner.got, back_out, low(dx))
    total = owner.over_chips()
    total, back_grad = together(
        total, lax.all_to_all(dx[inverse], "dp", split_axis=0, concat_axis=0, tiled=True)
    )
    gradient = owner.over_planes(total)
    offset = lax.axis_index(AXES) * share
    own_params = lax.dynamic_slice_in_dim(
        adapters.reshape(-1, ADAPTER_COLUMNS), offset, share
    ).astype(jnp.float32)
    first = first_moment_running.reshape(share, ADAPTER_COLUMNS)
    second = second_moment_running.reshape(share, ADAPTER_COLUMNS)
    fresh_first = first_decay_rate * first + (1.0 - first_decay_rate) * gradient
    fresh_second = second_decay_rate * second + (1.0 - second_decay_rate) * gradient * gradient
    unbiased_first = fresh_first / (1.0 - first_decay_rate**OPT_STEP)
    unbiased_second = fresh_second / (1.0 - second_decay_rate**OPT_STEP)
    update = (
        unbiased_first / (jnp.sqrt(unbiased_second) + adaptive_epsilon)
        + weight_shrink_rate * own_params
    )
    updated = gather_owners(place, low(own_params - learning_rate * update))

    return (
        back_out,
        back_grad,
        gradient.reshape(-1),
        fresh_first.reshape(-1),
        fresh_second.reshape(-1),
        updated,
    )


def solution(mesh):
    rows = P(AXES, None)
    weight = P("dp", None)
    return jax.shard_map(
        functools.partial(shards, mesh.shape["dp"], mesh.shape["shard"]),
        mesh=mesh,
        in_specs=(rows,) * 5 + (P(), P()) + (weight,) * 7 + (P(), P(AXES), P(AXES)),
        out_specs=(rows, rows, P(AXES), P(AXES), P(AXES), P()),
        check_vma=False,
    )
```

```python
import functools
import math

import jax
import jax.numpy as jnp
from jax import lax
from jax.experimental import pallas as pl
from jax.experimental.pallas import tpu as pltpu
from jax.sharding import PartitionSpec as P

MODEL_WIDTH = 2304
ATTENTION_HEADS = 36
HEAD_SIZE = 64
FEEDFORWARD_UNITS = 5760
ADAPTER_RANK = 16
OPT_STEP = 10
SEQ_DEV = 4
TOK_DEV = 256
ADAPTER_COLUMNS = 128


norm_eps = 1e-05
residual_branch_scale = 1.4 / math.sqrt(40.0)
adapter_scale = 2.0
rope_base = 10000.0
first_decay_rate = 0.9
second_decay_rate = 0.999
adaptive_epsilon = 1e-08
weight_shrink_rate = 0.01
learning_rate = 0.01


def matrix_product(left_side, right_side):
    return jnp.dot(left_side, right_side, preferred_element_type=jnp.float32)


def matrix_product_backward(left_side, right_side):
    return lax.dot_general(
        left_side, right_side, (((1,), (1,)), ((), ())), preferred_element_type=jnp.float32
    )


def outer_product_sum(left_side, right_side):
    return lax.dot_general(
        left_side, right_side, (((0,), (0,)), ((), ())), preferred_element_type=jnp.float32
    )


def low(values):
    return values.astype(jnp.bfloat16)


def block_tables(sequence_lengths, sequence_adapter_index):
    row_ids = jnp.arange(TOK_DEV, dtype=jnp.int32)
    seq_ends = jnp.cumsum(sequence_lengths, dtype=jnp.int32)
    seq_starts = seq_ends - sequence_lengths
    segment = jnp.sum(
        (row_ids[:, None] >= seq_ends[None, :]).astype(jnp.int32), axis=1, dtype=jnp.int32
    )
    member = (segment[:, None] == jnp.arange(SEQ_DEV, dtype=jnp.int32)[None, :]).astype(jnp.int32)
    position = row_ids - jnp.sum(member * seq_starts[None, :], axis=1, dtype=jnp.int32)
    token_adapter_index = jnp.sum(member * sequence_adapter_index[None, :], axis=1, dtype=jnp.int32)
    adapter_choice_index = (
        jnp.arange(ADAPTER_COLUMNS, dtype=jnp.int32)[None, :] // ADAPTER_RANK
        == token_adapter_index[:, None]
    ).astype(jnp.float32)
    allowed = (segment[:, None] == segment[None, :]) & (row_ids[None, :] <= row_ids[:, None])
    half_dim = HEAD_SIZE // 2
    inv_freq = jnp.power(rope_base, -2.0 * jnp.arange(half_dim, dtype=jnp.float32) / HEAD_SIZE)
    angles = position.astype(jnp.float32)[:, None] * inv_freq[None, :]
    cosine, sine = jnp.cos(angles), jnp.sin(angles)
    return (
        adapter_choice_index,
        allowed,
        jnp.concatenate([cosine] * 4, axis=1),
        jnp.concatenate([-sine, sine] * 2, axis=1),
    )


def restore_structure(flattened_vector):
    first_boundary = 6 * MODEL_WIDTH * ADAPTER_COLUMNS
    second_boundary = first_boundary + FEEDFORWARD_UNITS * ADAPTER_COLUMNS
    third_boundary = second_boundary + 5 * ADAPTER_COLUMNS * MODEL_WIDTH
    return (
        flattened_vector[:first_boundary].reshape(6, MODEL_WIDTH, ADAPTER_COLUMNS),
        flattened_vector[first_boundary:second_boundary].reshape(
            FEEDFORWARD_UNITS, ADAPTER_COLUMNS
        ),
        flattened_vector[second_boundary:third_boundary].reshape(5, ADAPTER_COLUMNS, MODEL_WIDTH),
        flattened_vector[third_boundary:].reshape(2, ADAPTER_COLUMNS, FEEDFORWARD_UNITS),
    )


def rms_scale(values):
    return lax.rsqrt(jnp.mean(values * values, axis=-1, keepdims=True) + norm_eps)


def norm_back(values, scale, gain, gradient_value):
    weighted = gradient_value * gain
    return scale * weighted - values * scale**3 * jnp.mean(
        values * weighted, axis=-1, keepdims=True
    )


def apply_adapter_delta(input_rows, adapter_down_pair, adapter_up_pair, adapter_choice_index):
    reduced_total = low(
        matrix_product(input_rows, adapter_down_pair) * adapter_choice_index
    )
    return (reduced_total, adapter_scale * matrix_product(reduced_total, adapter_up_pair))


def swap_halves(values):
    lane = lax.broadcasted_iota(jnp.int32, values.shape, 1)
    half, width = HEAD_SIZE // 2, values.shape[1]
    return jnp.where(
        lane % HEAD_SIZE < half, pltpu.roll(values, width - half, 1), pltpu.roll(values, half, 1)
    )


def head_scores(query, key, bias):
    scores = matrix_product_backward(query, key) * HEAD_SIZE ** (-0.5) + bias
    expanded = jnp.exp(scores - jnp.max(scores, axis=-1, keepdims=True))
    return expanded / jnp.sum(expanded, axis=-1, keepdims=True)


def attention_kernel(lin, z, up, cosine, sine, bias, qkv, attended):
    full = [lin[t] + adapter_scale * matrix_product(z[t], up[t]) for t in range(3)]
    query, key = (
        low(v * cosine[...] + swap_halves(v) * sine[...]) for v in full[:2]
    )
    value = low(full[2])
    qkv[0], qkv[1], qkv[2] = query, key, value
    first = lax.broadcasted_iota(jnp.int32, query.shape, 1) < HEAD_SIZE
    results = []
    for mine in (first, ~first):
        probs = head_scores(jnp.where(mine, query, jnp.zeros_like(query)), key, bias[...])
        results.append(matrix_product(low(probs), value))
    attended[...] = low(jnp.where(first, results[0], results[1]))


def attention_back_kernel(qkv, lin, dz, down, cosine, sine, bias, grads):
    query, key, value = qkv[0], qkv[1], qkv[2]
    grad = low(lin[...] + matrix_product_backward(dz[...], down[...]))
    first = lax.broadcasted_iota(jnp.int32, query.shape, 1) < HEAD_SIZE
    nothing = jnp.zeros_like(query)
    results = []
    for mine in (first, ~first):
        probs = head_scores(jnp.where(mine, query, nothing), key, bias[...])
        grad_probs = matrix_product_backward(jnp.where(mine, grad, nothing), value)
        row_delta = jnp.sum(probs * grad_probs, axis=-1, keepdims=True)
        grad_scores = low(probs * (grad_probs - row_delta))
        results.append(
            (
                matrix_product(grad_scores, key),
                outer_product_sum(grad_scores, query),
                outer_product_sum(low(probs), grad),
            )
        )
    scale = HEAD_SIZE ** (-0.5)
    grad_query, grad_key, grad_value = (
        jnp.where(first, one, two) for one, two in zip(*results)
    )
    for t, v in enumerate((grad_query * scale, grad_key * scale)):
        grads[t] = low(v * cosine[...] - swap_halves(v) * sine[...])
    grads[2] = low(grad_value)


def attention_call(kernel, operands, outs):
    pairs = 2 * HEAD_SIZE

    def spec(shape, axis):
        block = tuple(pairs if k == axis else n for k, n in enumerate(shape))
        return pl.BlockSpec(block, lambda i: tuple(i if k == axis else 0 for k in range(len(shape))))

    count = operands[-1][0].shape[0]
    return pl.pallas_call(
        kernel,
        grid=(ATTENTION_HEADS // 2,),
        out_shape=[jax.ShapeDtypeStruct(shape, jnp.bfloat16) for shape, _ in outs],
        in_specs=[spec(v.shape, axis) for v, axis in operands],
        out_specs=[spec(shape, axis) for shape, axis in outs],
        compiler_params=pltpu.CompilerParams(vmem_limit_bytes=48 << 20),
        cost_estimate=pl.CostEstimate(
            flops=8 * count * count * MODEL_WIDTH // 16,
            bytes_accessed=24 * count * MODEL_WIDTH // 16,
            transcendentals=0,
        ),
    )(*[v for v, _ in operands])


GROUP = 4
AXES = ("dp", "shard")


def together(*values):
    return lax.optimization_barrier(values)


class Place:
    def __init__(self, dp, shard):
        self.line, self.shard = dp // 2, shard
        i, s = lax.axis_index("dp"), lax.axis_index("shard")
        self.z, self.y, self.x, self.c = i // 2, i % 2, s // 2, s % 2
        self.q = self.y * 2 + self.c
        self.spots = [
            (z, y, x, c)
            for z in range(self.line)
            for y in range(2)
            for x in range(shard // 2)
            for c in range(2)
        ]

    def number(self, z, y, x, c):
        return (z * 2 + y) * self.shard + x * 2 + c

    def move(self, value, target):
        pairs = []
        for spot in self.spots:
            to = target(*spot)
            if to is not None:
                pairs.append((self.number(*spot), self.number(*to)))
        return lax.ppermute(value, AXES, pairs)

    def by_y(self, value):
        return self.move(value, lambda z, y, x, c: (z, 1 - y, x, c))

    def by_x(self, value):
        return self.move(value, lambda z, y, x, c: (z, y, 1 - x, c))

    def by_c(self, value):
        return self.move(value, lambda z, y, x, c: (z, y, x, 1 - c))

    def ring_z(self, value, step):
        return self.move(value, lambda z, y, x, c: ((z + step) % self.line, y, x, c))

    def all_z(self, block):
        groups = [[z * 2 + y for z in range(self.line)] for y in range(2)]
        return lax.all_gather(block, "dp", axis=0, axis_index_groups=groups)

    def other_z(self, blocks):
        return jnp.stack(
            [
                lax.dynamic_index_in_dim(blocks, (self.z + k) % self.line, 0, keepdims=False)
                for k in range(1, self.line)
            ]
        )

    def gather_group(self, rows):
        pair = jnp.concatenate([rows, self.by_y(rows)], axis=0)
        return jnp.concatenate([pair, self.by_c(pair)], axis=0)

    def half_sum(self, keep, send):
        return (keep + self.by_c(send).astype(jnp.float32)).reshape(2, -1, keep.shape[1])


def put(buffer, block, *where):
    block = block.reshape((1,) * len(where) + block.shape)
    return lax.dynamic_update_slice(
        buffer, block, tuple(where) + (0,) * (buffer.ndim - len(where))
    )


def put_quarter(place, planes, rest, mates):
    full = jnp.zeros((place.line, 2) + rest.shape, rest.dtype)
    full = lax.dynamic_update_slice(full, planes[:, None], (0, place.x) + (0,) * rest.ndim)
    full = put(full, rest, place.z, 1 - place.x)
    for k in range(1, place.line):
        full = put(full, mates[k - 1], (place.z + k) % place.line, 1 - place.x)
    return full.reshape((-1,) + rest.shape[1:])


class AttentionWeights:
    def __init__(self, place, weights, same, across, near):
        self.place, self.native = place, weights
        self.same, self.across, self.near = same, across, near
        self.s = place.x * 2 + place.c
        self.rows, self.half = weights[0].shape[0], weights[0].shape[1] // 2

    def full(self, t):
        place = self.place
        halves = []
        for h in range(2):
            cols = slice(h * self.half, (h + 1) * self.half)
            buffer = jnp.zeros((place.line, 2, self.rows, self.half), self.native[t].dtype)
            buffer = put(buffer, self.native[t][:, cols], place.z, place.y)
            for r in range(4):
                near = self.near[r][:, cols]
                with_r = put(buffer, near, place.z, 1 - place.y)
                for k in range(1, place.line):
                    plane = (place.z + k) % place.line
                    with_r = put(with_r, self.same[h][r][k - 1], plane, place.y)
                    with_r = put(with_r, self.across[h][r][k - 1], plane, 1 - place.y)
                buffer = jnp.where(self.s ^ r == t, with_r, buffer)
            halves.append(buffer.reshape(-1, self.half))
        return jnp.concatenate(halves, axis=1)

    def times(self, values, first, count):
        if self.rows % 16:
            return jnp.stack([matrix_product(values, self.full(first + j)) for j in range(count)])
        return self.call(values, first, count, False)

    def times_transposed(self, values, first, count):
        if self.rows % 16:
            return sum(
                matrix_product_backward(values[j], self.full(first + j)) for j in range(count)
            )
        return self.call(values, first, count, True)

    def call(self, values, first, count, back):
        place, rows, half = self.place, self.rows, self.half
        where = jnp.stack([place.z, place.y, self.s]).astype(jnp.int32)
        width, depth = 2 * half, rows * 2 * place.line
        tokens = values.shape[-2]
        shape = (tokens, depth) if back else (count, tokens, width)
        held = pl.BlockSpec(memory_space=pltpu.VMEM)
        given = pl.BlockSpec(memory_space=pl.ANY)
        pieces = (
            list(self.native[first : first + count])
            + [v for h in range(2) for v in self.same[h]]
            + [v for h in range(2) for v in self.across[h]]
            + list(self.near)
        )
        return pl.pallas_call(
            functools.partial(weights_kernel, place.line, first, count, back),
            out_shape=jax.ShapeDtypeStruct(shape, jnp.float32),
            in_specs=[pl.BlockSpec(memory_space=pltpu.SMEM), held] + [given] * len(pieces),
            out_specs=held,
            scratch_shapes=[
                pltpu.VMEM((2, count, depth, half), jnp.bfloat16),
                pltpu.SemaphoreType.DMA((2, count)),
            ],
            compiler_params=pltpu.CompilerParams(vmem_limit_bytes=56 << 20),
            cost_estimate=pl.CostEstimate(
                flops=2 * tokens * depth * width * count // 16,
                bytes_accessed=2 * depth * width * count // 16,
                transcendentals=0,
            ),
        )(where, values, *pieces)


def weights_kernel(line, first, count, back, where, values, *refs):
    native = refs[:count]
    same = (refs[count : count + 4], refs[count + 4 : count + 8])
    across = (refs[count + 8 : count + 12], refs[count + 12 : count + 16])
    near = refs[count + 16 : count + 20]
    out, held, sems = refs[count + 20 :]
    z, y, s = where[0], where[1], where[2]
    rows, width = native[0].shape
    half = width // 2

    def place(h, j, plane, side):
        start = pl.multiple_of(rows * (2 * plane + side), 16)
        return held.at[h, j, pl.ds(start, rows)]

    for h in range(2):
        cols = pl.ds(h * half, half)
        for j in range(count):
            pltpu.make_async_copy(
                native[j].at[:, cols], place(h, j, z, y), sems.at[h, j]
            ).start()
        for r in range(4):
            j = (s ^ r) - first

            @pl.when((j >= 0) & (j < count))
            def _():
                pltpu.make_async_copy(
                    near[r].at[:, cols], place(h, j, z, 1 - y), sems.at[h, j]
                ).start()
                for k in range(1, line):
                    plane = lax.rem(z + k, line)
                    pltpu.make_async_copy(
                        same[h][r].at[k - 1], place(h, j, plane, y), sems.at[h, j]
                    ).start()
                    pltpu.make_async_copy(
                        across[h][r].at[k - 1], place(h, j, plane, 1 - y), sems.at[h, j]
                    ).start()

    if back:
        out[...] = jnp.zeros_like(out)

    def step(i, carry):
        h, j = i // count, lax.rem(i, count)
        cols = pl.ds(pl.multiple_of(h * half, 128), half)
        pltpu.make_async_copy(held.at[h, j], held.at[h, j], sems.at[h, j]).wait()
        if back:
            out[...] += matrix_product_backward(values[j, :, cols], held[h, j])
        else:
            out[j, :, cols] = matrix_product(values[...], held[h, j])
        return carry

    lax.fori_loop(0, 2 * count, step, 0)


HIDDEN_TILE = 256


def quarter_copies(line, z, x, pieces, target, sem):
    planes, rest, mates = pieces
    rows = rest.shape[0]

    def copy(source, plane, side):
        start = pl.multiple_of(rows * (2 * plane + side), 16)
        pltpu.make_async_copy(source, target.at[pl.ds(start, rows)], sem).start()

    for plane in range(line):
        copy(planes.at[plane], plane, x)
    copy(rest, z, 1 - x)
    for k in range(1, line):
        copy(mates.at[k - 1], lax.rem(z + k, line), 1 - x)


def hidden_kernel(line, where, values, choices, down, up, planes, rest, mates, out, reduced, held, sems):
    step = pl.program_id(0)
    tiles = held.shape[0]

    @pl.when(step == 0)
    def _():
        def start(tile, carry):
            cols = pl.ds(pl.multiple_of(tile * HIDDEN_TILE, 128), HIDDEN_TILE)
            pieces = (planes.at[:, :, cols], rest.at[:, cols], mates.at[:, :, cols])
            quarter_copies(line, where[0], where[2], pieces, held.at[tile], sems.at[tile])
            return carry

        lax.fori_loop(0, tiles, start, 0)
        reduced[...] = low(matrix_product(values[...], down[...]) * choices[...])

    pltpu.make_async_copy(held.at[step], held.at[step], sems.at[step]).wait()
    out[...] = matrix_product(values[...], held[step]) + adapter_scale * matrix_product(
        reduced[...], up[...]
    )


def down_copies(line, where, left, right, target, sems):
    planes, rest, mates = left
    z, y, x = where[0], where[1], where[2]
    rows, cut = rest.shape

    def copy(source, plane, side, cols):
        block = 2 * plane + side
        start = pl.multiple_of(rows * block, 16)
        pltpu.make_async_copy(source, target.at[pl.ds(start, rows), cols], sems.at[block]).start()

    first, second = pl.ds(0, cut), pl.ds(cut, target.shape[1] - cut)
    for plane in range(line):
        copy(planes.at[plane], plane, x, first)
        copy(right.at[plane, 0], plane, y, second)
        copy(right.at[plane, 1], plane, 1 - y, second)
    copy(rest, z, 1 - x, first)
    for k in range(1, line):
        copy(mates.at[k - 1], lax.rem(z + k, line), 1 - x, first)


def wait_rows(target, rows, sems, block):
    part = target.at[pl.ds(pl.multiple_of(rows * block, 16), rows)]
    pltpu.make_async_copy(part, part, sems.at[block]).wait()


def feed_forward_back_kernel(
    line, where, gt, up, near, far, down_lower, upper_gate, upper_up, *refs
):
    left, right, gate_pieces, up_pieces = refs[:3], refs[3], refs[4:7], refs[7:10]
    hidden, e_gate, e_up, keep, send, total, down, held, down_sems, sems = refs[10:]
    step = pl.program_id(0)
    tiles, rows = held.shape[1], left[1].shape[0]
    blocks, width = 2 * line, down.shape[1]

    @pl.when(step == 0)
    def _():
        def start(tile, carry):
            cols = pl.ds(pl.multiple_of(tile * HIDDEN_TILE, 128), HIDDEN_TILE)
            for t, (planes, rest, mates) in enumerate((gate_pieces, up_pieces)):
                pieces = (planes.at[:, :, cols], rest.at[:, cols], mates.at[:, :, cols])
                quarter_copies(line, where[0], where[2], pieces, held.at[t, tile], sems.at[t, tile])
            return carry

        start(0, 0)
        down_copies(line, where, left, right, down, down_sems)
        lax.fori_loop(1, tiles, start, 0)
        keep[...] = jnp.zeros_like(keep)
        total[...] = jnp.zeros_like(total)

    seen = 0
    for tile in range(tiles):
        until = -(-(tile + 1) * HIDDEN_TILE // rows)

        @pl.when(step == tile)
        def _(seen=seen, until=until):
            for block in range(seen, until):
                wait_rows(down, rows, down_sems, block)

        seen = until
    for t in range(2):
        pltpu.make_async_copy(held.at[t, step], held.at[t, step], sems.at[t, step]).wait()

    tile_rows = down[pl.ds(pl.multiple_of(step * HIDDEN_TILE, HIDDEN_TILE), HIDDEN_TILE), :]
    count = keep.shape[0]
    for n, (sums, sent) in enumerate(((keep, near), (total, far))):
        own = slice(n * count, (n + 1) * count)
        gate_value, up_value = gt[own, :], up[own, :]
        dh = matrix_product_backward(sent[:, :width], tile_rows) + matrix_product_backward(
            sent[:, width:], down_lower[...]
        )
        sg = jax.nn.sigmoid(gate_value)
        act = gate_value * sg
        h = low(act * up_value)
        grad_gate = low(dh * up_value * (sg + gate_value * sg * (1.0 - sg)))
        grad_up = low(dh * act)
        hidden[own, :], e_gate[own, :], e_up[own, :] = h, grad_gate, grad_up
        sums[:, :width] += matrix_product_backward(
            grad_gate, held[0, step]
        ) + matrix_product_backward(grad_up, held[1, step])
        lanes = [width + k * ADAPTER_COLUMNS for k in range(4)]
        sums[:, lanes[0] : lanes[1]] += matrix_product_backward(grad_gate, upper_gate[...])
        sums[:, lanes[1] : lanes[2]] += matrix_product_backward(grad_up, upper_up[...])
        sums[:, lanes[2] : lanes[3]] += matrix_product(h, down_lower[...])

    @pl.when(step == tiles - 1)
    def _():
        send[...] = low(total[...])


def feed_forward_out_kernel(line, where, hidden, *refs):
    left, right = refs[:3], refs[3]
    keep, send, down, down_sems = refs[4:]
    rows = left[1].shape[0]
    down_copies(line, where, left, right, down, down_sems)
    for block in range(2 * line):
        wait_rows(down, rows, down_sems, block)
    count = keep.shape[0]
    keep[...] = matrix_product(hidden[:count, :], down[...])
    send[...] = low(matrix_product(hidden[count:, :], down[...]))


def small_cost(flops):
    return pl.CostEstimate(flops=flops // 16, bytes_accessed=flops // 8192, transcendentals=0)


class FeedForward:
    def __init__(self, place, left, right):
        self.place, self.left, self.right = place, left, right
        self.cut = left[1].shape[1]
        self.padded = left[1].shape[0]
        self.kernels = self.padded % 64 == 0
        self.where = jnp.stack([place.z, place.y, place.x]).astype(jnp.int32)

    def down(self):
        right = jnp.where(self.place.y == 0, self.right, self.right[:, ::-1])
        right = right.reshape(-1, right.shape[-1])
        return jnp.concatenate([put_quarter(self.place, *self.left), right], axis=1)

    def hidden(self, values, choices, lower, upper, pieces):
        count, width = values.shape[0], upper.shape[1]
        if not self.kernels:
            reduced = low(matrix_product(values, lower) * choices)
            full = put_quarter(self.place, *pieces)
            return matrix_product(values, full) + adapter_scale * matrix_product(
                reduced, upper
            ), reduced
        tiles = width // HIDDEN_TILE
        once = lambda v: pl.BlockSpec(v.shape, lambda i: (0, 0), pipeline_mode=pl.Buffered(1))
        columns = lambda n: pl.BlockSpec((n, HIDDEN_TILE), lambda i: (0, i))
        return pl.pallas_call(
            functools.partial(hidden_kernel, self.place.line),
            grid=(tiles,),
            out_shape=[
                jax.ShapeDtypeStruct((count, width), jnp.float32),
                jax.ShapeDtypeStruct((count, ADAPTER_COLUMNS), jnp.bfloat16),
            ],
            in_specs=[pl.BlockSpec(memory_space=pltpu.SMEM)]
            + [once(v) for v in (values, choices, lower)]
            + [columns(upper.shape[0])]
            + [pl.BlockSpec(memory_space=pl.ANY)] * 3,
            out_specs=[
                columns(count),
                pl.BlockSpec((count, ADAPTER_COLUMNS), lambda i: (0, 0)),
            ],
            scratch_shapes=[
                pltpu.VMEM((tiles, values.shape[1], HIDDEN_TILE), jnp.bfloat16),
                pltpu.SemaphoreType.DMA((tiles,)),
            ],
            compiler_params=pltpu.CompilerParams(vmem_limit_bytes=40 << 20),
            cost_estimate=small_cost(2 * count * width * values.shape[1]),
        )(self.where, values, choices, lower, upper, *pieces)

    def back(self, gt, up, sent, lower, upper_gate, upper_up, gate_pieces, up_pieces):
        count, width = gt.shape
        half = count // 2
        near, far = sent
        model = near.shape[1] - ADAPTER_COLUMNS
        sums = model + 3 * ADAPTER_COLUMNS
        if not self.kernels:
            sent = jnp.concatenate([near, far], axis=0)
            down = self.down()
            gate, up_part = put_quarter(self.place, *gate_pieces), put_quarter(self.place, *up_pieces)
            sg = jax.nn.sigmoid(gt)
            act = gt * sg
            h = low(act * up)
            dh = matrix_product_backward(sent[:, :model], down) + matrix_product_backward(
                sent[:, model:], lower
            )
            e_gate = low(dh * up * (sg + gt * sg * (1.0 - sg)))
            e_up = low(dh * act)
            total = jnp.concatenate(
                [
                    matrix_product_backward(e_gate, gate) + matrix_product_backward(e_up, up_part),
                    matrix_product_backward(e_gate, upper_gate),
                    matrix_product_backward(e_up, upper_up),
                    matrix_product(h, lower),
                ],
                axis=1,
            )
            return h, e_gate, e_up, total[:half], low(total[half:])
        tiles = width // HIDDEN_TILE
        once = lambda shape: pl.BlockSpec(shape, lambda i: (0, 0), pipeline_mode=pl.Buffered(1))
        columns = lambda n: pl.BlockSpec((n, HIDDEN_TILE), lambda i: (0, i))
        pieces = (*self.left, self.right, *gate_pieces, *up_pieces)
        return pl.pallas_call(
            functools.partial(feed_forward_back_kernel, self.place.line),
            grid=(tiles,),
            out_shape=[jax.ShapeDtypeStruct((count, width), jnp.bfloat16)] * 3
            + [
                jax.ShapeDtypeStruct((half, sums), jnp.float32),
                jax.ShapeDtypeStruct((half, sums), jnp.bfloat16),
            ],
            in_specs=[
                pl.BlockSpec(memory_space=pltpu.SMEM),
                columns(count),
                columns(count),
                once(near.shape),
                once(far.shape),
                pl.BlockSpec((HIDDEN_TILE, ADAPTER_COLUMNS), lambda i: (i, 0)),
                columns(ADAPTER_COLUMNS),
                columns(ADAPTER_COLUMNS),
            ]
            + [pl.BlockSpec(memory_space=pl.ANY)] * len(pieces),
            out_specs=[columns(count)] * 3 + [once((half, sums))] * 2,
            scratch_shapes=[
                pltpu.VMEM((half, sums), jnp.float32),
                pltpu.VMEM((width, model), jnp.bfloat16),
                pltpu.VMEM((2, tiles, model, HIDDEN_TILE), jnp.bfloat16),
                pltpu.SemaphoreType.DMA((2 * self.place.line,)),
                pltpu.SemaphoreType.DMA((2, tiles)),
            ],
            compiler_params=pltpu.CompilerParams(vmem_limit_bytes=60 << 20),
            cost_estimate=small_cost(6 * count * width * model),
        )(self.where, gt, up, near, far, lower, upper_gate, upper_up, *pieces)

    def out(self, h, model):
        count, width = h.shape
        half = count // 2
        if not self.kernels:
            total = matrix_product(h, self.down())
            return total[:half], low(total[half:])
        held = pl.BlockSpec(memory_space=pltpu.VMEM)
        return pl.pallas_call(
            functools.partial(feed_forward_out_kernel, self.place.line),
            out_shape=[
                jax.ShapeDtypeStruct((half, model), jnp.float32),
                jax.ShapeDtypeStruct((half, model), jnp.bfloat16),
            ],
            in_specs=[pl.BlockSpec(memory_space=pltpu.SMEM), held]
            + [pl.BlockSpec(memory_space=pl.ANY)] * 4,
            out_specs=[held] * 2,
            scratch_shapes=[
                pltpu.VMEM((width, model), jnp.bfloat16),
                pltpu.SemaphoreType.DMA((2 * self.place.line,)),
            ],
            compiler_params=pltpu.CompilerParams(vmem_limit_bytes=40 << 20),
            cost_estimate=small_cost(64 * count * width * model),
        )(self.where, h, *self.left, self.right)


def columns_kernel(own, padded, quarter, value, *outs):
    each, window = GROUP * own, 2 * padded
    rows, width = value.shape
    step = pl.program_id(0)
    lane = lax.broadcasted_iota(jnp.int32, (rows, window), 1)
    for out, k in zip(outs, (quarter[0], quarter[0] ^ 2)):
        turned = []
        for n in range(2):
            start = each * (2 * step + n) + own * k
            base = jnp.minimum(start // 128, (width - window) // 128) * 128
            piece = value[:, pl.ds(pl.multiple_of(base, 128), window)].astype(jnp.float32)
            turned.append(pltpu.roll(piece, lax.rem(window + n * padded - (start - base), window), 1))
        kept = jnp.where(lane < own, turned[0], 0.0)
        kept = jnp.where((lane >= padded) & (lane < padded + own), turned[1], kept)
        out[...] = low(kept)


def hidden_columns(place, value, blocks, padded):
    rows, width = value.shape
    own = width // (blocks * GROUP)
    if padded % 64 or 2 * padded > width:

        def take(k):
            def cut(given):
                pieces = []
                for i in range(blocks):
                    start = own * (GROUP * i + k)
                    piece = given[:, start : start + own]
                    pieces.append(jnp.pad(piece, ((0, 0), (0, padded - own))))
                return jnp.concatenate(pieces, axis=1)

            return cut

        branches = [take(k) for k in range(GROUP)]
        return [lax.switch(k, branches, value) for k in (place.q, place.q ^ 2)]
    return pl.pallas_call(
        functools.partial(columns_kernel, own, padded),
        grid=(blocks // 2,),
        out_shape=[jax.ShapeDtypeStruct((rows, blocks * padded), value.dtype)] * 2,
        in_specs=[
            pl.BlockSpec(memory_space=pltpu.SMEM),
            pl.BlockSpec((rows, width), lambda i: (0, 0)),
        ],
        out_specs=[pl.BlockSpec((rows, 2 * padded), lambda i: (0, i))] * 2,
        compiler_params=pltpu.CompilerParams(vmem_limit_bytes=32 << 20),
        cost_estimate=pl.CostEstimate(
            flops=8 * rows * width, bytes_accessed=4 * rows * width, transcendentals=0
        ),
    )(place.q.astype(jnp.int32).reshape(1), value)


def hidden_rows(place, value, quarter, blocks, padded):
    own = value.shape[0] // (blocks * GROUP)
    split = value.reshape(blocks, GROUP, own, -1)
    got = lax.dynamic_index_in_dim(split, quarter, 1, keepdims=False)
    return jnp.pad(got, ((0, 0), (0, padded - own), (0, 0))).reshape(blocks * padded, -1)


def spread_kernel(own, padded, quarter, value, out, total):
    rows, width = total.shape
    window = 2 * padded
    total[...] = jnp.zeros_like(total)
    lane = lax.broadcasted_iota(jnp.int32, (rows, window), 1)
    for i in range(width // (GROUP * own)):
        pair, n = i // 2, i % 2
        start = own * (GROUP * i + quarter[0])
        base = jnp.minimum(start // 128, (width - window) // 128) * 128
        piece = value[:, pair * window : (pair + 1) * window].astype(jnp.float32)
        inside = (lane >= n * padded) & (lane < n * padded + own)
        turned = pltpu.roll(
            jnp.where(inside, piece, 0.0),
            lax.rem(window - n * padded + (start - base), window),
            1,
        )
        total[:, pl.ds(pl.multiple_of(base, 128), window)] += turned
    out[...] = low(total[...])


def spread_columns(place, value, width, blocks, padded):
    rows = value.shape[0]
    own = width // (blocks * GROUP)
    if padded % 64 or 2 * padded > width:

        def lay(k):
            def build(given):
                pieces = []
                for i in range(blocks):
                    piece = given[:, padded * i : padded * i + own]
                    pieces.append(jnp.pad(piece, ((0, 0), (own * k, own * (GROUP - 1 - k)))))
                return jnp.concatenate(pieces, axis=1)

            return build

        return lax.switch(place.q, [lay(k) for k in range(GROUP)], value)
    return pl.pallas_call(
        functools.partial(spread_kernel, own, padded),
        out_shape=jax.ShapeDtypeStruct((rows, width), jnp.bfloat16),
        in_specs=[
            pl.BlockSpec(memory_space=pltpu.SMEM),
            pl.BlockSpec(memory_space=pltpu.VMEM),
        ],
        out_specs=pl.BlockSpec(memory_space=pltpu.VMEM),
        scratch_shapes=[pltpu.VMEM((rows, width), jnp.float32)],
        compiler_params=pltpu.CompilerParams(vmem_limit_bytes=32 << 20),
        cost_estimate=pl.CostEstimate(
            flops=8 * rows * width, bytes_accessed=4 * rows * width, transcendentals=0
        ),
    )(place.q.astype(jnp.int32).reshape(1), value)


def both(kept, got):
    return low(kept.astype(jnp.float32) + got.astype(jnp.float32))


def pick(values, index, axis):
    return lax.dynamic_index_in_dim(values, index, axis, keepdims=False)


def gradients_kernel(*refs):
    n1, dz_qkv, z_qkv, e_qkv, o, dz_out, z_out, e_out = refs[:8]
    n2, dz_gate, dz_up, z_down, e_down = refs[8:13]
    parts_given, (flat, turned, staged, sems, part_sems) = refs[13:16], refs[16:]
    lower = [(n1[...], dz_qkv[t]) for t in range(3)]
    lower += [(o[...], dz_out[...]), (n2[...], dz_gate[...]), (n2[...], dz_up[...])]
    upper = [(z_qkv[t], e_qkv[t]) for t in range(3)]
    upper += [(z_out[...], e_out[...]), (z_down[...], e_down[...])]
    rows = staged.shape[1]
    ranks = ADAPTER_COLUMNS
    parts = rows // ranks
    given = parts_given[0].shape[0]
    second = 6 * rows + given
    starts = [rows * k for k in range(6)] + [second + rows * k for k in range(5)]
    places = (6 * rows, second + 5 * rows, second + 5 * rows + given)
    moves = [
        pltpu.make_async_copy(part, flat.at[pl.ds(start, given)], part_sems.at[n])
        for n, (part, start) in enumerate(zip(parts_given, places))
    ]
    for move in moves:
        move.start()
    copies = []
    for k, start in enumerate(starts):
        slot = k % 2
        if k > 1:
            copies[k - 2].wait()
        if k < 6:
            staged[slot] = low(outer_product_sum(*lower[k]))
        else:
            full = adapter_scale * outer_product_sum(*upper[k - 6])
            for j in range(parts):
                turned[pl.ds(j, ranks, parts), :] = full[:, j * ranks : (j + 1) * ranks]
            staged[slot] = low(turned[...])
        copies.append(
            pltpu.make_async_copy(staged.at[slot], flat.at[pl.ds(start, rows)], sems.at[slot])
        )
        copies[k].start()
    copies[-2].wait()
    copies[-1].wait()
    for move in moves:
        move.wait()


def model_gradients(operands, hidden_parts):
    held = pl.BlockSpec(memory_space=pltpu.VMEM)
    apart = pl.BlockSpec(memory_space=pl.ANY)
    rows = 11 * MODEL_WIDTH + sum(part.shape[0] for part in hidden_parts)
    return pl.pallas_call(
        gradients_kernel,
        out_shape=jax.ShapeDtypeStruct((rows, ADAPTER_COLUMNS), jnp.bfloat16),
        in_specs=[held] * len(operands) + [apart] * len(hidden_parts),
        out_specs=apart,
        scratch_shapes=[
            pltpu.VMEM((MODEL_WIDTH, ADAPTER_COLUMNS), jnp.float32),
            pltpu.VMEM((2, MODEL_WIDTH, ADAPTER_COLUMNS), jnp.bfloat16),
            pltpu.SemaphoreType.DMA((2,)),
            pltpu.SemaphoreType.DMA((len(hidden_parts),)),
        ],
        compiler_params=pltpu.CompilerParams(vmem_limit_bytes=40 << 20),
        cost_estimate=pl.CostEstimate(flops=1 << 28, bytes_accessed=1 << 22, transcendentals=0),
    )(*operands, *hidden_parts)


def reduce_over_cores(place, flat, later):
    pairs = place.line * 2 * (place.shard // 2)
    rows = flat.shape[0] // pairs
    half = -(-rows // 16) * 8
    split = flat.reshape(place.line, 2, place.shard // 2, rows, ADAPTER_COLUMNS)
    start = rows - half
    keep = lax.dynamic_slice_in_dim(split, place.c * start, half, 3)
    send = lax.dynamic_slice_in_dim(split, (1 - place.c) * start, half, 3)
    got, later = together(place.by_c(send), later)
    return both(keep, got), later


class OwnerSum:
    def __init__(self, place, total, share):
        self.place, self.share, self.half = place, share, total.shape[3]
        cut = self.half // 16 * 8
        one, two = total[:, :, :, :cut], total[:, :, :, cut:]
        self.kept = (pick(one, place.y, 1), pick(two, place.x, 2))
        self.got = (
            place.by_y(pick(one, 1 - place.y, 1)),
            place.by_x(pick(two, 1 - place.x, 2)),
        )

    def over_chips(self):
        place = self.place
        one, two = both(self.kept[0], self.got[0]), both(self.kept[1], self.got[1])
        got_one = place.by_x(pick(one, 1 - place.x, 1))
        got_two = place.by_y(pick(two, 1 - place.y, 1))
        one, two = both(pick(one, place.x, 1), got_one), both(pick(two, place.y, 1), got_two)
        return jnp.concatenate([one, two], axis=1)

    def over_planes(self, total):
        place = self.place
        got = [
            place.ring_z(pick(total, (place.z + k) % place.line, 0), k)
            for k in range(1, place.line)
        ]
        result = pick(total, place.z, 0).astype(jnp.float32)
        for value in got:
            result = result + value.astype(jnp.float32)
        start = place.c * (self.half - self.share)
        return lax.dynamic_slice_in_dim(result, start, self.share, 0)


def gather_owners(place, own):
    share = own.shape[0]
    half = -(-share // 8) * 8
    start = 2 * share - half
    mate = place.by_c(own)
    head, tail = jnp.where(place.c == 0, own, mate), jnp.where(place.c == 0, mate, own)
    pair = jnp.concatenate([head, tail], axis=0)
    planes = place.all_z(lax.dynamic_slice_in_dim(pair, place.c * start, half, 0))
    cut = half // 16 * 8
    full = jnp.zeros(
        (place.line, 2, place.shard // 2, 2 * share, ADAPTER_COLUMNS), own.dtype
    )
    for part, x_first, at in ((planes[:, :cut], True, 0), (planes[:, cut:], False, cut)):
        x_part, y_part = place.by_x(part), place.by_y(part)
        xy_part = place.by_y(x_part) if x_first else place.by_x(y_part)
        for value, y, x in (
            (part, place.y, place.x),
            (x_part, place.y, 1 - place.x),
            (y_part, 1 - place.y, place.x),
            (xy_part, 1 - place.y, 1 - place.x),
        ):
            for held, c in ((value, place.c), (place.by_c(value), 1 - place.c)):
                where = (0, y, x, c * start + at, 0)
                full = lax.dynamic_update_slice(full, held[:, None, None], where)
    return full.reshape(-1)


def shards(
    dp,
    shard,
    tokens,
    cotangent,
    arrival,
    lengths,
    adapter_set,
    gain_one,
    gain_two,
    w_query,
    w_key,
    w_value,
    w_out,
    w_gate,
    w_up,
    w_down,
    adapters,
    first_moment_running,
    second_moment_running,
):
    place = Place(dp, shard)
    token_order = arrival[0]
    count = token_order.shape[0]
    padded = -(-(FEEDFORWARD_UNITS // (dp * GROUP)) // 16) * 16


    weights = (w_query, w_key, w_value, w_out)
    s, half = place.x * 2 + place.c, MODEL_WIDTH // 2
    cut = MODEL_WIDTH - MODEL_WIDTH // 3
    stacked = jnp.stack(weights)
    mine = lax.dynamic_index_in_dim(stacked, s, 0, keepdims=False)
    first = place.all_z(mine[:, :half])
    second = place.all_z(mine[:, half:])
    near_y = place.by_y(mine)
    table = jnp.concatenate([lengths, adapter_set], axis=1)
    table_y = place.by_y(table)
    own_gate, other_gate = hidden_columns(place, w_gate, dp, padded)
    own_up, other_up = hidden_columns(place, w_up, dp, padded)
    near_y, table_y, other_gate, other_up = together(near_y, table_y, other_gate, other_up)

    near_x = place.by_x(near_y)
    got_gate, got_up = place.by_y(other_gate), place.by_y(other_up)
    near_y_c = place.by_c(near_y)
    tables = jnp.concatenate([table, table_y], axis=0)
    tables_c = place.by_c(tables)
    own_down = hidden_rows(place, w_down, place.q, 1, padded)
    other_down = hidden_rows(place, w_down, place.q ^ 2, 1, padded)
    first, got_gate, got_up, near_x, near_y_c, tables_c, tokens = together(
        first, got_gate, got_up, near_x, near_y_c, tables_c, tokens
    )

    straight = place.y == place.x
    gate_planes = place.all_z(jnp.where(straight, own_gate, got_gate))
    up_planes = place.all_z(jnp.where(straight, own_up, got_up))
    gate_rest, up_rest = (
        jnp.where(straight, got_gate, own_gate),
        jnp.where(straight, got_up, own_up),
    )
    tables = jnp.concatenate([tables, tables_c], axis=0)
    lines = place.other_z(first)
    x0, y0, lines_c = place.by_x(lines), place.by_y(lines), place.by_c(lines)
    near_x_c = place.by_c(near_x)
    arrived_x = lax.all_to_all(tokens, "dp", split_axis=0, concat_axis=0, tiled=True)
    x0, y0, lines_c, near_x_c, second = together(x0, y0, lines_c, near_x_c, second)

    lines2 = place.other_z(second)
    x1, y1, lines2_c = place.by_x(lines2), place.by_y(lines2), place.by_c(lines2)
    x0_c, y0_c = place.by_c(x0), place.by_c(y0)
    x1, y1, lines2_c, x0_c, y0_c, x0, arrived_x = together(
        x1, y1, lines2_c, x0_c, y0_c, x0, arrived_x
    )

    A_model, A_hidden, B_model, B_hidden = restore_structure(adapters)
    B_gate, _ = hidden_columns(place, B_hidden[0], dp, padded)
    B_up, _ = hidden_columns(place, B_hidden[1], dp, padded)
    A_down = hidden_rows(place, A_hidden, place.q, dp, padded)
    choice, allowed, cosine_table, sine_table = block_tables(lengths[0], adapter_set[0])
    choices = jnp.concatenate(
        [block_tables(tables[k, :SEQ_DEV], tables[k, SEQ_DEV:])[0] for k in range(GROUP)], axis=0
    )
    xy0, xy1 = place.by_y(x0), place.by_x(y1)
    x1_c, y1_c = place.by_c(x1), place.by_c(y1)
    xy0, xy1, x1_c, y1_c, B_gate, B_up, A_down, choices, gate_planes, other_down, cotangent = together(
        xy0, xy1, x1_c, y1_c, B_gate, B_up, A_down, choices, gate_planes, other_down, cotangent
    )

    got_down = place.by_y(other_down)
    arrived_cot = lax.all_to_all(cotangent, "dp", split_axis=0, concat_axis=0, tiled=True)
    gate_mates = place.by_x(place.other_z(gate_planes))
    attention = AttentionWeights(
        place,
        weights,
        ((lines, lines_c, x0, x0_c), (lines2, lines2_c, x1, x1_c)),
        ((y0, y0_c, xy0, place.by_c(xy0)), (y1, y1_c, xy1, place.by_c(xy1))),
        (near_y, near_y_c, near_x, near_x_c),
    )
    gain_first = gain_one.astype(jnp.float32)
    gain_second = gain_two.astype(jnp.float32)

    x = arrived_x[token_order].astype(jnp.float32)
    scale_one = rms_scale(x)
    n1 = low(x * scale_one * gain_first)

    z_qkv = low(
        jnp.einsum("nd,tdr->tnr", n1, A_model[:3], preferred_element_type=jnp.float32) * choice
    )
    bias = jnp.where(allowed, 0.0, -jnp.inf)
    lin, got_down = together(attention.times(n1, 0, 3), got_down)
    left_planes = place.all_z(jnp.where(straight, own_down, got_down)[:, :cut])
    left_rest = jnp.where(straight, got_down, own_down)[:, :cut]
    right_planes = place.all_z(jnp.stack([own_down[:, cut:], got_down[:, cut:]]))
    qkv, o = attention_call(
        attention_kernel,
        (
            (lin, 2),
            (z_qkv, None),
            (B_model[:3], 2),
            (cosine_table, None),
            (sine_table, None),
            (bias, None),
        ),
        (((3, count, MODEL_WIDTH), 2), ((count, MODEL_WIDTH), 1)),
    )
    o, up_planes, gate_mates = together(o, up_planes, gate_mates)
    up_mates = place.by_x(place.other_z(up_planes))
    z_out, delta_out = apply_adapter_delta(o, A_model[3], B_model[3], choice)
    m = x + residual_branch_scale * (attention.times(o, 3, 1)[0] + delta_out)
    scale_two = rms_scale(m)
    n2 = low(m * scale_two * gain_second)

    n2_y = place.by_y(n2)
    n2_y, arrived_cot, left_planes, up_mates = together(
        n2_y, arrived_cot, left_planes, up_mates
    )
    left_mates = place.by_x(place.other_z(left_planes))
    g = arrived_cot[token_order].astype(jnp.float32)
    e_down = low(residual_branch_scale * g)
    dz_down = low(adapter_scale * matrix_product_backward(e_down, B_model[4]) * choice)
    sent = jnp.concatenate([e_down, dz_down], axis=1)
    sent_y = place.by_y(sent)
    n2_all = jnp.concatenate([n2, n2_y], axis=0)
    n2_all = jnp.concatenate([n2_all, place.by_c(n2_all)], axis=0)
    gate_pieces = (gate_planes, gate_rest, gate_mates)
    forward = FeedForward(place, (left_planes, left_rest, left_mates), right_planes)
    gt, z_gate = forward.hidden(n2_all, choices, A_model[4], B_gate, gate_pieces)
    up_pieces = (up_planes, up_rest, up_mates)
    up, z_up = forward.hidden(n2_all, choices, A_model[5], B_up, up_pieces)
    gt, up, left_mates, right_planes, sent_y = together(gt, up, left_mates, right_planes, sent_y)
    sent_pair = jnp.concatenate([sent, sent_y], axis=0)
    sent_mate = place.by_c(sent_pair)
    dz_down_all = jnp.concatenate(
        [sent_pair[:, MODEL_WIDTH:], sent_mate[:, MODEL_WIDTH:]], axis=0
    )
    feed = FeedForward(place, (left_planes, left_rest, left_mates), right_planes)
    h, e_gate, e_up, keep, send = feed.back(
        gt, up, (sent_pair, sent_mate), A_down, B_gate, B_up, gate_pieces, up_pieces
    )
    own_sum, other_sum = place.half_sum(keep, send)
    other_sum, h, e_gate, e_up = together(low(other_sum), h, e_gate, e_up)
    got = place.by_y(other_sum)
    y_keep, y_send = feed.out(h, MODEL_WIDTH)
    dA_down = low(outer_product_sum(h, dz_down_all))
    own_hidden = FEEDFORWARD_UNITS // (dp * GROUP)
    dA_hidden = lax.dynamic_update_slice(
        jnp.zeros((dp, GROUP, own_hidden, ADAPTER_COLUMNS), jnp.bfloat16),
        dA_down.reshape(dp, 1, padded, ADAPTER_COLUMNS)[:, :, :own_hidden],
        (0, place.q, 0, 0),
    )
    hidden_parts = [dA_hidden.reshape(-1, ADAPTER_COLUMNS)] + [
        spread_columns(
            place, low(adapter_scale * outer_product_sum(z, e)), FEEDFORWARD_UNITS, dp, padded
        ).reshape(-1, ADAPTER_COLUMNS)
        for z, e in ((z_gate, e_gate), (z_up, e_up))
    ]
    got, y_send, *hidden_parts = together(got, y_send, *hidden_parts)
    back_sum = own_sum + got.astype(jnp.float32)
    y_own, y_other = place.half_sum(y_keep, y_send)
    y_got = place.by_y(low(y_other))
    cuts = [MODEL_WIDTH + k * ADAPTER_COLUMNS for k in range(3)]
    dz_gate, dz_up, z_down = jnp.split(back_sum, cuts, axis=1)[1:]
    dz_gate, dz_up = low(adapter_scale * dz_gate * choice), low(adapter_scale * dz_up * choice)
    z_down = low(z_down * choice)
    dn2 = (
        back_sum[:, :MODEL_WIDTH]
        + matrix_product_backward(dz_gate, A_model[4])
        + matrix_product_backward(dz_up, A_model[5])
    )
    dm = g + norm_back(m, scale_two, gain_second, dn2)
    e_out = low(residual_branch_scale * dm)
    dz_out = low(adapter_scale * matrix_product_backward(e_out, B_model[3]) * choice)
    (e_qkv,) = attention_call(
        attention_back_kernel,
        (
            (qkv, 2),
            (attention.times_transposed(e_out[None], 3, 1), 1),
            (dz_out, None),
            (A_model[3], 0),
            (cosine_table, None),
            (sine_table, None),
            (bias, None),
        ),
        (((3, count, MODEL_WIDTH), 2),),
    )
    e_qkv, y_got = together(e_qkv, y_got)
    y = m + residual_branch_scale * (
        y_own + y_got.astype(jnp.float32) + adapter_scale * matrix_product(z_down, B_model[4])
    )
    inverse = (
        jnp.zeros_like(token_order).at[token_order].set(jnp.arange(count, dtype=jnp.int32))
    )
    dz_qkv = low(
        adapter_scale
        * jnp.einsum("tnd,trd->tnr", e_qkv, B_model[:3], preferred_element_type=jnp.float32)
        * choice
    )
    flat = model_gradients(
        (
            n1,
            dz_qkv,
            z_qkv,
            e_qkv,
            o,
            dz_out,
            z_out,
            e_out,
            n2,
            dz_gate,
            dz_up,
            z_down,
            e_down,
        ),
        hidden_parts,
    )
    share = flat.shape[0] // (dp * shard)
    total, (e_qkv, dz_qkv, y) = reduce_over_cores(place, flat, (e_qkv, dz_qkv, y))
    owner = OwnerSum(place, total, share)
    back_out = lax.all_to_all(low(y)[inverse], "dp", split_axis=0, concat_axis=0, tiled=True)
    dn1 = attention.times_transposed(e_qkv, 0, 3) + jnp.einsum(
        "tnr,tdr->nd", dz_qkv, A_model[:3], preferred_element_type=jnp.float32
    )
    dx = dm + norm_back(x, scale_one, gain_first, dn1)
    owner.got, back_out, dx = together(owner.got, back_out, low(dx))
    total = owner.over_chips()
    total, back_grad = together(
        total, lax.all_to_all(dx[inverse], "dp", split_axis=0, concat_axis=0, tiled=True)
    )
    gradient = owner.over_planes(total)
    offset = lax.axis_index(AXES) * share
    own_params = lax.dynamic_slice_in_dim(
        adapters.reshape(-1, ADAPTER_COLUMNS), offset, share
    ).astype(jnp.float32)
    first = first_moment_running.reshape(share, ADAPTER_COLUMNS)
    second = second_moment_running.reshape(share, ADAPTER_COLUMNS)
    fresh_first = first_decay_rate * first + (1.0 - first_decay_rate) * gradient
    fresh_second = second_decay_rate * second + (1.0 - second_decay_rate) * gradient * gradient
    unbiased_first = fresh_first / (1.0 - first_decay_rate**OPT_STEP)
    unbiased_second = fresh_second / (1.0 - second_decay_rate**OPT_STEP)
    update = (
        unbiased_first / (jnp.sqrt(unbiased_second) + adaptive_epsilon)
        + weight_shrink_rate * own_params
    )
    updated = gather_owners(place, low(own_params - learning_rate * update))

    return (
        back_out,
        back_grad,
        gradient.reshape(-1),
        fresh_first.reshape(-1),
        fresh_second.reshape(-1),
        updated,
    )


def solution(mesh):
    rows = P(AXES, None)
    weight = P("dp", None)
    return jax.shard_map(
        functools.partial(shards, mesh.shape["dp"], mesh.shape["shard"]),
        mesh=mesh,
        in_specs=(rows,) * 5 + (P(), P()) + (weight,) * 7 + (P(), P(AXES), P(AXES)),
        out_specs=(rows, rows, P(AXES), P(AXES), P(AXES), P()),
        check_vma=False,
    )
```

```python
import functools
import math

import jax
import jax.numpy as jnp
from jax import lax
from jax.experimental import pallas as pl
from jax.experimental.pallas import tpu as pltpu
from jax.sharding import PartitionSpec as P

MODEL_WIDTH = 2304
ATTENTION_HEADS = 36
HEAD_SIZE = 64
FEEDFORWARD_UNITS = 5760
ADAPTER_RANK = 16
OPT_STEP = 10
SEQ_DEV = 4
TOK_DEV = 256
ADAPTER_COLUMNS = 128


norm_eps = 1e-05
residual_branch_scale = 1.4 / math.sqrt(40.0)
adapter_scale = 2.0
rope_base = 10000.0
first_decay_rate = 0.9
second_decay_rate = 0.999
adaptive_epsilon = 1e-08
weight_shrink_rate = 0.01
learning_rate = 0.01


def matrix_product(left_side, right_side):
    return jnp.dot(left_side, right_side, preferred_element_type=jnp.float32)


def matrix_product_backward(left_side, right_side):
    return lax.dot_general(
        left_side, right_side, (((1,), (1,)), ((), ())), preferred_element_type=jnp.float32
    )


def outer_product_sum(left_side, right_side):
    return lax.dot_general(
        left_side, right_side, (((0,), (0,)), ((), ())), preferred_element_type=jnp.float32
    )


def low(values):
    return values.astype(jnp.bfloat16)


def block_tables(sequence_lengths, sequence_adapter_index):
    row_ids = jnp.arange(TOK_DEV, dtype=jnp.int32)
    seq_ends = jnp.cumsum(sequence_lengths, dtype=jnp.int32)
    seq_starts = seq_ends - sequence_lengths
    segment = jnp.sum(
        (row_ids[:, None] >= seq_ends[None, :]).astype(jnp.int32), axis=1, dtype=jnp.int32
    )
    member = (segment[:, None] == jnp.arange(SEQ_DEV, dtype=jnp.int32)[None, :]).astype(jnp.int32)
    position = row_ids - jnp.sum(member * seq_starts[None, :], axis=1, dtype=jnp.int32)
    token_adapter_index = jnp.sum(member * sequence_adapter_index[None, :], axis=1, dtype=jnp.int32)
    adapter_choice_index = (
        jnp.arange(ADAPTER_COLUMNS, dtype=jnp.int32)[None, :] // ADAPTER_RANK
        == token_adapter_index[:, None]
    ).astype(jnp.float32)
    allowed = (segment[:, None] == segment[None, :]) & (row_ids[None, :] <= row_ids[:, None])
    half_dim = HEAD_SIZE // 2
    inv_freq = jnp.power(rope_base, -2.0 * jnp.arange(half_dim, dtype=jnp.float32) / HEAD_SIZE)
    angles = position.astype(jnp.float32)[:, None] * inv_freq[None, :]
    cosine, sine = jnp.cos(angles), jnp.sin(angles)
    return (
        adapter_choice_index,
        allowed,
        jnp.concatenate([cosine] * (2 * HEADS_AT_ONCE), axis=1),
        jnp.concatenate([-sine, sine] * HEADS_AT_ONCE, axis=1),
    )


def restore_structure(flattened_vector):
    first_boundary = 6 * MODEL_WIDTH * ADAPTER_COLUMNS
    second_boundary = first_boundary + FEEDFORWARD_UNITS * ADAPTER_COLUMNS
    third_boundary = second_boundary + 5 * ADAPTER_COLUMNS * MODEL_WIDTH
    return (
        flattened_vector[:first_boundary].reshape(6, MODEL_WIDTH, ADAPTER_COLUMNS),
        flattened_vector[first_boundary:second_boundary].reshape(
            FEEDFORWARD_UNITS, ADAPTER_COLUMNS
        ),
        flattened_vector[second_boundary:third_boundary].reshape(5, ADAPTER_COLUMNS, MODEL_WIDTH),
        flattened_vector[third_boundary:].reshape(2, ADAPTER_COLUMNS, FEEDFORWARD_UNITS),
    )


def rms_scale(values):
    return lax.rsqrt(jnp.mean(values * values, axis=-1, keepdims=True) + norm_eps)


def norm_back(values, scale, gain, gradient_value):
    weighted = gradient_value * gain
    return scale * weighted - values * scale**3 * jnp.mean(
        values * weighted, axis=-1, keepdims=True
    )


def apply_adapter_delta(input_rows, adapter_down_pair, adapter_up_pair, adapter_choice_index):
    reduced_total = low(
        matrix_product(input_rows, adapter_down_pair) * adapter_choice_index
    )
    return (reduced_total, adapter_scale * matrix_product(reduced_total, adapter_up_pair))


HEADS_AT_ONCE = 4


def head_masks(shape):
    lane = lax.broadcasted_iota(jnp.int32, shape, 1)
    return [lane // HEAD_SIZE == n for n in range(HEADS_AT_ONCE)]


def join_heads(masks, results):
    joined = results[0]
    for mask, result in zip(masks[1:], results[1:]):
        joined = jnp.where(mask, result, joined)
    return joined


def swap_halves(values):
    lane = lax.broadcasted_iota(jnp.int32, values.shape, 1)
    half, width = HEAD_SIZE // 2, values.shape[1]
    return jnp.where(
        lane % HEAD_SIZE < half, pltpu.roll(values, width - half, 1), pltpu.roll(values, half, 1)
    )


def head_scores(query, key, bias):
    scores = matrix_product_backward(query, key) * HEAD_SIZE ** (-0.5) + bias
    expanded = jnp.exp(scores - jnp.max(scores, axis=-1, keepdims=True))
    return expanded / jnp.sum(expanded, axis=-1, keepdims=True)


def attention_kernel(lin, z, up, cosine, sine, bias, qkv, attended):
    full = [lin[t] + adapter_scale * matrix_product(z[t], up[t]) for t in range(3)]
    query, key = (
        low(v * cosine[...] + swap_halves(v) * sine[...]) for v in full[:2]
    )
    value = low(full[2])
    qkv[0], qkv[1], qkv[2] = query, key, value
    masks = head_masks(query.shape)
    results = []
    for mine in masks:
        probs = head_scores(jnp.where(mine, query, jnp.zeros_like(query)), key, bias[...])
        results.append(matrix_product(low(probs), value))
    attended[...] = low(join_heads(masks, results))


def attention_back_kernel(qkv, lin, dz, down, cosine, sine, bias, grads):
    query, key, value = qkv[0], qkv[1], qkv[2]
    grad = low(lin[...] + matrix_product_backward(dz[...], down[...]))
    masks = head_masks(query.shape)
    nothing = jnp.zeros_like(query)
    results = []
    for mine in masks:
        probs = head_scores(jnp.where(mine, query, nothing), key, bias[...])
        grad_probs = matrix_product_backward(jnp.where(mine, grad, nothing), value)
        row_delta = jnp.sum(probs * grad_probs, axis=-1, keepdims=True)
        grad_scores = low(probs * (grad_probs - row_delta))
        results.append(
            (
                matrix_product(grad_scores, key),
                outer_product_sum(grad_scores, query),
                outer_product_sum(low(probs), grad),
            )
        )
    scale = HEAD_SIZE ** (-0.5)
    grad_query, grad_key, grad_value = (
        join_heads(masks, parts) for parts in zip(*results)
    )
    for t, v in enumerate((grad_query * scale, grad_key * scale)):
        grads[t] = low(v * cosine[...] - swap_halves(v) * sine[...])
    grads[2] = low(grad_value)


def attention_call(kernel, operands, outs):
    pairs = HEADS_AT_ONCE * HEAD_SIZE

    def spec(shape, axis):
        block = tuple(pairs if k == axis else n for k, n in enumerate(shape))
        return pl.BlockSpec(block, lambda i: tuple(i if k == axis else 0 for k in range(len(shape))))

    count = operands[-1][0].shape[0]
    return pl.pallas_call(
        kernel,
        grid=(ATTENTION_HEADS // HEADS_AT_ONCE,),
        out_shape=[jax.ShapeDtypeStruct(shape, jnp.bfloat16) for shape, _ in outs],
        in_specs=[spec(v.shape, axis) for v, axis in operands],
        out_specs=[spec(shape, axis) for shape, axis in outs],
        compiler_params=pltpu.CompilerParams(vmem_limit_bytes=48 << 20),
        cost_estimate=pl.CostEstimate(
            flops=8 * count * count * MODEL_WIDTH // 16,
            bytes_accessed=24 * count * MODEL_WIDTH // 16,
            transcendentals=0,
        ),
    )(*[v for v, _ in operands])


GROUP = 4
AXES = ("dp", "shard")


def together(*values):
    return lax.optimization_barrier(values)


class Place:
    def __init__(self, dp, shard):
        self.line, self.shard = dp // 2, shard
        i, s = lax.axis_index("dp"), lax.axis_index("shard")
        self.z, self.y, self.x, self.c = i // 2, i % 2, s // 2, s % 2
        self.q = self.y * 2 + self.c
        self.spots = [
            (z, y, x, c)
            for z in range(self.line)
            for y in range(2)
            for x in range(shard // 2)
            for c in range(2)
        ]

    def number(self, z, y, x, c):
        return (z * 2 + y) * self.shard + x * 2 + c

    def move(self, value, target):
        pairs = []
        for spot in self.spots:
            to = target(*spot)
            if to is not None:
                pairs.append((self.number(*spot), self.number(*to)))
        return lax.ppermute(value, AXES, pairs)

    def by_y(self, value):
        return self.move(value, lambda z, y, x, c: (z, 1 - y, x, c))

    def by_x(self, value):
        return self.move(value, lambda z, y, x, c: (z, y, 1 - x, c))

    def by_c(self, value):
        return self.move(value, lambda z, y, x, c: (z, y, x, 1 - c))

    def ring_z(self, value, step):
        return self.move(value, lambda z, y, x, c: ((z + step) % self.line, y, x, c))

    def all_z(self, block):
        groups = [[z * 2 + y for z in range(self.line)] for y in range(2)]
        return lax.all_gather(block, "dp", axis=0, axis_index_groups=groups)

    def other_z(self, blocks):
        return jnp.stack(
            [
                lax.dynamic_index_in_dim(blocks, (self.z + k) % self.line, 0, keepdims=False)
                for k in range(1, self.line)
            ]
        )

    def gather_group(self, rows):
        pair = jnp.concatenate([rows, self.by_y(rows)], axis=0)
        return jnp.concatenate([pair, self.by_c(pair)], axis=0)

    def half_sum(self, keep, send):
        return (keep + self.by_c(send).astype(jnp.float32)).reshape(2, -1, keep.shape[1])


def put(buffer, block, *where):
    block = block.reshape((1,) * len(where) + block.shape)
    return lax.dynamic_update_slice(
        buffer, block, tuple(where) + (0,) * (buffer.ndim - len(where))
    )


def put_quarter(place, planes, rest, mates):
    full = jnp.zeros((place.line, 2) + rest.shape, rest.dtype)
    full = lax.dynamic_update_slice(full, planes[:, None], (0, place.x) + (0,) * rest.ndim)
    full = put(full, rest, place.z, 1 - place.x)
    for k in range(1, place.line):
        full = put(full, mates[k - 1], (place.z + k) % place.line, 1 - place.x)
    return full.reshape((-1,) + rest.shape[1:])


class AttentionWeights:
    def __init__(self, place, weights, same, across, near):
        self.place, self.native = place, weights
        self.same, self.across, self.near = same, across, near
        self.s = place.x * 2 + place.c
        self.rows, self.half = weights[0].shape[0], weights[0].shape[1] // 2

    def full(self, t):
        place = self.place
        halves = []
        for h in range(2):
            cols = slice(h * self.half, (h + 1) * self.half)
            buffer = jnp.zeros((place.line, 2, self.rows, self.half), self.native[t].dtype)
            buffer = put(buffer, self.native[t][:, cols], place.z, place.y)
            for r in range(4):
                near = self.near[r][:, cols]
                with_r = put(buffer, near, place.z, 1 - place.y)
                for k in range(1, place.line):
                    plane = (place.z + k) % place.line
                    with_r = put(with_r, self.same[h][r][k - 1], plane, place.y)
                    with_r = put(with_r, self.across[h][r][k - 1], plane, 1 - place.y)
                buffer = jnp.where(self.s ^ r == t, with_r, buffer)
            halves.append(buffer.reshape(-1, self.half))
        return jnp.concatenate(halves, axis=1)

    def times(self, values, first, count):
        if self.rows % 16:
            return jnp.stack([matrix_product(values, self.full(first + j)) for j in range(count)])
        return self.call(values, first, count, False)

    def times_transposed(self, values, first, count):
        if self.rows % 16:
            return sum(
                matrix_product_backward(values[j], self.full(first + j)) for j in range(count)
            )
        return self.call(values, first, count, True)

    def call(self, values, first, count, back):
        place, rows, half = self.place, self.rows, self.half
        where = jnp.stack([place.z, place.y, self.s]).astype(jnp.int32)
        width, depth = 2 * half, rows * 2 * place.line
        tokens = values.shape[-2]
        shape = (tokens, depth) if back else (count, tokens, width)
        held = pl.BlockSpec(memory_space=pltpu.VMEM)
        given = pl.BlockSpec(memory_space=pl.ANY)
        pieces = (
            list(self.native[first : first + count])
            + [v for h in range(2) for v in self.same[h]]
            + [v for h in range(2) for v in self.across[h]]
            + list(self.near)
        )
        return pl.pallas_call(
            functools.partial(weights_kernel, place.line, first, count, back),
            out_shape=jax.ShapeDtypeStruct(shape, jnp.float32),
            in_specs=[pl.BlockSpec(memory_space=pltpu.SMEM), held] + [given] * len(pieces),
            out_specs=held,
            scratch_shapes=[
                pltpu.VMEM((2, count, depth, half), jnp.bfloat16),
                pltpu.SemaphoreType.DMA((2, count)),
            ],
            compiler_params=pltpu.CompilerParams(vmem_limit_bytes=56 << 20),
            cost_estimate=pl.CostEstimate(
                flops=2 * tokens * depth * width * count // 16,
                bytes_accessed=2 * depth * width * count // 16,
                transcendentals=0,
            ),
        )(where, values, *pieces)


def weights_kernel(line, first, count, back, where, values, *refs):
    native = refs[:count]
    same = (refs[count : count + 4], refs[count + 4 : count + 8])
    across = (refs[count + 8 : count + 12], refs[count + 12 : count + 16])
    near = refs[count + 16 : count + 20]
    out, held, sems = refs[count + 20 :]
    z, y, s = where[0], where[1], where[2]
    rows, width = native[0].shape
    half = width // 2

    def place(h, j, plane, side):
        start = pl.multiple_of(rows * (2 * plane + side), 16)
        return held.at[h, j, pl.ds(start, rows)]

    for h in range(2):
        cols = pl.ds(h * half, half)
        for j in range(count):
            pltpu.make_async_copy(
                native[j].at[:, cols], place(h, j, z, y), sems.at[h, j]
            ).start()
        for r in range(4):
            j = (s ^ r) - first

            @pl.when((j >= 0) & (j < count))
            def _():
                pltpu.make_async_copy(
                    near[r].at[:, cols], place(h, j, z, 1 - y), sems.at[h, j]
                ).start()
                for k in range(1, line):
                    plane = lax.rem(z + k, line)
                    pltpu.make_async_copy(
                        same[h][r].at[k - 1], place(h, j, plane, y), sems.at[h, j]
                    ).start()
                    pltpu.make_async_copy(
                        across[h][r].at[k - 1], place(h, j, plane, 1 - y), sems.at[h, j]
                    ).start()

    if back:
        out[...] = jnp.zeros_like(out)

    def step(i, carry):
        h, j = i // count, lax.rem(i, count)
        cols = pl.ds(pl.multiple_of(h * half, 128), half)
        pltpu.make_async_copy(held.at[h, j], held.at[h, j], sems.at[h, j]).wait()
        if back:
            out[...] += matrix_product_backward(values[j, :, cols], held[h, j])
        else:
            out[j, :, cols] = matrix_product(values[...], held[h, j])
        return carry

    lax.fori_loop(0, 2 * count, step, 0)


HIDDEN_TILE = 256


def quarter_copies(line, z, x, pieces, target, sem):
    planes, rest, mates = pieces
    rows = rest.shape[0]

    def copy(source, plane, side):
        start = pl.multiple_of(rows * (2 * plane + side), 16)
        pltpu.make_async_copy(source, target.at[pl.ds(start, rows)], sem).start()

    for plane in range(line):
        copy(planes.at[plane], plane, x)
    copy(rest, z, 1 - x)
    for k in range(1, line):
        copy(mates.at[k - 1], lax.rem(z + k, line), 1 - x)


def hidden_kernel(line, where, values, choices, down, up, planes, rest, mates, out, reduced, held, sems):
    step = pl.program_id(0)
    tiles = held.shape[0]

    @pl.when(step == 0)
    def _():
        def start(tile, carry):
            cols = pl.ds(pl.multiple_of(tile * HIDDEN_TILE, 128), HIDDEN_TILE)
            pieces = (planes.at[:, :, cols], rest.at[:, cols], mates.at[:, :, cols])
            quarter_copies(line, where[0], where[2], pieces, held.at[tile], sems.at[tile])
            return carry

        lax.fori_loop(0, tiles, start, 0)
        reduced[...] = low(matrix_product(values[...], down[...]) * choices[...])

    pltpu.make_async_copy(held.at[step], held.at[step], sems.at[step]).wait()
    out[...] = matrix_product(values[...], held[step]) + adapter_scale * matrix_product(
        reduced[...], up[...]
    )


def down_copies(line, where, left, right, target, sems):
    planes, rest, mates = left
    z, y, x = where[0], where[1], where[2]
    rows, cut = rest.shape

    def copy(source, plane, side, cols):
        block = 2 * plane + side
        start = pl.multiple_of(rows * block, 16)
        pltpu.make_async_copy(source, target.at[pl.ds(start, rows), cols], sems.at[block]).start()

    first, second = pl.ds(0, cut), pl.ds(cut, target.shape[1] - cut)
    for plane in range(line):
        copy(planes.at[plane], plane, x, first)
        copy(right.at[plane, 0], plane, y, second)
        copy(right.at[plane, 1], plane, 1 - y, second)
    copy(rest, z, 1 - x, first)
    for k in range(1, line):
        copy(mates.at[k - 1], lax.rem(z + k, line), 1 - x, first)


def wait_rows(target, rows, sems, block):
    part = target.at[pl.ds(pl.multiple_of(rows * block, 16), rows)]
    pltpu.make_async_copy(part, part, sems.at[block]).wait()


def feed_forward_back_kernel(
    line, where, gt, up, near, far, down_lower, upper_gate, upper_up, *refs
):
    left, right, gate_pieces, up_pieces = refs[:3], refs[3], refs[4:7], refs[7:10]
    hidden, e_gate, e_up, keep, send, total, down, held, down_sems, sems = refs[10:]
    step = pl.program_id(0)
    tiles, rows = held.shape[1], left[1].shape[0]
    blocks, width = 2 * line, down.shape[1]

    @pl.when(step == 0)
    def _():
        def start(tile, carry):
            cols = pl.ds(pl.multiple_of(tile * HIDDEN_TILE, 128), HIDDEN_TILE)
            for t, (planes, rest, mates) in enumerate((gate_pieces, up_pieces)):
                pieces = (planes.at[:, :, cols], rest.at[:, cols], mates.at[:, :, cols])
                quarter_copies(line, where[0], where[2], pieces, held.at[t, tile], sems.at[t, tile])
            return carry

        start(0, 0)
        down_copies(line, where, left, right, down, down_sems)
        lax.fori_loop(1, tiles, start, 0)
        keep[...] = jnp.zeros_like(keep)
        total[...] = jnp.zeros_like(total)

    seen = 0
    for tile in range(tiles):
        until = -(-(tile + 1) * HIDDEN_TILE // rows)

        @pl.when(step == tile)
        def _(seen=seen, until=until):
            for block in range(seen, until):
                wait_rows(down, rows, down_sems, block)

        seen = until
    for t in range(2):
        pltpu.make_async_copy(held.at[t, step], held.at[t, step], sems.at[t, step]).wait()

    tile_rows = down[pl.ds(pl.multiple_of(step * HIDDEN_TILE, HIDDEN_TILE), HIDDEN_TILE), :]
    count = keep.shape[0]
    for n, (sums, sent) in enumerate(((keep, near), (total, far))):
        own = slice(n * count, (n + 1) * count)
        gate_value, up_value = gt[own, :], up[own, :]
        dh = matrix_product_backward(sent[:, :width], tile_rows) + matrix_product_backward(
            sent[:, width:], down_lower[...]
        )
        sg = jax.nn.sigmoid(gate_value)
        act = gate_value * sg
        h = low(act * up_value)
        grad_gate = low(dh * up_value * (sg + gate_value * sg * (1.0 - sg)))
        grad_up = low(dh * act)
        hidden[own, :], e_gate[own, :], e_up[own, :] = h, grad_gate, grad_up
        sums[:, :width] += matrix_product_backward(
            grad_gate, held[0, step]
        ) + matrix_product_backward(grad_up, held[1, step])
        lanes = [width + k * ADAPTER_COLUMNS for k in range(4)]
        sums[:, lanes[0] : lanes[1]] += matrix_product_backward(grad_gate, upper_gate[...])
        sums[:, lanes[1] : lanes[2]] += matrix_product_backward(grad_up, upper_up[...])
        sums[:, lanes[2] : lanes[3]] += matrix_product(h, down_lower[...])

    @pl.when(step == tiles - 1)
    def _():
        send[...] = low(total[...])


def feed_forward_out_kernel(line, where, hidden, *refs):
    left, right = refs[:3], refs[3]
    keep, send, down, down_sems = refs[4:]
    rows = left[1].shape[0]
    down_copies(line, where, left, right, down, down_sems)
    for block in range(2 * line):
        wait_rows(down, rows, down_sems, block)
    count = keep.shape[0]
    keep[...] = matrix_product(hidden[:count, :], down[...])
    send[...] = low(matrix_product(hidden[count:, :], down[...]))


def small_cost(flops):
    return pl.CostEstimate(flops=flops // 16, bytes_accessed=flops // 8192, transcendentals=0)


class FeedForward:
    def __init__(self, place, left, right):
        self.place, self.left, self.right = place, left, right
        self.cut = left[1].shape[1]
        self.padded = left[1].shape[0]
        self.kernels = self.padded % 64 == 0
        self.where = jnp.stack([place.z, place.y, place.x]).astype(jnp.int32)

    def down(self):
        right = jnp.where(self.place.y == 0, self.right, self.right[:, ::-1])
        right = right.reshape(-1, right.shape[-1])
        return jnp.concatenate([put_quarter(self.place, *self.left), right], axis=1)

    def hidden(self, values, choices, lower, upper, pieces):
        count, width = values.shape[0], upper.shape[1]
        if not self.kernels:
            reduced = low(matrix_product(values, lower) * choices)
            full = put_quarter(self.place, *pieces)
            return matrix_product(values, full) + adapter_scale * matrix_product(
                reduced, upper
            ), reduced
        tiles = width // HIDDEN_TILE
        once = lambda v: pl.BlockSpec(v.shape, lambda i: (0, 0), pipeline_mode=pl.Buffered(1))
        columns = lambda n: pl.BlockSpec((n, HIDDEN_TILE), lambda i: (0, i))
        return pl.pallas_call(
            functools.partial(hidden_kernel, self.place.line),
            grid=(tiles,),
            out_shape=[
                jax.ShapeDtypeStruct((count, width), jnp.float32),
                jax.ShapeDtypeStruct((count, ADAPTER_COLUMNS), jnp.bfloat16),
            ],
            in_specs=[pl.BlockSpec(memory_space=pltpu.SMEM)]
            + [once(v) for v in (values, choices, lower)]
            + [columns(upper.shape[0])]
            + [pl.BlockSpec(memory_space=pl.ANY)] * 3,
            out_specs=[
                columns(count),
                pl.BlockSpec((count, ADAPTER_COLUMNS), lambda i: (0, 0)),
            ],
            scratch_shapes=[
                pltpu.VMEM((tiles, values.shape[1], HIDDEN_TILE), jnp.bfloat16),
                pltpu.SemaphoreType.DMA((tiles,)),
            ],
            compiler_params=pltpu.CompilerParams(vmem_limit_bytes=40 << 20),
            cost_estimate=small_cost(2 * count * width * values.shape[1]),
        )(self.where, values, choices, lower, upper, *pieces)

    def back(self, gt, up, sent, lower, upper_gate, upper_up, gate_pieces, up_pieces):
        count, width = gt.shape
        half = count // 2
        near, far = sent
        model = near.shape[1] - ADAPTER_COLUMNS
        sums = model + 3 * ADAPTER_COLUMNS
        if not self.kernels:
            sent = jnp.concatenate([near, far], axis=0)
            down = self.down()
            gate, up_part = put_quarter(self.place, *gate_pieces), put_quarter(self.place, *up_pieces)
            sg = jax.nn.sigmoid(gt)
            act = gt * sg
            h = low(act * up)
            dh = matrix_product_backward(sent[:, :model], down) + matrix_product_backward(
                sent[:, model:], lower
            )
            e_gate = low(dh * up * (sg + gt * sg * (1.0 - sg)))
            e_up = low(dh * act)
            total = jnp.concatenate(
                [
                    matrix_product_backward(e_gate, gate) + matrix_product_backward(e_up, up_part),
                    matrix_product_backward(e_gate, upper_gate),
                    matrix_product_backward(e_up, upper_up),
                    matrix_product(h, lower),
                ],
                axis=1,
            )
            return h, e_gate, e_up, total[:half], low(total[half:])
        tiles = width // HIDDEN_TILE
        once = lambda shape: pl.BlockSpec(shape, lambda i: (0, 0), pipeline_mode=pl.Buffered(1))
        columns = lambda n: pl.BlockSpec((n, HIDDEN_TILE), lambda i: (0, i))
        pieces = (*self.left, self.right, *gate_pieces, *up_pieces)
        return pl.pallas_call(
            functools.partial(feed_forward_back_kernel, self.place.line),
            grid=(tiles,),
            out_shape=[jax.ShapeDtypeStruct((count, width), jnp.bfloat16)] * 3
            + [
                jax.ShapeDtypeStruct((half, sums), jnp.float32),
                jax.ShapeDtypeStruct((half, sums), jnp.bfloat16),
            ],
            in_specs=[
                pl.BlockSpec(memory_space=pltpu.SMEM),
                columns(count),
                columns(count),
                once(near.shape),
                once(far.shape),
                pl.BlockSpec((HIDDEN_TILE, ADAPTER_COLUMNS), lambda i: (i, 0)),
                columns(ADAPTER_COLUMNS),
                columns(ADAPTER_COLUMNS),
            ]
            + [pl.BlockSpec(memory_space=pl.ANY)] * len(pieces),
            out_specs=[columns(count)] * 3 + [once((half, sums))] * 2,
            scratch_shapes=[
                pltpu.VMEM((half, sums), jnp.float32),
                pltpu.VMEM((width, model), jnp.bfloat16),
                pltpu.VMEM((2, tiles, model, HIDDEN_TILE), jnp.bfloat16),
                pltpu.SemaphoreType.DMA((2 * self.place.line,)),
                pltpu.SemaphoreType.DMA((2, tiles)),
            ],
            compiler_params=pltpu.CompilerParams(vmem_limit_bytes=60 << 20),
            cost_estimate=small_cost(6 * count * width * model),
        )(self.where, gt, up, near, far, lower, upper_gate, upper_up, *pieces)

    def out(self, h, model):
        count, width = h.shape
        half = count // 2
        if not self.kernels:
            total = matrix_product(h, self.down())
            return total[:half], low(total[half:])
        held = pl.BlockSpec(memory_space=pltpu.VMEM)
        return pl.pallas_call(
            functools.partial(feed_forward_out_kernel, self.place.line),
            out_shape=[
                jax.ShapeDtypeStruct((half, model), jnp.float32),
                jax.ShapeDtypeStruct((half, model), jnp.bfloat16),
            ],
            in_specs=[pl.BlockSpec(memory_space=pltpu.SMEM), held]
            + [pl.BlockSpec(memory_space=pl.ANY)] * 4,
            out_specs=[held] * 2,
            scratch_shapes=[
                pltpu.VMEM((width, model), jnp.bfloat16),
                pltpu.SemaphoreType.DMA((2 * self.place.line,)),
            ],
            compiler_params=pltpu.CompilerParams(vmem_limit_bytes=40 << 20),
            cost_estimate=small_cost(64 * count * width * model),
        )(self.where, h, *self.left, self.right)


def columns_kernel(own, padded, quarter, value, *outs):
    each, window = GROUP * own, 2 * padded
    rows, width = value.shape
    step = pl.program_id(0)
    lane = lax.broadcasted_iota(jnp.int32, (rows, window), 1)
    for out, k in zip(outs, (quarter[0], quarter[0] ^ 2)):
        turned = []
        for n in range(2):
            start = each * (2 * step + n) + own * k
            base = jnp.minimum(start // 128, (width - window) // 128) * 128
            piece = value[:, pl.ds(pl.multiple_of(base, 128), window)].astype(jnp.float32)
            turned.append(pltpu.roll(piece, lax.rem(window + n * padded - (start - base), window), 1))
        kept = jnp.where(lane < own, turned[0], 0.0)
        kept = jnp.where((lane >= padded) & (lane < padded + own), turned[1], kept)
        out[...] = low(kept)


def hidden_columns(place, value, blocks, padded):
    rows, width = value.shape
    own = width // (blocks * GROUP)
    if padded % 64 or 2 * padded > width:

        def take(k):
            def cut(given):
                pieces = []
                for i in range(blocks):
                    start = own * (GROUP * i + k)
                    piece = given[:, start : start + own]
                    pieces.append(jnp.pad(piece, ((0, 0), (0, padded - own))))
                return jnp.concatenate(pieces, axis=1)

            return cut

        branches = [take(k) for k in range(GROUP)]
        return [lax.switch(k, branches, value) for k in (place.q, place.q ^ 2)]
    return pl.pallas_call(
        functools.partial(columns_kernel, own, padded),
        grid=(blocks // 2,),
        out_shape=[jax.ShapeDtypeStruct((rows, blocks * padded), value.dtype)] * 2,
        in_specs=[
            pl.BlockSpec(memory_space=pltpu.SMEM),
            pl.BlockSpec((rows, width), lambda i: (0, 0)),
        ],
        out_specs=[pl.BlockSpec((rows, 2 * padded), lambda i: (0, i))] * 2,
        compiler_params=pltpu.CompilerParams(vmem_limit_bytes=32 << 20),
        cost_estimate=pl.CostEstimate(
            flops=8 * rows * width, bytes_accessed=4 * rows * width, transcendentals=0
        ),
    )(place.q.astype(jnp.int32).reshape(1), value)


def hidden_rows(place, value, quarter, blocks, padded):
    own = value.shape[0] // (blocks * GROUP)
    split = value.reshape(blocks, GROUP, own, -1)
    got = lax.dynamic_index_in_dim(split, quarter, 1, keepdims=False)
    return jnp.pad(got, ((0, 0), (0, padded - own), (0, 0))).reshape(blocks * padded, -1)


def spread_kernel(own, padded, quarter, value, out, total):
    rows, width = total.shape
    window = 2 * padded
    total[...] = jnp.zeros_like(total)
    lane = lax.broadcasted_iota(jnp.int32, (rows, window), 1)
    for i in range(width // (GROUP * own)):
        pair, n = i // 2, i % 2
        start = own * (GROUP * i + quarter[0])
        base = jnp.minimum(start // 128, (width - window) // 128) * 128
        piece = value[:, pair * window : (pair + 1) * window].astype(jnp.float32)
        inside = (lane >= n * padded) & (lane < n * padded + own)
        turned = pltpu.roll(
            jnp.where(inside, piece, 0.0),
            lax.rem(window - n * padded + (start - base), window),
            1,
        )
        total[:, pl.ds(pl.multiple_of(base, 128), window)] += turned
    out[...] = low(total[...])


def spread_columns(place, value, width, blocks, padded):
    rows = value.shape[0]
    own = width // (blocks * GROUP)
    if padded % 64 or 2 * padded > width:

        def lay(k):
            def build(given):
                pieces = []
                for i in range(blocks):
                    piece = given[:, padded * i : padded * i + own]
                    pieces.append(jnp.pad(piece, ((0, 0), (own * k, own * (GROUP - 1 - k)))))
                return jnp.concatenate(pieces, axis=1)

            return build

        return lax.switch(place.q, [lay(k) for k in range(GROUP)], value)
    return pl.pallas_call(
        functools.partial(spread_kernel, own, padded),
        out_shape=jax.ShapeDtypeStruct((rows, width), jnp.bfloat16),
        in_specs=[
            pl.BlockSpec(memory_space=pltpu.SMEM),
            pl.BlockSpec(memory_space=pltpu.VMEM),
        ],
        out_specs=pl.BlockSpec(memory_space=pltpu.VMEM),
        scratch_shapes=[pltpu.VMEM((rows, width), jnp.float32)],
        compiler_params=pltpu.CompilerParams(vmem_limit_bytes=32 << 20),
        cost_estimate=pl.CostEstimate(
            flops=8 * rows * width, bytes_accessed=4 * rows * width, transcendentals=0
        ),
    )(place.q.astype(jnp.int32).reshape(1), value)


def both(kept, got):
    return low(kept.astype(jnp.float32) + got.astype(jnp.float32))


def pick(values, index, axis):
    return lax.dynamic_index_in_dim(values, index, axis, keepdims=False)


def gradients_kernel(*refs):
    n1, dz_qkv, z_qkv, e_qkv, o, dz_out, z_out, e_out = refs[:8]
    n2, dz_gate, dz_up, z_down, e_down = refs[8:13]
    parts_given, (flat, turned, staged, sems, part_sems) = refs[13:16], refs[16:]
    lower = [(n1[...], dz_qkv[t]) for t in range(3)]
    lower += [(o[...], dz_out[...]), (n2[...], dz_gate[...]), (n2[...], dz_up[...])]
    upper = [(z_qkv[t], e_qkv[t]) for t in range(3)]
    upper += [(z_out[...], e_out[...]), (z_down[...], e_down[...])]
    rows = staged.shape[1]
    ranks = ADAPTER_COLUMNS
    parts = rows // ranks
    given = parts_given[0].shape[0]
    second = 6 * rows + given
    starts = [rows * k for k in range(6)] + [second + rows * k for k in range(5)]
    places = (6 * rows, second + 5 * rows, second + 5 * rows + given)
    moves = [
        pltpu.make_async_copy(part, flat.at[pl.ds(start, given)], part_sems.at[n])
        for n, (part, start) in enumerate(zip(parts_given, places))
    ]
    for move in moves:
        move.start()
    copies = []
    for k, start in enumerate(starts):
        slot = k % 2
        if k > 1:
            copies[k - 2].wait()
        if k < 6:
            staged[slot] = low(outer_product_sum(*lower[k]))
        else:
            full = adapter_scale * outer_product_sum(*upper[k - 6])
            for j in range(parts):
                turned[pl.ds(j, ranks, parts), :] = full[:, j * ranks : (j + 1) * ranks]
            staged[slot] = low(turned[...])
        copies.append(
            pltpu.make_async_copy(staged.at[slot], flat.at[pl.ds(start, rows)], sems.at[slot])
        )
        copies[k].start()
    copies[-2].wait()
    copies[-1].wait()
    for move in moves:
        move.wait()


def model_gradients(operands, hidden_parts):
    held = pl.BlockSpec(memory_space=pltpu.VMEM)
    apart = pl.BlockSpec(memory_space=pl.ANY)
    rows = 11 * MODEL_WIDTH + sum(part.shape[0] for part in hidden_parts)
    return pl.pallas_call(
        gradients_kernel,
        out_shape=jax.ShapeDtypeStruct((rows, ADAPTER_COLUMNS), jnp.bfloat16),
        in_specs=[held] * len(operands) + [apart] * len(hidden_parts),
        out_specs=apart,
        scratch_shapes=[
            pltpu.VMEM((MODEL_WIDTH, ADAPTER_COLUMNS), jnp.float32),
            pltpu.VMEM((2, MODEL_WIDTH, ADAPTER_COLUMNS), jnp.bfloat16),
            pltpu.SemaphoreType.DMA((2,)),
            pltpu.SemaphoreType.DMA((len(hidden_parts),)),
        ],
        compiler_params=pltpu.CompilerParams(vmem_limit_bytes=40 << 20),
        cost_estimate=pl.CostEstimate(flops=1 << 28, bytes_accessed=1 << 22, transcendentals=0),
    )(*operands, *hidden_parts)


def reduce_over_cores(place, flat, later):
    pairs = place.line * 2 * (place.shard // 2)
    rows = flat.shape[0] // pairs
    half = -(-rows // 16) * 8
    split = flat.reshape(place.line, 2, place.shard // 2, rows, ADAPTER_COLUMNS)
    start = rows - half
    keep = lax.dynamic_slice_in_dim(split, place.c * start, half, 3)
    send = lax.dynamic_slice_in_dim(split, (1 - place.c) * start, half, 3)
    got, later = together(place.by_c(send), later)
    return both(keep, got), later


class OwnerSum:
    def __init__(self, place, total, share):
        self.place, self.share, self.half = place, share, total.shape[3]
        cut = self.half // 16 * 8
        one, two = total[:, :, :, :cut], total[:, :, :, cut:]
        self.kept = (pick(one, place.y, 1), pick(two, place.x, 2))
        self.got = (
            place.by_y(pick(one, 1 - place.y, 1)),
            place.by_x(pick(two, 1 - place.x, 2)),
        )

    def over_chips(self):
        place = self.place
        one, two = both(self.kept[0], self.got[0]), both(self.kept[1], self.got[1])
        got_one = place.by_x(pick(one, 1 - place.x, 1))
        got_two = place.by_y(pick(two, 1 - place.y, 1))
        one, two = both(pick(one, place.x, 1), got_one), both(pick(two, place.y, 1), got_two)
        return jnp.concatenate([one, two], axis=1)

    def over_planes(self, total):
        place = self.place
        got = [
            place.ring_z(pick(total, (place.z + k) % place.line, 0), k)
            for k in range(1, place.line)
        ]
        result = pick(total, place.z, 0).astype(jnp.float32)
        for value in got:
            result = result + value.astype(jnp.float32)
        start = place.c * (self.half - self.share)
        return lax.dynamic_slice_in_dim(result, start, self.share, 0)


def gather_owners(place, own):
    share = own.shape[0]
    half = -(-share // 8) * 8
    start = 2 * share - half
    mate = place.by_c(own)
    head, tail = jnp.where(place.c == 0, own, mate), jnp.where(place.c == 0, mate, own)
    pair = jnp.concatenate([head, tail], axis=0)
    planes = place.all_z(lax.dynamic_slice_in_dim(pair, place.c * start, half, 0))
    cut = half // 16 * 8
    full = jnp.zeros(
        (place.line, 2, place.shard // 2, 2 * share, ADAPTER_COLUMNS), own.dtype
    )
    for part, x_first, at in ((planes[:, :cut], True, 0), (planes[:, cut:], False, cut)):
        x_part, y_part = place.by_x(part), place.by_y(part)
        xy_part = place.by_y(x_part) if x_first else place.by_x(y_part)
        for value, y, x in (
            (part, place.y, place.x),
            (x_part, place.y, 1 - place.x),
            (y_part, 1 - place.y, place.x),
            (xy_part, 1 - place.y, 1 - place.x),
        ):
            for held, c in ((value, place.c), (place.by_c(value), 1 - place.c)):
                where = (0, y, x, c * start + at, 0)
                full = lax.dynamic_update_slice(full, held[:, None, None], where)
    return full.reshape(-1)


def shards(
    dp,
    shard,
    tokens,
    cotangent,
    arrival,
    lengths,
    adapter_set,
    gain_one,
    gain_two,
    w_query,
    w_key,
    w_value,
    w_out,
    w_gate,
    w_up,
    w_down,
    adapters,
    first_moment_running,
    second_moment_running,
):
    place = Place(dp, shard)
    token_order = arrival[0]
    count = token_order.shape[0]
    padded = -(-(FEEDFORWARD_UNITS // (dp * GROUP)) // 16) * 16


    weights = (w_query, w_key, w_value, w_out)
    s, half = place.x * 2 + place.c, MODEL_WIDTH // 2
    cut = MODEL_WIDTH - MODEL_WIDTH // 3
    stacked = jnp.stack(weights)
    mine = lax.dynamic_index_in_dim(stacked, s, 0, keepdims=False)
    first = place.all_z(mine[:, :half])
    second = place.all_z(mine[:, half:])
    near_y = place.by_y(mine)
    table = jnp.concatenate([lengths, adapter_set], axis=1)
    table_y = place.by_y(table)
    own_gate, other_gate = hidden_columns(place, w_gate, dp, padded)
    own_up, other_up = hidden_columns(place, w_up, dp, padded)
    near_y, table_y, other_gate, other_up = together(near_y, table_y, other_gate, other_up)

    near_x = place.by_x(near_y)
    got_gate, got_up = place.by_y(other_gate), place.by_y(other_up)
    near_y_c = place.by_c(near_y)
    tables = jnp.concatenate([table, table_y], axis=0)
    tables_c = place.by_c(tables)
    own_down = hidden_rows(place, w_down, place.q, 1, padded)
    other_down = hidden_rows(place, w_down, place.q ^ 2, 1, padded)
    first, got_gate, got_up, near_x, near_y_c, tables_c, tokens = together(
        first, got_gate, got_up, near_x, near_y_c, tables_c, tokens
    )

    straight = place.y == place.x
    gate_planes = place.all_z(jnp.where(straight, own_gate, got_gate))
    up_planes = place.all_z(jnp.where(straight, own_up, got_up))
    gate_rest, up_rest = (
        jnp.where(straight, got_gate, own_gate),
        jnp.where(straight, got_up, own_up),
    )
    tables = jnp.concatenate([tables, tables_c], axis=0)
    lines = place.other_z(first)
    x0, y0, lines_c = place.by_x(lines), place.by_y(lines), place.by_c(lines)
    near_x_c = place.by_c(near_x)
    arrived_x = lax.all_to_all(tokens, "dp", split_axis=0, concat_axis=0, tiled=True)
    x0, y0, lines_c, near_x_c, second = together(x0, y0, lines_c, near_x_c, second)

    lines2 = place.other_z(second)
    x1, y1, lines2_c = place.by_x(lines2), place.by_y(lines2), place.by_c(lines2)
    x0_c, y0_c = place.by_c(x0), place.by_c(y0)
    x1, y1, lines2_c, x0_c, y0_c, x0, arrived_x = together(
        x1, y1, lines2_c, x0_c, y0_c, x0, arrived_x
    )

    A_model, A_hidden, B_model, B_hidden = restore_structure(adapters)
    B_gate, _ = hidden_columns(place, B_hidden[0], dp, padded)
    B_up, _ = hidden_columns(place, B_hidden[1], dp, padded)
    A_down = hidden_rows(place, A_hidden, place.q, dp, padded)
    choice, allowed, cosine_table, sine_table = block_tables(lengths[0], adapter_set[0])
    choices = jnp.concatenate(
        [block_tables(tables[k, :SEQ_DEV], tables[k, SEQ_DEV:])[0] for k in range(GROUP)], axis=0
    )
    xy0, xy1 = place.by_y(x0), place.by_x(y1)
    x1_c, y1_c = place.by_c(x1), place.by_c(y1)
    xy0, xy1, x1_c, y1_c, B_gate, B_up, A_down, choices, gate_planes, other_down, cotangent = together(
        xy0, xy1, x1_c, y1_c, B_gate, B_up, A_down, choices, gate_planes, other_down, cotangent
    )

    got_down = place.by_y(other_down)
    arrived_cot = lax.all_to_all(cotangent, "dp", split_axis=0, concat_axis=0, tiled=True)
    gate_mates = place.by_x(place.other_z(gate_planes))
    attention = AttentionWeights(
        place,
        weights,
        ((lines, lines_c, x0, x0_c), (lines2, lines2_c, x1, x1_c)),
        ((y0, y0_c, xy0, place.by_c(xy0)), (y1, y1_c, xy1, place.by_c(xy1))),
        (near_y, near_y_c, near_x, near_x_c),
    )
    gain_first = gain_one.astype(jnp.float32)
    gain_second = gain_two.astype(jnp.float32)

    x = arrived_x[token_order].astype(jnp.float32)
    scale_one = rms_scale(x)
    n1 = low(x * scale_one * gain_first)

    z_qkv = low(
        jnp.einsum("nd,tdr->tnr", n1, A_model[:3], preferred_element_type=jnp.float32) * choice
    )
    bias = jnp.where(allowed, 0.0, -jnp.inf)
    lin, got_down = together(attention.times(n1, 0, 3), got_down)
    left_planes = place.all_z(jnp.where(straight, own_down, got_down)[:, :cut])
    left_rest = jnp.where(straight, got_down, own_down)[:, :cut]
    right_planes = place.all_z(jnp.stack([own_down[:, cut:], got_down[:, cut:]]))
    qkv, o = attention_call(
        attention_kernel,
        (
            (lin, 2),
            (z_qkv, None),
            (B_model[:3], 2),
            (cosine_table, None),
            (sine_table, None),
            (bias, None),
        ),
        (((3, count, MODEL_WIDTH), 2), ((count, MODEL_WIDTH), 1)),
    )
    o, up_planes, gate_mates = together(o, up_planes, gate_mates)
    up_mates = place.by_x(place.other_z(up_planes))
    z_out, delta_out = apply_adapter_delta(o, A_model[3], B_model[3], choice)
    m = x + residual_branch_scale * (attention.times(o, 3, 1)[0] + delta_out)
    scale_two = rms_scale(m)
    n2 = low(m * scale_two * gain_second)

    n2_y = place.by_y(n2)
    n2_y, arrived_cot, left_planes, up_mates = together(
        n2_y, arrived_cot, left_planes, up_mates
    )
    left_mates = place.by_x(place.other_z(left_planes))
    g = arrived_cot[token_order].astype(jnp.float32)
    e_down = low(residual_branch_scale * g)
    dz_down = low(adapter_scale * matrix_product_backward(e_down, B_model[4]) * choice)
    sent = jnp.concatenate([e_down, dz_down], axis=1)
    sent_y = place.by_y(sent)
    n2_all = jnp.concatenate([n2, n2_y], axis=0)
    n2_all = jnp.concatenate([n2_all, place.by_c(n2_all)], axis=0)
    gate_pieces = (gate_planes, gate_rest, gate_mates)
    forward = FeedForward(place, (left_planes, left_rest, left_mates), right_planes)
    gt, z_gate = forward.hidden(n2_all, choices, A_model[4], B_gate, gate_pieces)
    up_pieces = (up_planes, up_rest, up_mates)
    up, z_up = forward.hidden(n2_all, choices, A_model[5], B_up, up_pieces)
    gt, up, left_mates, right_planes, sent_y = together(gt, up, left_mates, right_planes, sent_y)
    sent_pair = jnp.concatenate([sent, sent_y], axis=0)
    sent_mate = place.by_c(sent_pair)
    dz_down_all = jnp.concatenate(
        [sent_pair[:, MODEL_WIDTH:], sent_mate[:, MODEL_WIDTH:]], axis=0
    )
    feed = FeedForward(place, (left_planes, left_rest, left_mates), right_planes)
    h, e_gate, e_up, keep, send = feed.back(
        gt, up, (sent_pair, sent_mate), A_down, B_gate, B_up, gate_pieces, up_pieces
    )
    own_sum, other_sum = place.half_sum(keep, send)
    other_sum, h, e_gate, e_up = together(low(other_sum), h, e_gate, e_up)
    got = place.by_y(other_sum)
    y_keep, y_send = feed.out(h, MODEL_WIDTH)
    dA_down = low(outer_product_sum(h, dz_down_all))
    own_hidden = FEEDFORWARD_UNITS // (dp * GROUP)
    dA_hidden = lax.dynamic_update_slice(
        jnp.zeros((dp, GROUP, own_hidden, ADAPTER_COLUMNS), jnp.bfloat16),
        dA_down.reshape(dp, 1, padded, ADAPTER_COLUMNS)[:, :, :own_hidden],
        (0, place.q, 0, 0),
    )
    hidden_parts = [dA_hidden.reshape(-1, ADAPTER_COLUMNS)] + [
        spread_columns(
            place, low(adapter_scale * outer_product_sum(z, e)), FEEDFORWARD_UNITS, dp, padded
        ).reshape(-1, ADAPTER_COLUMNS)
        for z, e in ((z_gate, e_gate), (z_up, e_up))
    ]
    got, y_send, *hidden_parts = together(got, y_send, *hidden_parts)
    back_sum = own_sum + got.astype(jnp.float32)
    y_own, y_other = place.half_sum(y_keep, y_send)
    y_got = place.by_y(low(y_other))
    cuts = [MODEL_WIDTH + k * ADAPTER_COLUMNS for k in range(3)]
    dz_gate, dz_up, z_down = jnp.split(back_sum, cuts, axis=1)[1:]
    dz_gate, dz_up = low(adapter_scale * dz_gate * choice), low(adapter_scale * dz_up * choice)
    z_down = low(z_down * choice)
    dn2 = (
        back_sum[:, :MODEL_WIDTH]
        + matrix_product_backward(dz_gate, A_model[4])
        + matrix_product_backward(dz_up, A_model[5])
    )
    dm = g + norm_back(m, scale_two, gain_second, dn2)
    e_out = low(residual_branch_scale * dm)
    dz_out = low(adapter_scale * matrix_product_backward(e_out, B_model[3]) * choice)
    (e_qkv,) = attention_call(
        attention_back_kernel,
        (
            (qkv, 2),
            (attention.times_transposed(e_out[None], 3, 1), 1),
            (dz_out, None),
            (A_model[3], 0),
            (cosine_table, None),
            (sine_table, None),
            (bias, None),
        ),
        (((3, count, MODEL_WIDTH), 2),),
    )
    e_qkv, y_got = together(e_qkv, y_got)
    y = m + residual_branch_scale * (
        y_own + y_got.astype(jnp.float32) + adapter_scale * matrix_product(z_down, B_model[4])
    )
    inverse = (
        jnp.zeros_like(token_order).at[token_order].set(jnp.arange(count, dtype=jnp.int32))
    )
    dz_qkv = low(
        adapter_scale
        * jnp.einsum("tnd,trd->tnr", e_qkv, B_model[:3], preferred_element_type=jnp.float32)
        * choice
    )
    flat = model_gradients(
        (
            n1,
            dz_qkv,
            z_qkv,
            e_qkv,
            o,
            dz_out,
            z_out,
            e_out,
            n2,
            dz_gate,
            dz_up,
            z_down,
            e_down,
        ),
        hidden_parts,
    )
    share = flat.shape[0] // (dp * shard)
    total, (e_qkv, dz_qkv, y) = reduce_over_cores(place, flat, (e_qkv, dz_qkv, y))
    owner = OwnerSum(place, total, share)
    back_out = lax.all_to_all(low(y)[inverse], "dp", split_axis=0, concat_axis=0, tiled=True)
    dn1 = attention.times_transposed(e_qkv, 0, 3) + jnp.einsum(
        "tnr,tdr->nd", dz_qkv, A_model[:3], preferred_element_type=jnp.float32
    )
    dx = dm + norm_back(x, scale_one, gain_first, dn1)
    owner.got, back_out, dx = together(owner.got, back_out, low(dx))
    total = owner.over_chips()
    total, back_grad = together(
        total, lax.all_to_all(dx[inverse], "dp", split_axis=0, concat_axis=0, tiled=True)
    )
    gradient = owner.over_planes(total)
    offset = lax.axis_index(AXES) * share
    own_params = lax.dynamic_slice_in_dim(
        adapters.reshape(-1, ADAPTER_COLUMNS), offset, share
    ).astype(jnp.float32)
    first = first_moment_running.reshape(share, ADAPTER_COLUMNS)
    second = second_moment_running.reshape(share, ADAPTER_COLUMNS)
    fresh_first = first_decay_rate * first + (1.0 - first_decay_rate) * gradient
    fresh_second = second_decay_rate * second + (1.0 - second_decay_rate) * gradient * gradient
    unbiased_first = fresh_first / (1.0 - first_decay_rate**OPT_STEP)
    unbiased_second = fresh_second / (1.0 - second_decay_rate**OPT_STEP)
    update = (
        unbiased_first / (jnp.sqrt(unbiased_second) + adaptive_epsilon)
        + weight_shrink_rate * own_params
    )
    updated = gather_owners(place, low(own_params - learning_rate * update))

    return (
        back_out,
        back_grad,
        gradient.reshape(-1),
        fresh_first.reshape(-1),
        fresh_second.reshape(-1),
        updated,
    )


def solution(mesh):
    rows = P(AXES, None)
    weight = P("dp", None)
    return jax.shard_map(
        functools.partial(shards, mesh.shape["dp"], mesh.shape["shard"]),
        mesh=mesh,
        in_specs=(rows,) * 5 + (P(), P()) + (weight,) * 7 + (P(), P(AXES), P(AXES)),
        out_specs=(rows, rows, P(AXES), P(AXES), P(AXES), P()),
        check_vma=False,
    )
```

```python
import functools
import math

import jax
import jax.numpy as jnp
from jax import lax
from jax.experimental import pallas as pl
from jax.experimental.pallas import tpu as pltpu
from jax.sharding import PartitionSpec as P

MODEL_WIDTH = 2304
ATTENTION_HEADS = 36
HEAD_SIZE = 64
FEEDFORWARD_UNITS = 5760
ADAPTER_RANK = 16
OPT_STEP = 10
SEQ_DEV = 4
TOK_DEV = 256
ADAPTER_COLUMNS = 128


norm_eps = 1e-05
residual_branch_scale = 1.4 / math.sqrt(40.0)
adapter_scale = 2.0
rope_base = 10000.0
first_decay_rate = 0.9
second_decay_rate = 0.999
adaptive_epsilon = 1e-08
weight_shrink_rate = 0.01
learning_rate = 0.01


def matrix_product(left_side, right_side):
    return jnp.dot(left_side, right_side, preferred_element_type=jnp.float32)


def matrix_product_backward(left_side, right_side):
    return lax.dot_general(
        left_side, right_side, (((1,), (1,)), ((), ())), preferred_element_type=jnp.float32
    )


def outer_product_sum(left_side, right_side):
    return lax.dot_general(
        left_side, right_side, (((0,), (0,)), ((), ())), preferred_element_type=jnp.float32
    )


def low(values):
    return values.astype(jnp.bfloat16)


def block_tables(sequence_lengths, sequence_adapter_index):
    row_ids = jnp.arange(TOK_DEV, dtype=jnp.int32)
    seq_ends = jnp.cumsum(sequence_lengths, dtype=jnp.int32)
    seq_starts = seq_ends - sequence_lengths
    segment = jnp.sum(
        (row_ids[:, None] >= seq_ends[None, :]).astype(jnp.int32), axis=1, dtype=jnp.int32
    )
    member = (segment[:, None] == jnp.arange(SEQ_DEV, dtype=jnp.int32)[None, :]).astype(jnp.int32)
    position = row_ids - jnp.sum(member * seq_starts[None, :], axis=1, dtype=jnp.int32)
    token_adapter_index = jnp.sum(member * sequence_adapter_index[None, :], axis=1, dtype=jnp.int32)
    adapter_choice_index = (
        jnp.arange(ADAPTER_COLUMNS, dtype=jnp.int32)[None, :] // ADAPTER_RANK
        == token_adapter_index[:, None]
    ).astype(jnp.float32)
    allowed = (segment[:, None] == segment[None, :]) & (row_ids[None, :] <= row_ids[:, None])
    half_dim = HEAD_SIZE // 2
    inv_freq = jnp.power(rope_base, -2.0 * jnp.arange(half_dim, dtype=jnp.float32) / HEAD_SIZE)
    angles = position.astype(jnp.float32)[:, None] * inv_freq[None, :]
    cosine, sine = jnp.cos(angles), jnp.sin(angles)
    return (
        adapter_choice_index,
        allowed,
        jnp.concatenate([cosine] * (2 * HEADS_AT_ONCE), axis=1),
        jnp.concatenate([-sine, sine] * HEADS_AT_ONCE, axis=1),
    )


def restore_structure(flattened_vector):
    first_boundary = 6 * MODEL_WIDTH * ADAPTER_COLUMNS
    second_boundary = first_boundary + FEEDFORWARD_UNITS * ADAPTER_COLUMNS
    third_boundary = second_boundary + 5 * ADAPTER_COLUMNS * MODEL_WIDTH
    return (
        flattened_vector[:first_boundary].reshape(6, MODEL_WIDTH, ADAPTER_COLUMNS),
        flattened_vector[first_boundary:second_boundary].reshape(
            FEEDFORWARD_UNITS, ADAPTER_COLUMNS
        ),
        flattened_vector[second_boundary:third_boundary].reshape(5, ADAPTER_COLUMNS, MODEL_WIDTH),
        flattened_vector[third_boundary:].reshape(2, ADAPTER_COLUMNS, FEEDFORWARD_UNITS),
    )


def rms_scale(values):
    return lax.rsqrt(jnp.mean(values * values, axis=-1, keepdims=True) + norm_eps)


def norm_back(values, scale, gain, gradient_value):
    weighted = gradient_value * gain
    return scale * weighted - values * scale**3 * jnp.mean(
        values * weighted, axis=-1, keepdims=True
    )


def apply_adapter_delta(input_rows, adapter_down_pair, adapter_up_pair, adapter_choice_index):
    reduced_total = low(
        matrix_product(input_rows, adapter_down_pair) * adapter_choice_index
    )
    return (reduced_total, adapter_scale * matrix_product(reduced_total, adapter_up_pair))


HEADS_AT_ONCE = 4


def head_masks(shape):
    lane = lax.broadcasted_iota(jnp.int32, shape, 1)
    return [lane // HEAD_SIZE == n for n in range(HEADS_AT_ONCE)]


def join_heads(masks, results):
    joined = results[0]
    for mask, result in zip(masks[1:], results[1:]):
        joined = jnp.where(mask, result, joined)
    return joined


def swap_halves(values):
    lane = lax.broadcasted_iota(jnp.int32, values.shape, 1)
    half, width = HEAD_SIZE // 2, values.shape[1]
    return jnp.where(
        lane % HEAD_SIZE < half, pltpu.roll(values, width - half, 1), pltpu.roll(values, half, 1)
    )


def head_scores(query, key, bias):
    scores = matrix_product_backward(query, key) * HEAD_SIZE ** (-0.5) + bias
    expanded = jnp.exp(scores - jnp.max(scores, axis=-1, keepdims=True))
    return expanded / jnp.sum(expanded, axis=-1, keepdims=True)


def attention_kernel(lin, z, up, cosine, sine, bias, qkv, attended):
    full = [lin[t] + adapter_scale * matrix_product(z[t], up[t]) for t in range(3)]
    query, key = (
        low(v * cosine[...] + swap_halves(v) * sine[...]) for v in full[:2]
    )
    value = low(full[2])
    qkv[0], qkv[1], qkv[2] = query, key, value
    masks = head_masks(query.shape)
    results = []
    for mine in masks:
        probs = head_scores(jnp.where(mine, query, jnp.zeros_like(query)), key, bias[...])
        results.append(matrix_product(low(probs), value))
    attended[...] = low(join_heads(masks, results))


def attention_back_kernel(qkv, lin, dz, down, cosine, sine, bias, grads):
    query, key, value = qkv[0], qkv[1], qkv[2]
    grad = low(lin[...] + matrix_product_backward(dz[...], down[...]))
    masks = head_masks(query.shape)
    nothing = jnp.zeros_like(query)
    results = []
    for mine in masks:
        probs = head_scores(jnp.where(mine, query, nothing), key, bias[...])
        grad_probs = matrix_product_backward(jnp.where(mine, grad, nothing), value)
        row_delta = jnp.sum(probs * grad_probs, axis=-1, keepdims=True)
        grad_scores = low(probs * (grad_probs - row_delta))
        results.append(
            (
                matrix_product(grad_scores, key),
                outer_product_sum(grad_scores, query),
                outer_product_sum(low(probs), grad),
            )
        )
    scale = HEAD_SIZE ** (-0.5)
    grad_query, grad_key, grad_value = (
        join_heads(masks, parts) for parts in zip(*results)
    )
    for t, v in enumerate((grad_query * scale, grad_key * scale)):
        grads[t] = low(v * cosine[...] - swap_halves(v) * sine[...])
    grads[2] = low(grad_value)


def attention_call(kernel, operands, outs):
    pairs = HEADS_AT_ONCE * HEAD_SIZE

    def spec(shape, axis):
        block = tuple(pairs if k == axis else n for k, n in enumerate(shape))
        return pl.BlockSpec(block, lambda i: tuple(i if k == axis else 0 for k in range(len(shape))))

    count = operands[-1][0].shape[0]
    return pl.pallas_call(
        kernel,
        grid=(ATTENTION_HEADS // HEADS_AT_ONCE,),
        out_shape=[jax.ShapeDtypeStruct(shape, jnp.bfloat16) for shape, _ in outs],
        in_specs=[spec(v.shape, axis) for v, axis in operands],
        out_specs=[spec(shape, axis) for shape, axis in outs],
        compiler_params=pltpu.CompilerParams(vmem_limit_bytes=48 << 20),
        cost_estimate=pl.CostEstimate(
            flops=8 * count * count * MODEL_WIDTH // 16,
            bytes_accessed=24 * count * MODEL_WIDTH // 16,
            transcendentals=0,
        ),
    )(*[v for v, _ in operands])


GROUP = 4
AXES = ("dp", "shard")


def together(*values):
    return lax.optimization_barrier(values)


class Place:
    def __init__(self, dp, shard):
        self.line, self.shard = dp // 2, shard
        i, s = lax.axis_index("dp"), lax.axis_index("shard")
        self.z, self.y, self.x, self.c = i // 2, i % 2, s // 2, s % 2
        self.q = self.y * 2 + self.c
        self.spots = [
            (z, y, x, c)
            for z in range(self.line)
            for y in range(2)
            for x in range(shard // 2)
            for c in range(2)
        ]

    def number(self, z, y, x, c):
        return (z * 2 + y) * self.shard + x * 2 + c

    def move(self, value, target):
        pairs = []
        for spot in self.spots:
            to = target(*spot)
            if to is not None:
                pairs.append((self.number(*spot), self.number(*to)))
        return lax.ppermute(value, AXES, pairs)

    def by_y(self, value):
        return self.move(value, lambda z, y, x, c: (z, 1 - y, x, c))

    def by_x(self, value):
        return self.move(value, lambda z, y, x, c: (z, y, 1 - x, c))

    def by_c(self, value):
        return self.move(value, lambda z, y, x, c: (z, y, x, 1 - c))

    def ring_z(self, value, step):
        return self.move(value, lambda z, y, x, c: ((z + step) % self.line, y, x, c))

    def all_z(self, block):
        groups = [[z * 2 + y for z in range(self.line)] for y in range(2)]
        return lax.all_gather(block, "dp", axis=0, axis_index_groups=groups)

    def other_z(self, blocks):
        return jnp.stack(
            [
                lax.dynamic_index_in_dim(blocks, (self.z + k) % self.line, 0, keepdims=False)
                for k in range(1, self.line)
            ]
        )

    def gather_group(self, rows):
        pair = jnp.concatenate([rows, self.by_y(rows)], axis=0)
        return jnp.concatenate([pair, self.by_c(pair)], axis=0)

    def half_sum(self, keep, send):
        return (keep + self.by_c(send).astype(jnp.float32)).reshape(2, -1, keep.shape[1])


def put(buffer, block, *where):
    block = block.reshape((1,) * len(where) + block.shape)
    return lax.dynamic_update_slice(
        buffer, block, tuple(where) + (0,) * (buffer.ndim - len(where))
    )


def put_quarter(place, planes, rest, mates):
    full = jnp.zeros((place.line, 2) + rest.shape, rest.dtype)
    full = lax.dynamic_update_slice(full, planes[:, None], (0, place.x) + (0,) * rest.ndim)
    full = put(full, rest, place.z, 1 - place.x)
    for k in range(1, place.line):
        full = put(full, mates[k - 1], (place.z + k) % place.line, 1 - place.x)
    return full.reshape((-1,) + rest.shape[1:])


class AttentionWeights:
    def __init__(self, place, weights, same, across, near):
        self.place, self.native = place, weights
        self.same, self.across, self.near = same, across, near
        self.s = place.x * 2 + place.c
        self.rows, self.half = weights[0].shape[0], weights[0].shape[1] // 2

    def full(self, t):
        place = self.place
        halves = []
        for h in range(2):
            cols = slice(h * self.half, (h + 1) * self.half)
            buffer = jnp.zeros((place.line, 2, self.rows, self.half), self.native[t].dtype)
            buffer = put(buffer, self.native[t][:, cols], place.z, place.y)
            for r in range(4):
                near = self.near[r][:, cols]
                with_r = put(buffer, near, place.z, 1 - place.y)
                for k in range(1, place.line):
                    plane = (place.z + k) % place.line
                    with_r = put(with_r, self.same[h][r][k - 1], plane, place.y)
                    with_r = put(with_r, self.across[h][r][k - 1], plane, 1 - place.y)
                buffer = jnp.where(self.s ^ r == t, with_r, buffer)
            halves.append(buffer.reshape(-1, self.half))
        return jnp.concatenate(halves, axis=1)

    def times(self, values, first, count):
        if self.rows % 16:
            return jnp.stack([matrix_product(values, self.full(first + j)) for j in range(count)])
        return self.call(values, first, count, False)

    def times_transposed(self, values, first, count):
        if self.rows % 16:
            return sum(
                matrix_product_backward(values[j], self.full(first + j)) for j in range(count)
            )
        return self.call(values, first, count, True)

    def call(self, values, first, count, back):
        place, rows, half = self.place, self.rows, self.half
        where = jnp.stack([place.z, place.y, self.s]).astype(jnp.int32)
        width, depth = 2 * half, rows * 2 * place.line
        tokens = values.shape[-2]
        shape = (tokens, depth) if back else (count, tokens, width)
        held = pl.BlockSpec(memory_space=pltpu.VMEM)
        given = pl.BlockSpec(memory_space=pl.ANY)
        pieces = (
            list(self.native[first : first + count])
            + [v for h in range(2) for v in self.same[h]]
            + [v for h in range(2) for v in self.across[h]]
            + list(self.near)
        )
        return pl.pallas_call(
            functools.partial(weights_kernel, place.line, first, count, back),
            out_shape=jax.ShapeDtypeStruct(shape, jnp.float32),
            in_specs=[pl.BlockSpec(memory_space=pltpu.SMEM), held] + [given] * len(pieces),
            out_specs=held,
            scratch_shapes=[
                pltpu.VMEM((2, count, depth, half), jnp.bfloat16),
                pltpu.SemaphoreType.DMA((2, count)),
            ],
            compiler_params=pltpu.CompilerParams(vmem_limit_bytes=56 << 20),
            cost_estimate=pl.CostEstimate(
                flops=2 * tokens * depth * width * count // 16,
                bytes_accessed=2 * depth * width * count // 16,
                transcendentals=0,
            ),
        )(where, values, *pieces)


def weights_kernel(line, first, count, back, where, values, *refs):
    native = refs[:count]
    same = (refs[count : count + 4], refs[count + 4 : count + 8])
    across = (refs[count + 8 : count + 12], refs[count + 12 : count + 16])
    near = refs[count + 16 : count + 20]
    out, held, sems = refs[count + 20 :]
    z, y, s = where[0], where[1], where[2]
    rows, width = native[0].shape
    half = width // 2

    def place(h, j, plane, side):
        start = pl.multiple_of(rows * (2 * plane + side), 16)
        return held.at[h, j, pl.ds(start, rows)]

    for h in range(2):
        cols = pl.ds(h * half, half)
        for j in range(count):
            pltpu.make_async_copy(
                native[j].at[:, cols], place(h, j, z, y), sems.at[h, j]
            ).start()
        for r in range(4):
            j = (s ^ r) - first

            @pl.when((j >= 0) & (j < count))
            def _():
                pltpu.make_async_copy(
                    near[r].at[:, cols], place(h, j, z, 1 - y), sems.at[h, j]
                ).start()
                for k in range(1, line):
                    plane = lax.rem(z + k, line)
                    pltpu.make_async_copy(
                        same[h][r].at[k - 1], place(h, j, plane, y), sems.at[h, j]
                    ).start()
                    pltpu.make_async_copy(
                        across[h][r].at[k - 1], place(h, j, plane, 1 - y), sems.at[h, j]
                    ).start()

    if back:
        out[...] = jnp.zeros_like(out)

    def step(i, carry):
        h, j = i // count, lax.rem(i, count)
        cols = pl.ds(pl.multiple_of(h * half, 128), half)
        pltpu.make_async_copy(held.at[h, j], held.at[h, j], sems.at[h, j]).wait()
        if back:
            out[...] += matrix_product_backward(values[j, :, cols], held[h, j])
        else:
            out[j, :, cols] = matrix_product(values[...], held[h, j])
        return carry

    lax.fori_loop(0, 2 * count, step, 0)


HIDDEN_TILE = 256


def quarter_copies(line, z, x, pieces, target, sem):
    planes, rest, mates = pieces
    rows = rest.shape[0]

    def copy(source, plane, side):
        start = pl.multiple_of(rows * (2 * plane + side), 16)
        pltpu.make_async_copy(source, target.at[pl.ds(start, rows)], sem).start()

    for plane in range(line):
        copy(planes.at[plane], plane, x)
    copy(rest, z, 1 - x)
    for k in range(1, line):
        copy(mates.at[k - 1], lax.rem(z + k, line), 1 - x)


def hidden_kernel(line, where, values, choices, down, up, planes, rest, mates, out, reduced, held, sems):
    step = pl.program_id(0)
    tiles = held.shape[0]

    @pl.when(step == 0)
    def _():
        def start(tile, carry):
            cols = pl.ds(pl.multiple_of(tile * HIDDEN_TILE, 128), HIDDEN_TILE)
            pieces = (planes.at[:, :, cols], rest.at[:, cols], mates.at[:, :, cols])
            quarter_copies(line, where[0], where[2], pieces, held.at[tile], sems.at[tile])
            return carry

        lax.fori_loop(0, tiles, start, 0)
        reduced[...] = low(matrix_product(values[...], down[...]) * choices[...])

    pltpu.make_async_copy(held.at[step], held.at[step], sems.at[step]).wait()
    out[...] = matrix_product(values[...], held[step]) + adapter_scale * matrix_product(
        reduced[...], up[...]
    )


def down_copies(line, where, left, right, target, sems):
    planes, rest, mates = left
    z, y, x = where[0], where[1], where[2]
    rows, cut = rest.shape

    def copy(source, plane, side, cols):
        block = 2 * plane + side
        start = pl.multiple_of(rows * block, 16)
        pltpu.make_async_copy(source, target.at[pl.ds(start, rows), cols], sems.at[block]).start()

    first, second = pl.ds(0, cut), pl.ds(cut, target.shape[1] - cut)
    for plane in range(line):
        copy(planes.at[plane], plane, x, first)
        copy(right.at[plane, 0], plane, y, second)
        copy(right.at[plane, 1], plane, 1 - y, second)
    copy(rest, z, 1 - x, first)
    for k in range(1, line):
        copy(mates.at[k - 1], lax.rem(z + k, line), 1 - x, first)


def wait_rows(target, rows, sems, block):
    part = target.at[pl.ds(pl.multiple_of(rows * block, 16), rows)]
    pltpu.make_async_copy(part, part, sems.at[block]).wait()


def feed_forward_back_kernel(
    line, where, gt, up, near, far, down_lower, upper_gate, upper_up, *refs
):
    left, right, gate_pieces, up_pieces = refs[:3], refs[3], refs[4:7], refs[7:10]
    hidden, e_gate, e_up, keep, send, total, down, held, down_sems, sems = refs[10:]
    step = pl.program_id(0)
    tiles, rows = held.shape[1], left[1].shape[0]
    blocks, width = 2 * line, down.shape[1]

    @pl.when(step == 0)
    def _():
        def start(tile, carry):
            cols = pl.ds(pl.multiple_of(tile * HIDDEN_TILE, 128), HIDDEN_TILE)
            for t, (planes, rest, mates) in enumerate((gate_pieces, up_pieces)):
                pieces = (planes.at[:, :, cols], rest.at[:, cols], mates.at[:, :, cols])
                quarter_copies(line, where[0], where[2], pieces, held.at[t, tile], sems.at[t, tile])
            return carry

        start(0, 0)
        down_copies(line, where, left, right, down, down_sems)
        lax.fori_loop(1, tiles, start, 0)
        keep[...] = jnp.zeros_like(keep)
        total[...] = jnp.zeros_like(total)

    seen = 0
    for tile in range(tiles):
        until = -(-(tile + 1) * HIDDEN_TILE // rows)

        @pl.when(step == tile)
        def _(seen=seen, until=until):
            for block in range(seen, until):
                wait_rows(down, rows, down_sems, block)

        seen = until
    for t in range(2):
        pltpu.make_async_copy(held.at[t, step], held.at[t, step], sems.at[t, step]).wait()

    tile_rows = down[pl.ds(pl.multiple_of(step * HIDDEN_TILE, HIDDEN_TILE), HIDDEN_TILE), :]
    count = keep.shape[0]
    for n, (sums, sent) in enumerate(((keep, near), (total, far))):
        own = slice(n * count, (n + 1) * count)
        gate_value, up_value = gt[own, :], up[own, :]
        dh = matrix_product_backward(sent[:, :width], tile_rows) + matrix_product_backward(
            sent[:, width:], down_lower[...]
        )
        sg = jax.nn.sigmoid(gate_value)
        act = gate_value * sg
        h = low(act * up_value)
        grad_gate = low(dh * up_value * (sg + gate_value * sg * (1.0 - sg)))
        grad_up = low(dh * act)
        hidden[own, :], e_gate[own, :], e_up[own, :] = h, grad_gate, grad_up
        sums[:, :width] += matrix_product_backward(
            grad_gate, held[0, step]
        ) + matrix_product_backward(grad_up, held[1, step])
        lanes = [width + k * ADAPTER_COLUMNS for k in range(4)]
        sums[:, lanes[0] : lanes[1]] += matrix_product_backward(grad_gate, upper_gate[...])
        sums[:, lanes[1] : lanes[2]] += matrix_product_backward(grad_up, upper_up[...])
        sums[:, lanes[2] : lanes[3]] += matrix_product(h, down_lower[...])

    @pl.when(step == tiles - 1)
    def _():
        send[...] = low(total[...])


def feed_forward_out_kernel(line, where, hidden, *refs):
    left, right = refs[:3], refs[3]
    keep, send, down, down_sems = refs[4:]
    rows = left[1].shape[0]
    down_copies(line, where, left, right, down, down_sems)
    for block in range(2 * line):
        wait_rows(down, rows, down_sems, block)
    count = keep.shape[0]
    keep[...] = matrix_product(hidden[:count, :], down[...])
    send[...] = low(matrix_product(hidden[count:, :], down[...]))


def small_cost(flops):
    return pl.CostEstimate(flops=flops // 16, bytes_accessed=flops // 8192, transcendentals=0)


class FeedForward:
    def __init__(self, place, left, right):
        self.place, self.left, self.right = place, left, right
        self.cut = left[1].shape[1]
        self.padded = left[1].shape[0]
        self.kernels = self.padded % 64 == 0
        self.where = jnp.stack([place.z, place.y, place.x]).astype(jnp.int32)

    def down(self):
        right = jnp.where(self.place.y == 0, self.right, self.right[:, ::-1])
        right = right.reshape(-1, right.shape[-1])
        return jnp.concatenate([put_quarter(self.place, *self.left), right], axis=1)

    def hidden(self, values, choices, lower, upper, pieces):
        count, width = values.shape[0], upper.shape[1]
        if not self.kernels:
            reduced = low(matrix_product(values, lower) * choices)
            full = put_quarter(self.place, *pieces)
            return matrix_product(values, full) + adapter_scale * matrix_product(
                reduced, upper
            ), reduced
        tiles = width // HIDDEN_TILE
        once = lambda v: pl.BlockSpec(v.shape, lambda i: (0, 0), pipeline_mode=pl.Buffered(1))
        columns = lambda n: pl.BlockSpec((n, HIDDEN_TILE), lambda i: (0, i))
        return pl.pallas_call(
            functools.partial(hidden_kernel, self.place.line),
            grid=(tiles,),
            out_shape=[
                jax.ShapeDtypeStruct((count, width), jnp.float32),
                jax.ShapeDtypeStruct((count, ADAPTER_COLUMNS), jnp.bfloat16),
            ],
            in_specs=[pl.BlockSpec(memory_space=pltpu.SMEM)]
            + [once(v) for v in (values, choices, lower)]
            + [columns(upper.shape[0])]
            + [pl.BlockSpec(memory_space=pl.ANY)] * 3,
            out_specs=[
                columns(count),
                pl.BlockSpec((count, ADAPTER_COLUMNS), lambda i: (0, 0)),
            ],
            scratch_shapes=[
                pltpu.VMEM((tiles, values.shape[1], HIDDEN_TILE), jnp.bfloat16),
                pltpu.SemaphoreType.DMA((tiles,)),
            ],
            compiler_params=pltpu.CompilerParams(vmem_limit_bytes=40 << 20),
            cost_estimate=small_cost(2 * count * width * values.shape[1]),
        )(self.where, values, choices, lower, upper, *pieces)

    def back(self, gt, up, sent, lower, upper_gate, upper_up, gate_pieces, up_pieces):
        count, width = gt.shape
        half = count // 2
        near, far = sent
        model = near.shape[1] - ADAPTER_COLUMNS
        sums = model + 3 * ADAPTER_COLUMNS
        if not self.kernels:
            sent = jnp.concatenate([near, far], axis=0)
            down = self.down()
            gate, up_part = put_quarter(self.place, *gate_pieces), put_quarter(self.place, *up_pieces)
            sg = jax.nn.sigmoid(gt)
            act = gt * sg
            h = low(act * up)
            dh = matrix_product_backward(sent[:, :model], down) + matrix_product_backward(
                sent[:, model:], lower
            )
            e_gate = low(dh * up * (sg + gt * sg * (1.0 - sg)))
            e_up = low(dh * act)
            total = jnp.concatenate(
                [
                    matrix_product_backward(e_gate, gate) + matrix_product_backward(e_up, up_part),
                    matrix_product_backward(e_gate, upper_gate),
                    matrix_product_backward(e_up, upper_up),
                    matrix_product(h, lower),
                ],
                axis=1,
            )
            return h, e_gate, e_up, total[:half], low(total[half:])
        tiles = width // HIDDEN_TILE
        once = lambda shape: pl.BlockSpec(shape, lambda i: (0, 0), pipeline_mode=pl.Buffered(1))
        columns = lambda n: pl.BlockSpec((n, HIDDEN_TILE), lambda i: (0, i))
        pieces = (*self.left, self.right, *gate_pieces, *up_pieces)
        return pl.pallas_call(
            functools.partial(feed_forward_back_kernel, self.place.line),
            grid=(tiles,),
            out_shape=[jax.ShapeDtypeStruct((count, width), jnp.bfloat16)] * 3
            + [
                jax.ShapeDtypeStruct((half, sums), jnp.float32),
                jax.ShapeDtypeStruct((half, sums), jnp.bfloat16),
            ],
            in_specs=[
                pl.BlockSpec(memory_space=pltpu.SMEM),
                columns(count),
                columns(count),
                once(near.shape),
                once(far.shape),
                pl.BlockSpec((HIDDEN_TILE, ADAPTER_COLUMNS), lambda i: (i, 0)),
                columns(ADAPTER_COLUMNS),
                columns(ADAPTER_COLUMNS),
            ]
            + [pl.BlockSpec(memory_space=pl.ANY)] * len(pieces),
            out_specs=[columns(count)] * 3 + [once((half, sums))] * 2,
            scratch_shapes=[
                pltpu.VMEM((half, sums), jnp.float32),
                pltpu.VMEM((width, model), jnp.bfloat16),
                pltpu.VMEM((2, tiles, model, HIDDEN_TILE), jnp.bfloat16),
                pltpu.SemaphoreType.DMA((2 * self.place.line,)),
                pltpu.SemaphoreType.DMA((2, tiles)),
            ],
            compiler_params=pltpu.CompilerParams(vmem_limit_bytes=60 << 20),
            cost_estimate=small_cost(6 * count * width * model),
        )(self.where, gt, up, near, far, lower, upper_gate, upper_up, *pieces)

    def out(self, h, model):
        count, width = h.shape
        half = count // 2
        if not self.kernels:
            total = matrix_product(h, self.down())
            return total[:half], low(total[half:])
        held = pl.BlockSpec(memory_space=pltpu.VMEM)
        return pl.pallas_call(
            functools.partial(feed_forward_out_kernel, self.place.line),
            out_shape=[
                jax.ShapeDtypeStruct((half, model), jnp.float32),
                jax.ShapeDtypeStruct((half, model), jnp.bfloat16),
            ],
            in_specs=[pl.BlockSpec(memory_space=pltpu.SMEM), held]
            + [pl.BlockSpec(memory_space=pl.ANY)] * 4,
            out_specs=[held] * 2,
            scratch_shapes=[
                pltpu.VMEM((width, model), jnp.bfloat16),
                pltpu.SemaphoreType.DMA((2 * self.place.line,)),
            ],
            compiler_params=pltpu.CompilerParams(vmem_limit_bytes=40 << 20),
            cost_estimate=small_cost(64 * count * width * model),
        )(self.where, h, *self.left, self.right)


def columns_kernel(own, padded, quarter, value, *outs):
    each, window = GROUP * own, 2 * padded
    rows, width = value.shape
    step = pl.program_id(0)
    lane = lax.broadcasted_iota(jnp.int32, (rows, window), 1)
    for out, k in zip(outs, (quarter[0], quarter[0] ^ 2)):
        turned = []
        for n in range(2):
            start = each * (2 * step + n) + own * k
            base = jnp.minimum(start // 128, (width - window) // 128) * 128
            piece = value[:, pl.ds(pl.multiple_of(base, 128), window)].astype(jnp.float32)
            turned.append(pltpu.roll(piece, lax.rem(window + n * padded - (start - base), window), 1))
        kept = jnp.where(lane < own, turned[0], 0.0)
        kept = jnp.where((lane >= padded) & (lane < padded + own), turned[1], kept)
        out[...] = low(kept)


def hidden_columns(place, value, blocks, padded):
    rows, width = value.shape
    own = width // (blocks * GROUP)
    if padded % 64 or 2 * padded > width:

        def take(k):
            def cut(given):
                pieces = []
                for i in range(blocks):
                    start = own * (GROUP * i + k)
                    piece = given[:, start : start + own]
                    pieces.append(jnp.pad(piece, ((0, 0), (0, padded - own))))
                return jnp.concatenate(pieces, axis=1)

            return cut

        branches = [take(k) for k in range(GROUP)]
        return [lax.switch(k, branches, value) for k in (place.q, place.q ^ 2)]
    return pl.pallas_call(
        functools.partial(columns_kernel, own, padded),
        grid=(blocks // 2,),
        out_shape=[jax.ShapeDtypeStruct((rows, blocks * padded), value.dtype)] * 2,
        in_specs=[
            pl.BlockSpec(memory_space=pltpu.SMEM),
            pl.BlockSpec((rows, width), lambda i: (0, 0)),
        ],
        out_specs=[pl.BlockSpec((rows, 2 * padded), lambda i: (0, i))] * 2,
        compiler_params=pltpu.CompilerParams(vmem_limit_bytes=32 << 20),
        cost_estimate=pl.CostEstimate(
            flops=8 * rows * width, bytes_accessed=4 * rows * width, transcendentals=0
        ),
    )(place.q.astype(jnp.int32).reshape(1), value)


def hidden_rows(place, value, quarter, blocks, padded):
    own = value.shape[0] // (blocks * GROUP)
    split = value.reshape(blocks, GROUP, own, -1)
    got = lax.dynamic_index_in_dim(split, quarter, 1, keepdims=False)
    return jnp.pad(got, ((0, 0), (0, padded - own), (0, 0))).reshape(blocks * padded, -1)


def spread_kernel(own, padded, quarter, value, out, total):
    rows, width = total.shape
    window = 2 * padded
    total[...] = jnp.zeros_like(total)
    lane = lax.broadcasted_iota(jnp.int32, (rows, window), 1)
    for i in range(width // (GROUP * own)):
        pair, n = i // 2, i % 2
        start = own * (GROUP * i + quarter[0])
        base = jnp.minimum(start // 128, (width - window) // 128) * 128
        piece = value[:, pair * window : (pair + 1) * window].astype(jnp.float32)
        inside = (lane >= n * padded) & (lane < n * padded + own)
        turned = pltpu.roll(
            jnp.where(inside, piece, 0.0),
            lax.rem(window - n * padded + (start - base), window),
            1,
        )
        total[:, pl.ds(pl.multiple_of(base, 128), window)] += turned
    out[...] = low(total[...])


def spread_columns(place, value, width, blocks, padded):
    rows = value.shape[0]
    own = width // (blocks * GROUP)
    if padded % 64 or 2 * padded > width:

        def lay(k):
            def build(given):
                pieces = []
                for i in range(blocks):
                    piece = given[:, padded * i : padded * i + own]
                    pieces.append(jnp.pad(piece, ((0, 0), (own * k, own * (GROUP - 1 - k)))))
                return jnp.concatenate(pieces, axis=1)

            return build

        return lax.switch(place.q, [lay(k) for k in range(GROUP)], value)
    return pl.pallas_call(
        functools.partial(spread_kernel, own, padded),
        out_shape=jax.ShapeDtypeStruct((rows, width), jnp.bfloat16),
        in_specs=[
            pl.BlockSpec(memory_space=pltpu.SMEM),
            pl.BlockSpec(memory_space=pltpu.VMEM),
        ],
        out_specs=pl.BlockSpec(memory_space=pltpu.VMEM),
        scratch_shapes=[pltpu.VMEM((rows, width), jnp.float32)],
        compiler_params=pltpu.CompilerParams(vmem_limit_bytes=32 << 20),
        cost_estimate=pl.CostEstimate(
            flops=8 * rows * width, bytes_accessed=4 * rows * width, transcendentals=0
        ),
    )(place.q.astype(jnp.int32).reshape(1), value)


def both(kept, got):
    return low(kept.astype(jnp.float32) + got.astype(jnp.float32))


def pick(values, index, axis):
    return lax.dynamic_index_in_dim(values, index, axis, keepdims=False)


def gradients_kernel(*refs):
    n1, dz_qkv, z_qkv, e_qkv, o, dz_out, z_out, e_out = refs[:8]
    n2, dz_gate, dz_up, z_down, e_down = refs[8:13]
    parts_given, (flat, turned, staged, sems, part_sems) = refs[13:16], refs[16:]
    lower = [(n1[...], dz_qkv[t]) for t in range(3)]
    lower += [(o[...], dz_out[...]), (n2[...], dz_gate[...]), (n2[...], dz_up[...])]
    upper = [(z_qkv[t], e_qkv[t]) for t in range(3)]
    upper += [(z_out[...], e_out[...]), (z_down[...], e_down[...])]
    rows = staged.shape[1]
    ranks = ADAPTER_COLUMNS
    parts = rows // ranks
    given = parts_given[0].shape[0]
    second = 6 * rows + given
    starts = [rows * k for k in range(6)] + [second + rows * k for k in range(5)]
    places = (6 * rows, second + 5 * rows, second + 5 * rows + given)
    moves = [
        pltpu.make_async_copy(part, flat.at[pl.ds(start, given)], part_sems.at[n])
        for n, (part, start) in enumerate(zip(parts_given, places))
    ]
    for move in moves:
        move.start()
    copies = []
    for k, start in enumerate(starts):
        slot = k % 2
        if k > 1:
            copies[k - 2].wait()
        if k < 6:
            staged[slot] = low(outer_product_sum(*lower[k]))
        else:
            full = adapter_scale * outer_product_sum(*upper[k - 6])
            for j in range(parts):
                turned[pl.ds(j, ranks, parts), :] = full[:, j * ranks : (j + 1) * ranks]
            staged[slot] = low(turned[...])
        copies.append(
            pltpu.make_async_copy(staged.at[slot], flat.at[pl.ds(start, rows)], sems.at[slot])
        )
        copies[k].start()
    copies[-2].wait()
    copies[-1].wait()
    for move in moves:
        move.wait()


def model_gradients(operands, hidden_parts):
    held = pl.BlockSpec(memory_space=pltpu.VMEM)
    apart = pl.BlockSpec(memory_space=pl.ANY)
    rows = 11 * MODEL_WIDTH + sum(part.shape[0] for part in hidden_parts)
    return pl.pallas_call(
        gradients_kernel,
        out_shape=jax.ShapeDtypeStruct((rows, ADAPTER_COLUMNS), jnp.bfloat16),
        in_specs=[held] * len(operands) + [apart] * len(hidden_parts),
        out_specs=apart,
        scratch_shapes=[
            pltpu.VMEM((MODEL_WIDTH, ADAPTER_COLUMNS), jnp.float32),
            pltpu.VMEM((2, MODEL_WIDTH, ADAPTER_COLUMNS), jnp.bfloat16),
            pltpu.SemaphoreType.DMA((2,)),
            pltpu.SemaphoreType.DMA((len(hidden_parts),)),
        ],
        compiler_params=pltpu.CompilerParams(vmem_limit_bytes=40 << 20),
        cost_estimate=pl.CostEstimate(flops=1 << 28, bytes_accessed=1 << 22, transcendentals=0),
    )(*operands, *hidden_parts)


def reduce_over_cores(place, flat, later):
    pairs = place.line * 2 * (place.shard // 2)
    rows = flat.shape[0] // pairs
    half = -(-rows // 16) * 8
    split = flat.reshape(place.line, 2, place.shard // 2, rows, ADAPTER_COLUMNS)
    start = rows - half
    keep = lax.dynamic_slice_in_dim(split, place.c * start, half, 3)
    send = lax.dynamic_slice_in_dim(split, (1 - place.c) * start, half, 3)
    got, later = together(place.by_c(send), later)
    return both(keep, got), later


class OwnerSum:
    def __init__(self, place, total, share):
        self.place, self.share, self.half = place, share, total.shape[3]
        cut = self.half // 16 * 8
        one, two = total[:, :, :, :cut], total[:, :, :, cut:]
        self.kept = (pick(one, place.y, 1), pick(two, place.x, 2))
        self.got = (
            place.by_y(pick(one, 1 - place.y, 1)),
            place.by_x(pick(two, 1 - place.x, 2)),
        )

    def over_chips(self):
        place = self.place
        one, two = both(self.kept[0], self.got[0]), both(self.kept[1], self.got[1])
        got_one = place.by_x(pick(one, 1 - place.x, 1))
        got_two = place.by_y(pick(two, 1 - place.y, 1))
        one, two = both(pick(one, place.x, 1), got_one), both(pick(two, place.y, 1), got_two)
        return jnp.concatenate([one, two], axis=1)

    def over_planes(self, total):
        place = self.place
        got = [
            place.ring_z(pick(total, (place.z + k) % place.line, 0), k)
            for k in range(1, place.line)
        ]
        result = pick(total, place.z, 0).astype(jnp.float32)
        for value in got:
            result = result + value.astype(jnp.float32)
        start = place.c * (self.half - self.share)
        return lax.dynamic_slice_in_dim(result, start, self.share, 0)


def gather_owners(place, own):
    share = own.shape[0]
    half = -(-share // 8) * 8
    start = 2 * share - half
    mate = place.by_c(own)
    head, tail = jnp.where(place.c == 0, own, mate), jnp.where(place.c == 0, mate, own)
    pair = jnp.concatenate([head, tail], axis=0)
    planes = place.all_z(lax.dynamic_slice_in_dim(pair, place.c * start, half, 0))
    cut = half // 16 * 8
    full = jnp.zeros(
        (place.line, 2, place.shard // 2, 2 * share, ADAPTER_COLUMNS), own.dtype
    )
    for part, x_first, at in ((planes[:, :cut], True, 0), (planes[:, cut:], False, cut)):
        x_part, y_part = place.by_x(part), place.by_y(part)
        xy_part = place.by_y(x_part) if x_first else place.by_x(y_part)
        for value, y, x in (
            (part, place.y, place.x),
            (x_part, place.y, 1 - place.x),
            (y_part, 1 - place.y, place.x),
            (xy_part, 1 - place.y, 1 - place.x),
        ):
            for held, c in ((value, place.c), (place.by_c(value), 1 - place.c)):
                where = (0, y, x, c * start + at, 0)
                full = lax.dynamic_update_slice(full, held[:, None, None], where)
    return full.reshape(-1)


def shards(
    dp,
    shard,
    tokens,
    cotangent,
    arrival,
    lengths,
    adapter_set,
    gain_one,
    gain_two,
    w_query,
    w_key,
    w_value,
    w_out,
    w_gate,
    w_up,
    w_down,
    adapters,
    first_moment_running,
    second_moment_running,
):
    place = Place(dp, shard)
    token_order = arrival[0]
    count = token_order.shape[0]
    padded = -(-(FEEDFORWARD_UNITS // (dp * GROUP)) // 16) * 16


    weights = (w_query, w_key, w_value, w_out)
    s, half = place.x * 2 + place.c, MODEL_WIDTH // 2
    cut = MODEL_WIDTH - MODEL_WIDTH // 3
    stacked = jnp.stack(weights)
    mine = lax.dynamic_index_in_dim(stacked, s, 0, keepdims=False)
    first = place.all_z(mine[:, :half])
    second = place.all_z(mine[:, half:])
    near_y = place.by_y(mine)
    table = jnp.concatenate([lengths, adapter_set], axis=1)
    table_y = place.by_y(table)
    own_gate, other_gate = hidden_columns(place, w_gate, dp, padded)
    own_up, other_up = hidden_columns(place, w_up, dp, padded)
    near_y, table_y, other_gate, other_up = together(near_y, table_y, other_gate, other_up)

    near_x = place.by_x(near_y)
    got_gate, got_up = place.by_y(other_gate), place.by_y(other_up)
    near_y_c = place.by_c(near_y)
    tables = jnp.concatenate([table, table_y], axis=0)
    tables_c = place.by_c(tables)
    own_down = hidden_rows(place, w_down, place.q, 1, padded)
    other_down = hidden_rows(place, w_down, place.q ^ 2, 1, padded)
    first, got_gate, got_up, near_x, near_y_c, tables_c, tokens = together(
        first, got_gate, got_up, near_x, near_y_c, tables_c, tokens
    )

    straight = place.y == place.x
    gate_planes = place.all_z(jnp.where(straight, own_gate, got_gate))
    up_planes = place.all_z(jnp.where(straight, own_up, got_up))
    gate_rest, up_rest = (
        jnp.where(straight, got_gate, own_gate),
        jnp.where(straight, got_up, own_up),
    )
    tables = jnp.concatenate([tables, tables_c], axis=0)
    lines = place.other_z(first)
    x0, y0, lines_c = place.by_x(lines), place.by_y(lines), place.by_c(lines)
    near_x_c = place.by_c(near_x)
    arrived_x = lax.all_to_all(tokens, "dp", split_axis=0, concat_axis=0, tiled=True)
    x0, y0, lines_c, near_x_c, second = together(x0, y0, lines_c, near_x_c, second)

    lines2 = place.other_z(second)
    x1, y1, lines2_c = place.by_x(lines2), place.by_y(lines2), place.by_c(lines2)
    x0_c, y0_c = place.by_c(x0), place.by_c(y0)
    x1, y1, lines2_c, x0_c, y0_c, x0, arrived_x = together(
        x1, y1, lines2_c, x0_c, y0_c, x0, arrived_x
    )

    A_model, A_hidden, B_model, B_hidden = restore_structure(adapters)
    B_gate, _ = hidden_columns(place, B_hidden[0], dp, padded)
    B_up, _ = hidden_columns(place, B_hidden[1], dp, padded)
    A_down = hidden_rows(place, A_hidden, place.q, dp, padded)
    choice, allowed, cosine_table, sine_table = block_tables(lengths[0], adapter_set[0])
    choices = jnp.concatenate(
        [block_tables(tables[k, :SEQ_DEV], tables[k, SEQ_DEV:])[0] for k in range(GROUP)], axis=0
    )
    xy0, xy1 = place.by_y(x0), place.by_x(y1)
    x1_c, y1_c = place.by_c(x1), place.by_c(y1)
    xy0, xy1, x1_c, y1_c, B_gate, B_up, A_down, choices, gate_planes, other_down, cotangent = together(
        xy0, xy1, x1_c, y1_c, B_gate, B_up, A_down, choices, gate_planes, other_down, cotangent
    )

    got_down = place.by_y(other_down)
    arrived_cot = lax.all_to_all(cotangent, "dp", split_axis=0, concat_axis=0, tiled=True)
    gate_mates = place.by_x(place.other_z(gate_planes))
    attention = AttentionWeights(
        place,
        weights,
        ((lines, lines_c, x0, x0_c), (lines2, lines2_c, x1, x1_c)),
        ((y0, y0_c, xy0, place.by_c(xy0)), (y1, y1_c, xy1, place.by_c(xy1))),
        (near_y, near_y_c, near_x, near_x_c),
    )
    gain_first = gain_one.astype(jnp.float32)
    gain_second = gain_two.astype(jnp.float32)

    x = arrived_x[token_order].astype(jnp.float32)
    scale_one = rms_scale(x)
    n1 = low(x * scale_one * gain_first)

    z_qkv = low(
        jnp.einsum("nd,tdr->tnr", n1, A_model[:3], preferred_element_type=jnp.float32) * choice
    )
    bias = jnp.where(allowed, 0.0, -jnp.inf)
    lin, got_down = together(attention.times(n1, 0, 3), got_down)
    left_planes = place.all_z(jnp.where(straight, own_down, got_down)[:, :cut])
    left_rest = jnp.where(straight, got_down, own_down)[:, :cut]
    right_planes = place.all_z(jnp.stack([own_down[:, cut:], got_down[:, cut:]]))
    qkv, o = attention_call(
        attention_kernel,
        (
            (lin, 2),
            (z_qkv, None),
            (B_model[:3], 2),
            (cosine_table, None),
            (sine_table, None),
            (bias, None),
        ),
        (((3, count, MODEL_WIDTH), 2), ((count, MODEL_WIDTH), 1)),
    )
    o, up_planes = together(o, up_planes)
    up_mates = place.by_x(place.other_z(up_planes))
    z_out, delta_out = apply_adapter_delta(o, A_model[3], B_model[3], choice)
    out_rows, gate_mates = together(attention.times(o, 3, 1), gate_mates)
    m = x + residual_branch_scale * (out_rows[0] + delta_out)
    scale_two = rms_scale(m)
    n2 = low(m * scale_two * gain_second)

    n2_y = place.by_y(n2)
    n2_y, arrived_cot, left_planes, up_mates = together(
        n2_y, arrived_cot, left_planes, up_mates
    )
    left_mates = place.by_x(place.other_z(left_planes))
    g = arrived_cot[token_order].astype(jnp.float32)
    e_down = low(residual_branch_scale * g)
    dz_down = low(adapter_scale * matrix_product_backward(e_down, B_model[4]) * choice)
    sent = jnp.concatenate([e_down, dz_down], axis=1)
    sent_y = place.by_y(sent)
    n2_all = jnp.concatenate([n2, n2_y], axis=0)
    n2_all = jnp.concatenate([n2_all, place.by_c(n2_all)], axis=0)
    gate_pieces = (gate_planes, gate_rest, gate_mates)
    forward = FeedForward(place, (left_planes, left_rest, left_mates), right_planes)
    gt, z_gate = forward.hidden(n2_all, choices, A_model[4], B_gate, gate_pieces)
    up_pieces = (up_planes, up_rest, up_mates)
    up, z_up = forward.hidden(n2_all, choices, A_model[5], B_up, up_pieces)
    gt, up, left_mates, right_planes, sent_y = together(gt, up, left_mates, right_planes, sent_y)
    sent_pair = jnp.concatenate([sent, sent_y], axis=0)
    sent_mate = place.by_c(sent_pair)
    dz_down_all = jnp.concatenate(
        [sent_pair[:, MODEL_WIDTH:], sent_mate[:, MODEL_WIDTH:]], axis=0
    )
    feed = FeedForward(place, (left_planes, left_rest, left_mates), right_planes)
    h, e_gate, e_up, keep, send = feed.back(
        gt, up, (sent_pair, sent_mate), A_down, B_gate, B_up, gate_pieces, up_pieces
    )
    own_sum, other_sum = place.half_sum(keep, send)
    other_sum, h, e_gate, e_up = together(low(other_sum), h, e_gate, e_up)
    got = place.by_y(other_sum)
    y_keep, y_send = feed.out(h, MODEL_WIDTH)
    dA_down = low(outer_product_sum(h, dz_down_all))
    own_hidden = FEEDFORWARD_UNITS // (dp * GROUP)
    dA_hidden = lax.dynamic_update_slice(
        jnp.zeros((dp, GROUP, own_hidden, ADAPTER_COLUMNS), jnp.bfloat16),
        dA_down.reshape(dp, 1, padded, ADAPTER_COLUMNS)[:, :, :own_hidden],
        (0, place.q, 0, 0),
    )
    hidden_parts = [dA_hidden.reshape(-1, ADAPTER_COLUMNS)] + [
        spread_columns(
            place, low(adapter_scale * outer_product_sum(z, e)), FEEDFORWARD_UNITS, dp, padded
        ).reshape(-1, ADAPTER_COLUMNS)
        for z, e in ((z_gate, e_gate), (z_up, e_up))
    ]
    got, y_send, *hidden_parts = together(got, y_send, *hidden_parts)
    back_sum = own_sum + got.astype(jnp.float32)
    y_own, y_other = place.half_sum(y_keep, y_send)
    y_got = place.by_y(low(y_other))
    cuts = [MODEL_WIDTH + k * ADAPTER_COLUMNS for k in range(3)]
    dz_gate, dz_up, z_down = jnp.split(back_sum, cuts, axis=1)[1:]
    dz_gate, dz_up = low(adapter_scale * dz_gate * choice), low(adapter_scale * dz_up * choice)
    z_down = low(z_down * choice)
    dn2 = (
        back_sum[:, :MODEL_WIDTH]
        + matrix_product_backward(dz_gate, A_model[4])
        + matrix_product_backward(dz_up, A_model[5])
    )
    dm = g + norm_back(m, scale_two, gain_second, dn2)
    e_out = low(residual_branch_scale * dm)
    dz_out = low(adapter_scale * matrix_product_backward(e_out, B_model[3]) * choice)
    (e_qkv,) = attention_call(
        attention_back_kernel,
        (
            (qkv, 2),
            (attention.times_transposed(e_out[None], 3, 1), 1),
            (dz_out, None),
            (A_model[3], 0),
            (cosine_table, None),
            (sine_table, None),
            (bias, None),
        ),
        (((3, count, MODEL_WIDTH), 2),),
    )
    e_qkv, y_got = together(e_qkv, y_got)
    y = m + residual_branch_scale * (
        y_own + y_got.astype(jnp.float32) + adapter_scale * matrix_product(z_down, B_model[4])
    )
    inverse = (
        jnp.zeros_like(token_order).at[token_order].set(jnp.arange(count, dtype=jnp.int32))
    )
    dz_qkv = low(
        adapter_scale
        * jnp.einsum("tnd,trd->tnr", e_qkv, B_model[:3], preferred_element_type=jnp.float32)
        * choice
    )
    flat = model_gradients(
        (
            n1,
            dz_qkv,
            z_qkv,
            e_qkv,
            o,
            dz_out,
            z_out,
            e_out,
            n2,
            dz_gate,
            dz_up,
            z_down,
            e_down,
        ),
        hidden_parts,
    )
    share = flat.shape[0] // (dp * shard)
    total, (e_qkv, dz_qkv, y) = reduce_over_cores(place, flat, (e_qkv, dz_qkv, y))
    owner = OwnerSum(place, total, share)
    back_out = lax.all_to_all(low(y)[inverse], "dp", split_axis=0, concat_axis=0, tiled=True)
    dn1 = attention.times_transposed(e_qkv, 0, 3) + jnp.einsum(
        "tnr,tdr->nd", dz_qkv, A_model[:3], preferred_element_type=jnp.float32
    )
    dx = dm + norm_back(x, scale_one, gain_first, dn1)
    owner.got, back_out, dx = together(owner.got, back_out, low(dx))
    total = owner.over_chips()
    total, back_grad = together(
        total, lax.all_to_all(dx[inverse], "dp", split_axis=0, concat_axis=0, tiled=True)
    )
    gradient = owner.over_planes(total)
    offset = lax.axis_index(AXES) * share
    own_params = lax.dynamic_slice_in_dim(
        adapters.reshape(-1, ADAPTER_COLUMNS), offset, share
    ).astype(jnp.float32)
    first = first_moment_running.reshape(share, ADAPTER_COLUMNS)
    second = second_moment_running.reshape(share, ADAPTER_COLUMNS)
    fresh_first = first_decay_rate * first + (1.0 - first_decay_rate) * gradient
    fresh_second = second_decay_rate * second + (1.0 - second_decay_rate) * gradient * gradient
    unbiased_first = fresh_first / (1.0 - first_decay_rate**OPT_STEP)
    unbiased_second = fresh_second / (1.0 - second_decay_rate**OPT_STEP)
    update = (
        unbiased_first / (jnp.sqrt(unbiased_second) + adaptive_epsilon)
        + weight_shrink_rate * own_params
    )
    updated = gather_owners(place, low(own_params - learning_rate * update))

    return (
        back_out,
        back_grad,
        gradient.reshape(-1),
        fresh_first.reshape(-1),
        fresh_second.reshape(-1),
        updated,
    )


def solution(mesh):
    rows = P(AXES, None)
    weight = P("dp", None)
    return jax.shard_map(
        functools.partial(shards, mesh.shape["dp"], mesh.shape["shard"]),
        mesh=mesh,
        in_specs=(rows,) * 5 + (P(), P()) + (weight,) * 7 + (P(), P(AXES), P(AXES)),
        out_specs=(rows, rows, P(AXES), P(AXES), P(AXES), P()),
        check_vma=False,
    )
```
